512 devices in a mesh: gx: 16 (over y_lo, x), gy: 32 (over z, y_hi, core).
Axes of the slice: x: 4, y: 8 (y_hi: 2, y_lo: 4; y = y_hi * 4 + y_lo), z: 8, core: 2. Of those that a mesh axis runs over, the one named last changes fastest.
Arguments:
- right_side: float32 [2, 128, 512, 256], P(None, 'gx', 'gy'), may hold values from -6 to 6
- diagonal: float32 [128, 512, 256], P('gx', 'gy'), may hold values from 0.05 to 2
Outputs:
- solution_field: float32 [2, 128, 512, 256], P(None, 'gx', 'gy')
- residual: float32 [2, 128, 512, 256], P(None, 'gx', 'gy')
- direction: float32 [2, 128, 512, 256], P(None, 'gx', 'gy')
The draws below stay inside these ranges and needn't reach their ends.
All inputs are finite; a program needn't handle non-finite values.
Results may differ from the reference program's by a relative error of at most 0.0003.
Values sent between devices are 32-bit elements; how exact they have to be, the bound alone decides.
No kernel may reach another device: no remote copies, remote signals or barrier semaphores. Data moves between devices by JAX's collectives and lax.ppermute only.
A program may use at most 64 MiB of HBM per device.

```python
import math
import jax
import jax.numpy as jnp

NZ = 256
KX = 16
KY = 16
KZ = 8
SMOOTH = 2
CSWEEPS = 4
NX = 128
NY = 512


def draw_right_side(key, part):
    key = jax.random.fold_in(key, 7)
    shape = (2, NX, NY, NZ)
    values = jax.random.normal(key, shape, jnp.float32)
    return jnp.clip(values, -6.0, 6.0).astype(jnp.float32)


def steps_of(rng, extent, shards, smallest, largest):
    level = 1.0
    for position, shards_of in shards:
        heights = jax.random.uniform(jax.random.fold_in(jax.random.fold_in(rng, 6), position), (shards_of,), jnp.float32, smallest / len(shards), largest / len(shards))
        level = level * jnp.repeat(jnp.exp(heights), extent[position] // shards_of).reshape((-1,) + (1,) * (len(extent) - 1 - position))
    return level


def setup_inputs(seed: int = 0) -> dict:
    streams_of = jax.random.split(jax.random.key(seed), 3)
    right_side = draw_right_side(jax.random.fold_in(streams_of[2], 71), 0)
    diagonal = jnp.clip(jnp.exp(math.log(2.0) - 3.6888794 * jax.random.uniform(streams_of[1], (NX, NY, NZ), jnp.float32) ** steps_of(streams_of[1], (NX, NY, NZ), ((0, 16), (1, 32)), -0.2, 0.2)), 0.05, 2.0)
    return dict(right_side=right_side, diagonal=diagonal)


OMEGA = 0.8


def stencil(padded, weight_x, weight_y, weight_z):
    along_x = padded[:, 2:, 1:-1, 1:-1] + padded[:, :-2, 1:-1, 1:-1]
    along_y = padded[:, 1:-1, 2:, 1:-1] + padded[:, 1:-1, :-2, 1:-1]
    along_z = padded[:, 1:-1, 1:-1, 2:] + padded[:, 1:-1, 1:-1, :-2]
    return weight_x * along_x + weight_y * along_y + weight_z * along_z


def padded_all(field):
    return jnp.pad(field, ((0, 0), (1, 1), (1, 1), (1, 1)))


def block_sum(field, size_x, size_y, size_z):
    count, ext_x, ext_y, ext_z = field.shape
    shaped = field.reshape(count, ext_x // size_x, size_x, ext_y // size_y, size_y, ext_z // size_z, size_z)
    return shaped.sum(axis=(2, 4, 6))


def spread_up(field, size_x, size_y, size_z):
    return jnp.repeat(jnp.repeat(jnp.repeat(field, size_x, 1), size_y, 2), size_z, 3)


def smooth_pre(rhs, apply_op, diag):
    guess = OMEGA * rhs / diag
    for sweep in range(SMOOTH - 1):
        guess = guess + OMEGA * (rhs - apply_op(guess)) / diag
    return guess


def smooth_post(guess, rhs, apply_op, diag):
    for sweep in range(SMOOTH):
        guess = guess + OMEGA * (rhs - apply_op(guess)) / diag
    return guess


def reference(right_side, diagonal):
    kappa = diagonal[None]
    fine_diag = 6.0 + kappa
    level_extra = block_sum(kappa, 2, 2, 2) / 4.0
    level_diag = 6.0 + level_extra
    block_x = (NX // 2) // KX
    block_y = (NY // 2) // KY
    block_z = (NZ // 2) // KZ
    weight_x = float(block_y * block_z)
    weight_y = float(block_x * block_z)
    weight_z = float(block_x * block_y)
    coarse_diag = 2.0 * (weight_x + weight_y + weight_z) + block_sum(level_extra, block_x, block_y, block_z)

    def fine_apply(field):
        return fine_diag * field - stencil(padded_all(field), 1.0, 1.0, 1.0)

    def level_apply(field):
        return level_diag * field - stencil(padded_all(field), 1.0, 1.0, 1.0)

    def coarse_apply(field):
        return coarse_diag * field - stencil(padded_all(field), weight_x, weight_y, weight_z)

    def level_cycle(rhs):
        guess = smooth_pre(rhs, level_apply, level_diag)
        coarse_rhs = block_sum(rhs - level_apply(guess), block_x, block_y, block_z)
        coarse = OMEGA * coarse_rhs / coarse_diag
        for sweep in range(CSWEEPS - 1):
            coarse = coarse + OMEGA * (coarse_rhs - coarse_apply(coarse)) / coarse_diag
        guess = guess + spread_up(coarse, block_x, block_y, block_z)
        return smooth_post(guess, rhs, level_apply, level_diag)

    def fine_cycle(rhs):
        guess = smooth_pre(rhs, fine_apply, fine_diag)
        level_rhs = block_sum(rhs - fine_apply(guess), 2, 2, 2) / 4.0
        guess = guess + spread_up(level_cycle(level_rhs), 2, 2, 2)
        return smooth_post(guess, rhs, fine_apply, fine_diag)

    precond = fine_cycle(right_side)
    image = fine_apply(precond)
    rz = jnp.sum(right_side * precond, axis=(1, 2, 3))
    pq = jnp.sum(precond * image, axis=(1, 2, 3))
    alpha = (rz / pq)[:, None, None, None]
    solution_field = alpha * precond
    residual = right_side - alpha * image
    after = fine_cycle(residual)
    beta = (jnp.sum(residual * after, axis=(1, 2, 3)) / rz)[:, None, None, None]
    direction = after + beta * precond
    return solution_field, residual, direction
```

```python
import jax
import jax.numpy as jnp
from jax import lax
from jax.sharding import PartitionSpec as P

KX = 16
KY = 16
KZ = 8
CSWEEPS = 4
OMEGA = 0.8
BOTH = ("gx", "gy")
HIGH = lax.Precision.HIGHEST


def extended(block, width):
    for axis, dim in (("gx", 1), ("gy", 2)):
        count = lax.axis_size(axis)
        forward = [(i, i + 1) for i in range(count - 1)]
        backward = [(target, source) for source, target in forward]
        low = lax.ppermute(
            lax.slice_in_dim(block, block.shape[dim] - width, None, axis=dim), axis, forward
        )
        high = lax.ppermute(lax.slice_in_dim(block, 0, width, axis=dim), axis, backward)
        block = jnp.concatenate([low, block, high], axis=dim)
    return block


def trim(block, cut):
    if cut == 0:
        return block
    return block[:, cut:-cut, cut:-cut, :]


def neighbours(field):
    along_x = field[:, 2:, 1:-1, :] + field[:, :-2, 1:-1, :]
    along_y = field[:, 1:-1, 2:, :] + field[:, 1:-1, :-2, :]
    inner = jnp.pad(field[:, 1:-1, 1:-1, :], ((0, 0), (0, 0), (0, 0), (1, 1)))
    return along_x + along_y + inner[..., 2:] + inner[..., :-2]


def apply(diag, field):
    return diag * trim(field, 1) - neighbours(field)


def sweep(field, rhs, diag, inverse):
    return trim(field, 1) + inverse * (rhs - apply(diag, field))


def pair_sum(field):
    depth = field.shape[3]
    table = (jnp.arange(depth)[:, None] // 2 == jnp.arange(depth // 2)[None, :]).astype(jnp.float32)
    across = field[:, 0::2] + field[:, 1::2]
    across = across[:, :, 0::2] + across[:, :, 1::2]
    return jnp.einsum("cxyz,zk->cxyk", across, table, precision=HIGH)


def pair_copy(field):
    half = field.shape[3]
    table = (jnp.arange(half)[:, None] == jnp.arange(2 * half)[None, :] // 2).astype(jnp.float32)
    wide = jnp.einsum("cxyk,kz->cxyz", field, table, precision=HIGH)
    return jnp.repeat(jnp.repeat(wide, 2, 1), 2, 2)


def coarse_neighbours(field, weight_x, weight_y, weight_z):
    padded = jnp.pad(field, ((0, 0), (1, 1), (1, 1), (1, 1)))
    along_x = padded[:, 2:, 1:-1, 1:-1] + padded[:, :-2, 1:-1, 1:-1]
    along_y = padded[:, 1:-1, 2:, 1:-1] + padded[:, 1:-1, :-2, 1:-1]
    along_z = padded[:, 1:-1, 1:-1, 2:] + padded[:, 1:-1, 1:-1, :-2]
    return weight_x * along_x + weight_y * along_y + weight_z * along_z


def local(right_side, diagonal):
    rows_x = right_side.shape[1]
    rows_y = right_side.shape[2]
    depth = right_side.shape[3]
    size_x = lax.axis_size("gx")
    size_y = lax.axis_size("gy")
    block_x = rows_x * size_x // 2 // KX
    block_y = rows_y * size_y // 2 // KY
    block_z = depth // 2 // KZ
    weight_x = float(block_y * block_z)
    weight_y = float(block_x * block_z)
    weight_z = float(block_x * block_y)
    share = size_y // KY
    place_x = lax.axis_index("gx")
    place_y = lax.axis_index("gy")

    def z_blocks(field):
        total = field.sum(axis=(1, 2))
        return total.reshape(total.shape[0], KZ, block_z).sum(axis=2)

    def coarse_grid(everyone):
        cells = everyone.reshape(size_x, KY, share, -1, KZ).sum(axis=2)
        return cells.transpose(2, 0, 1, 3)

    def coarse_solve(rhs, diag):
        value = OMEGA * rhs / diag
        for _ in range(CSWEEPS - 1):
            image = diag * value - coarse_neighbours(value, weight_x, weight_y, weight_z)
            value = value + OMEGA * (rhs - image) / diag
        return value

    def coarse_copy(value, width):
        padded = jnp.pad(value, ((0, 0), (1, 1), (1, 1), (0, 0)))
        start_y = place_y * (rows_y // 2) - width
        owners_y = jnp.floor_divide(start_y + jnp.arange(rows_y // 2 + 2 * width), block_y) + 1
        start_x = place_x * (rows_x // 2) - width
        owners_x = jnp.floor_divide(start_x + jnp.arange(rows_x // 2 + 2 * width), block_x) + 1
        table_x = (owners_x[:, None] == jnp.arange(KX + 2)[None]).astype(jnp.float32)
        table_y = (owners_y[:, None] == jnp.arange(KY + 2)[None]).astype(jnp.float32)
        rows = jnp.einsum("cijk,xi->cxjk", padded, table_x, precision=HIGH)
        rows = jnp.einsum("cxjk,yj->cxyk", rows, table_y, precision=HIGH)
        return jnp.repeat(rows, block_z, 3)

    def gather_all(values):
        flat = jnp.pad(values.reshape(1, -1), ((0, 0), (0, 128 - values.size)))
        flat = lax.all_gather(flat, BOTH, axis=0, tiled=True)
        return flat[:, : values.size].reshape((-1,) + values.shape)

    def exchange_all(values):
        spread = jnp.broadcast_to(values[None], (size_x * size_y,) + values.shape)
        return lax.all_to_all(spread, BOTH, 0, 0, tiled=True)

    both = extended(jnp.concatenate([right_side, diagonal[None]], axis=0), 3)
    rhs3 = both[:2]
    kappa3 = both[2:]
    fine3 = 6.0 + kappa3
    inv3 = jnp.where(kappa3 > 0.0, OMEGA / fine3, 0.0)
    fine2, inv2, rhs2 = trim(fine3, 1), trim(inv3, 1), trim(rhs3, 1)
    fine1, inv1, rhs1 = trim(fine3, 2), trim(inv3, 2), trim(rhs3, 2)
    fine0, inv0 = trim(fine3, 3), trim(inv3, 3)

    def fine_pre(wide):
        guess = sweep(inv3 * wide, trim(wide, 1), fine2, inv2)
        left = trim(wide, 3) - apply(fine0, trim(guess, 1))
        return guess, left, pair_sum(left) / 4.0

    guess, left, rhs_level = fine_pre(rhs3)
    extra = pair_sum(diagonal[None]) / 4.0
    level = extended(jnp.concatenate([rhs_level, extra], axis=0), 4)
    extra4 = level[2:]
    lev4 = 6.0 + extra4
    linv4 = jnp.where(extra4 > 0.0, OMEGA / lev4, 0.0)
    lev3, linv3 = trim(lev4, 1), trim(linv4, 1)

    def level_pre(wide):
        coarse_guess = sweep(linv4 * wide, trim(wide, 1), lev3, linv3)
        return coarse_guess, trim(wide, 4) - apply(trim(lev4, 4), trim(coarse_guess, 2))

    def post(value, guess, level_guess, level_wide, wide):
        e = level_guess + coarse_copy(value, 3)
        e = sweep(e, trim(level_wide, 2), trim(lev4, 2), trim(linv4, 2))
        e = sweep(e, trim(level_wide, 3), trim(lev4, 3), trim(linv4, 3))
        f = guess + pair_copy(e)
        f = sweep(f, trim(wide, 2), fine1, inv1)
        return sweep(f, trim(wide, 3), fine0, inv0)

    level_guess, level_left = level_pre(level[:2])
    cells = coarse_grid(
        gather_all(jnp.concatenate([z_blocks(level_left), z_blocks(extra)], axis=0))
    )
    coarse_diag = 2.0 * (weight_x + weight_y + weight_z) + cells[2:]
    value = coarse_solve(cells[:2], coarse_diag)
    precond = post(value, guess, level_guess, level[:2], rhs3)

    wide_p = extended(precond, 4)
    image3 = apply(fine3, wide_p)
    image = trim(image3, 3)
    guess_q, left_q, rhs_level_q = fine_pre(image3)
    level_q = extended(rhs_level_q, 4)
    level_guess_q, level_left_q = level_pre(level_q)
    axes = (1, 2, 3)
    rz = jnp.sum(right_side * precond, axis=axes)
    pq = jnp.sum(precond * image, axis=axes)
    energy = jnp.sum(trim(guess_q, 2) * (image + left_q), axis=axes)
    energy = energy + 4.0 * jnp.sum(
        trim(level_guess_q, 3) * (rhs_level_q + level_left_q), axis=axes
    )
    scalars = jnp.pad(jnp.stack([rz, pq, energy]), ((0, 0), (0, 0))).reshape(-1)
    scalars = jnp.pad(scalars, (0, KZ - scalars.shape[0]))[None]
    everyone = exchange_all(jnp.concatenate([z_blocks(level_left_q), scalars], axis=0))
    totals = everyone[:, 2].sum(axis=0)
    cells_q = coarse_grid(everyone[:, :2])
    value_q = coarse_solve(cells_q, coarse_diag)
    rz, pq, energy = totals[0:2], totals[2:4], totals[4:6]
    energy = energy + 4.0 * jnp.sum(cells_q * value_q, axis=axes)
    alpha = rz / pq
    beta = alpha * alpha * energy / rz - 1.0
    alpha = alpha[:, None, None, None]
    beta = beta[:, None, None, None]
    after_q = post(value_q, guess_q, level_guess_q, level_q, image3)
    solution_field = alpha * precond
    residual = right_side - alpha * image
    direction = precond - alpha * after_q + beta * precond
    return (solution_field, residual, direction)


def solution(mesh):
    placed = (P(None, "gx", "gy", None), P("gx", "gy", None))
    return jax.shard_map(
        local,
        mesh=mesh,
        in_specs=placed,
        out_specs=(P(None, "gx", "gy", None),) * 3,
        check_vma=False,
    )
```

```python
import functools

import jax
import jax.numpy as jnp
from jax import lax
from jax.experimental import pallas as pl
from jax.experimental.pallas import tpu as pltpu
from jax.sharding import PartitionSpec as P

KX = 16
KY = 16
KZ = 8
CSWEEPS = 4
OMEGA = 0.8
HIGH = lax.Precision.HIGHEST
F32 = jnp.float32
LANES = 128
DIAG_LANE = 16
TOTAL_LANE = 24


def dot(a, b):
    return jnp.dot(a, b, precision=HIGH, preferred_element_type=F32)


def iota(shape, dim):
    return lax.broadcasted_iota(jnp.int32, shape, dim)


def z_sides(row):
    depth = row.shape[-1]
    lane = iota(row.shape, 1)
    before = jnp.where(lane == 0, 0.0, pltpu.roll(row, 1, 1))
    after = jnp.where(lane == depth - 1, 0.0, pltpu.roll(row, depth - 1, 1))
    return before + after


def sides(ref, r, x):
    row = ref[r, x]
    rows = row.shape[0]
    along_y = pltpu.roll(row, 1, 0) + pltpu.roll(row, rows - 1, 0)
    return ref[r, x - 1] + ref[r, x + 1] + along_y + z_sides(row)


def sweep_rows(out, field, rhs, kappa, inverse, count, shift_rhs, shift_diag):
    for r in range(2):
        for x in range(count):
            image = (6.0 + kappa(x + shift_diag)) * field[r, x + 1] - sides(field, r, x + 1)
            step = inverse(x + shift_diag) * (rhs(r, x + shift_rhs) - image)
            out[r, x] = field[r, x + 1] + step


def inverse_of(kappa):
    return jnp.where(kappa > 0.0, OMEGA / (6.0 + kappa), 0.0)


def pair_table(wide, narrow):
    return (iota((wide, narrow), 0) // 2 == iota((wide, narrow), 1)).astype(F32)


def copy_table(narrow, wide):
    return (iota((narrow, wide), 0) == iota((narrow, wide), 1) // 2).astype(F32)


def fine_pre(wide, kappa, inv, zero, guess, sums, level, extra):
    for r in range(2):
        for x in range(14):
            zero[r, x] = inv(x) * wide[r, x]
    sweep_rows(guess, zero, lambda r, x: wide[r, x], kappa, inv, 12, 1, 1)
    left = []
    for r in range(2):
        rows = []
        for x in range(8):
            image = (6.0 + kappa(x + 3)) * guess[r, x + 2] - sides(guess, r, x + 2)
            rows.append(wide[r, x + 3] - image)
        left.append(rows)
    count = 3 if extra else 2
    table = pair_table(256, LANES)
    for c in range(count):
        rows = left[c] if c < 2 else [kappa(x + 3) for x in range(8)]
        for x in range(4):
            sums[pl.ds(24 * (4 * c + x), 24), :] = dot(rows[2 * x] + rows[2 * x + 1], table)
    for c in range(count):
        for x in range(4):
            base = 24 * (4 * c + x) + 4
            pair = sums[pl.ds(base, 8, stride=2), :] + sums[pl.ds(base + 1, 8, stride=2), :]
            level[c, x] = pair * 0.25
    return left


def fine_kernel(both, inv, guess, level, zero, sums):
    for x in range(14):
        inv[x] = inverse_of(both[2, x])
    fine_pre(both, lambda x: both[2, x], lambda x: inv[x], zero, guess, sums, level, True)


def block_table(channel):
    k = iota((LANES, LANES), 0) // (LANES // KZ)
    return (iota((LANES, LANES), 1) == channel * KZ + k).astype(F32)


def total_table(place):
    return (iota((LANES, LANES), 1) == TOTAL_LANE + place).astype(F32)


def own_rows(shape, low, high):
    row = iota(shape, 0)
    return (row >= low) & (row < high)


def level_pre(rhs, extra, guess, zero):
    linv = [inverse_of(extra(x)) for x in range(12)]
    for r in range(2):
        for x in range(12):
            zero[r, x] = linv[x] * rhs(r, x)
    sweep_rows(guess, zero, rhs, extra, lambda x: linv[x], 10, 1, 1)
    left = []
    for r in range(2):
        rows = []
        for x in range(4):
            image = (6.0 + extra(x + 4)) * guess[r, x + 3] - sides(guess, r, x + 3)
            rows.append(rhs(r, x + 4) - image)
        left.append(rows)
    return left


def total(rows):
    out = rows[0]
    for row in rows[1:]:
        out = out + row
    return out


def level_kernel(level, guess, line, zero):
    left = level_pre(lambda r, x: level[r, x], lambda x: level[2, x], guess, zero)
    own = own_rows((16, LANES), 4, 12)
    out = None
    for c in range(3):
        rows = left[c] if c < 2 else [level[2, x + 4] for x in range(4)]
        part = dot(jnp.where(own, total(rows), 0.0), block_table(c))
        out = part if out is None else out + part
    line[...] = jnp.sum(out, axis=0, keepdims=True)


def level_kernel_q(level, first, sums, guess, line, zero):
    left = level_pre(lambda r, x: level[r, x], lambda x: first[2, x], guess, zero)
    own = own_rows((16, LANES), 4, 12)
    out = None
    for r in range(2):
        part = dot(jnp.where(own, total(left[r]), 0.0), block_table(r))
        out = part if out is None else out + part
        terms = [guess[r, x + 3] * (level[r, x + 4] + left[r][x]) for x in range(4)]
        out = out + dot(4.0 * jnp.where(own, total(terms), 0.0), total_table(4 + r))
    line_sum = jnp.sum(out, axis=0, keepdims=True)
    for place in range(6):
        part = dot(sums[place], total_table(place))
        line_sum = line_sum + jnp.sum(part, axis=0, keepdims=True)
    line[...] = line_sum


def fold(field):
    folded = field[0:8] + field[8:16] + field[16:24]
    return folded[:, :LANES] + folded[:, LANES:]


def image_kernel(wide, both, inv, image, guess, level, out, zero, sums):
    for r in range(2):
        for x in range(14):
            image[r, x] = (6.0 + both[2, x]) * wide[r, x + 1] - sides(wide, r, x + 1)
    left = fine_pre(image, lambda x: both[2, x], lambda x: inv[x], zero, guess, sums, level, False)
    own = own_rows((24, 256), 4, 20)
    for r in range(2):
        rz = total([both[r, x + 3] * wide[r, x + 4] for x in range(8)])
        pq = total([image[r, x + 3] * wide[r, x + 4] for x in range(8)])
        en = total([guess[r, x + 2] * (image[r, x + 3] + left[r][x]) for x in range(8)])
        out[r] = fold(jnp.where(own, rz, 0.0))
        out[2 + r] = fold(jnp.where(own, pq, 0.0))
        out[4 + r] = fold(jnp.where(own, en, 0.0))


def pair_rows(gathered):
    return [gathered[2 * y] + gathered[2 * y + 1] for y in range(KY)]


def coarse_solve(rhs, diag, weights):
    weight_x, weight_y, weight_z = weights
    shape = rhs[0].shape
    row = iota(shape, 0)
    lane = iota(shape, 1) % KZ
    inverse = [OMEGA / d for d in diag]
    value = [i * b for i, b in zip(inverse, rhs)]
    nothing = jnp.zeros(shape, F32)
    for _ in range(CSWEEPS - 1):
        new = []
        for y in range(KY):
            v = value[y]
            below = value[y - 1] if y > 0 else nothing
            above = value[y + 1] if y < KY - 1 else nothing
            along_x = jnp.where(row == 0, 0.0, pltpu.roll(v, 1, 0))
            along_x = along_x + jnp.where(row == KX - 1, 0.0, pltpu.roll(v, shape[0] - 1, 0))
            along_z = jnp.where(lane == 0, 0.0, pltpu.roll(v, 1, 1))
            along_z = along_z + jnp.where(lane == KZ - 1, 0.0, pltpu.roll(v, LANES - 1, 1))
            image = diag[y] * v - (
                weight_x * along_x + weight_y * (below + above) + weight_z * along_z
            )
            new.append(v + inverse[y] * (rhs[y] - image))
        value = new
    return value


def coarse_diag_of(rows, weights):
    lane = iota(rows[0].shape, 1)
    base = 2.0 * (weights[0] + weights[1] + weights[2])
    out = []
    for row in rows:
        first = pltpu.roll(row, LANES - DIAG_LANE, 1)
        second = pltpu.roll(row, LANES - DIAG_LANE + KZ, 1)
        both = jnp.where(lane < KZ, first, jnp.where(lane < 2 * KZ, second, 0.0))
        out.append(base + both)
    return out


def up_blocks(place, value, spread, narrow, target):
    gx, gy = place[0], place[1]
    spread[...] = jnp.zeros(spread.shape, F32)
    lane_table = iota((LANES, LANES), 0)
    col = iota((LANES, LANES), 1) // (LANES // KZ)
    for r in range(2):
        table = (lane_table == r * KZ + col).astype(F32)
        for y in range(KY):
            spread[r, y + 1, pl.ds(8, KX), :] = dot(value[y], table)
    iy = gy // 2
    odd = gy % 2
    low = iy + odd
    row = iota((16, LANES), 0)
    limit = 4 + 8 * odd
    for r in range(2):
        for x in range(3):
            first = spread[r, low, pl.ds(gx + 7 + x, 1), :]
            second = spread[r, low + 1, pl.ds(gx + 7 + x, 1), :]
            tile = jnp.where(row < limit, first, second)
            for i in ((0, 1, 2), (3, 4, 5, 6), (7, 8, 9))[x]:
                target[r, i] = narrow[r, i] + tile


def post(place, value, spread, narrow, level_rhs, extra, guess, rhs, both, inv, s10, s8, s6, f12, f10, out):
    up_blocks(place, value, spread, narrow, s10)
    linv = {x: inverse_of(extra(x)) for x in range(2, 10)}
    sweep_rows(s8, s10, level_rhs, extra, lambda x: linv[x], 8, 2, 2)
    sweep_rows(s6, s8, level_rhs, extra, lambda x: linv[x], 6, 3, 3)
    table_y = (iota((24, 16), 1) == 2 + iota((24, 16), 0) // 2).astype(F32)
    table_z = copy_table(LANES, 256)
    for r in range(2):
        for x in range(6):
            wide = dot(dot(table_y, s6[r, x]), table_z)
            for i in range(2):
                f12[r, 2 * x + i] = guess[r, 2 * x + i] + wide
    kappa = lambda x: both[2, x]
    sweep_rows(f10, f12, rhs, kappa, lambda x: inv[x], 10, 2, 2)
    for r in range(2):
        for x in range(8):
            image = (6.0 + kappa(x + 3)) * f10[r, x + 1] - sides(f10, r, x + 1)
            out(r, x, f10[r, x + 1] + inv[x + 3] * (rhs(r, x + 3) - image))


def middle(row):
    return pltpu.roll(row, row.shape[0] - 4, 0)[0:16]


def precond_kernel(weights, place, gathered, narrow, level, guess, both, inv, precond, diag_out, spread, s10, s8, s6, f12, f10):
    rows = pair_rows(gathered)
    diag = coarse_diag_of(rows, weights)
    for y in range(KY):
        diag_out[y] = diag[y]
    lane = iota(rows[0].shape, 1)
    rhs = [jnp.where(lane < 2 * KZ, row, 0.0) for row in rows]
    value = coarse_solve(rhs, diag, weights)

    def out(r, x, row):
        precond[r, x] = middle(row)

    post(
        place, value, spread, narrow, lambda r, x: level[r, x], lambda x: level[2, x],
        guess, lambda r, x: both[r, x], both, inv, s10, s8, s6, f12, f10, out,
    )


def final_kernel(weights, place, gathered, diag_in, narrow, level, first, guess, image, both, inv, precond, right,
                 solution_field, residual, direction, spread, s10, s8, s6, f12, f10):
    rows = pair_rows(gathered)
    diag = [diag_in[y] for y in range(KY)]
    lane = iota(rows[0].shape, 1)
    rhs = [jnp.where(lane < 2 * KZ, row, 0.0) for row in rows]
    value = coarse_solve(rhs, diag, weights)
    sums = jnp.sum(total(rows), axis=0, keepdims=True)
    product = jnp.sum(total([a * b for a, b in zip(rhs, value)]), axis=0, keepdims=True)
    line = iota(sums.shape, 1)

    def pick(row, low, high):
        return jnp.sum(jnp.where((line >= low) & (line < high), row, 0.0), axis=1, keepdims=True)

    alphas, betas = [], []
    for r in range(2):
        rz = pick(sums, TOTAL_LANE + r, TOTAL_LANE + r + 1)
        pq = pick(sums, TOTAL_LANE + 2 + r, TOTAL_LANE + 3 + r)
        energy = pick(sums, TOTAL_LANE + 4 + r, TOTAL_LANE + 5 + r)
        energy = energy + 4.0 * pick(product, r * KZ, (r + 1) * KZ)
        alpha = rz / pq
        alphas.append(alpha)
        betas.append(alpha * alpha * energy / rz - 1.0)

    def out(r, x, row):
        p = precond[r, x]
        solution_field[r, x] = alphas[r] * p
        residual[r, x] = right[r, x] - alphas[r] * middle(image[r, x + 3])
        direction[r, x] = p - alphas[r] * middle(row) + betas[r] * p

    post(
        place, value, spread, narrow, lambda r, x: level[r, x], lambda x: first[2, x],
        guess, lambda r, x: image[r, x], both, inv, s10, s8, s6, f12, f10, out,
    )


def call(kernel, outs, scratch, place=None):
    vmem = pl.BlockSpec(memory_space=pltpu.VMEM)

    def run(*args):
        specs = [vmem] * len(args)
        if place is not None:
            args = (place,) + args
            specs = [pl.BlockSpec(memory_space=pltpu.SMEM)] + specs
        return pl.pallas_call(
            kernel,
            out_shape=[jax.ShapeDtypeStruct(shape, F32) for shape in outs],
            in_specs=specs,
            out_specs=[vmem] * len(outs),
            scratch_shapes=[pltpu.VMEM(shape, F32) for shape in scratch],
            compiler_params=pltpu.CompilerParams(vmem_limit_bytes=40 * 1024 * 1024),
        )(*args)

    return run


def extended(block, width_y, width_x, pad_y):
    count_y = lax.axis_size("gy")
    even = lax.axis_index("gy") % 2 == 0
    near_pairs = [(i, i + 1) for i in range(0, count_y, 2)]
    far_pairs = [(i, i + 1) for i in range(1, count_y - 1, 2)]
    near_pairs = near_pairs + [(b, a) for a, b in near_pairs]
    far_pairs = far_pairs + [(b, a) for a, b in far_pairs]
    low = block[:, :, :width_y]
    high = block[:, :, block.shape[2] - width_y :]
    far = lax.ppermute(jnp.where(even, low, high), "gy", far_pairs)
    near = lax.ppermute(jnp.where(even, high, low), "gy", near_pairs)
    parts = [jnp.where(even, far, near), block, jnp.where(even, near, far)]
    block = jnp.concatenate(parts, axis=2)
    if pad_y:
        block = jnp.pad(block, ((0, 0), (0, 0), (pad_y, pad_y), (0, 0)))
    count_x = lax.axis_size("gx")
    forward = [(i, i + 1) for i in range(count_x - 1)]
    backward = [(b, a) for a, b in forward]
    low = lax.ppermute(block[:, block.shape[1] - width_x :], "gx", forward)
    high = lax.ppermute(block[:, :width_x], "gx", backward)
    return jnp.concatenate([low, block, high], axis=1)


def gather_all(line):
    size_x = lax.axis_size("gx")
    size_y = lax.axis_size("gy")
    spread = jnp.broadcast_to(line[None], (size_x, 1, LANES))
    rows = lax.all_to_all(spread, "gx", 0, 0, tiled=True).reshape(size_x, LANES)
    spread = jnp.broadcast_to(rows[None], (size_y, size_x, LANES))
    return lax.all_to_all(spread, "gy", 0, 0, tiled=True)


def local(right_side, diagonal):
    block_x = right_side.shape[1] * lax.axis_size("gx") // 2 // KX
    block_y = right_side.shape[2] * lax.axis_size("gy") // 2 // KY
    block_z = right_side.shape[3] // 2 // KZ
    weights = (float(block_y * block_z), float(block_x * block_z), float(block_x * block_y))
    place = jnp.stack([lax.axis_index("gx"), lax.axis_index("gy")]).astype(jnp.int32)

    both = extended(jnp.concatenate([right_side, diagonal[None]], axis=0), 3, 3, 1)
    inv, guess, level = call(
        fine_kernel,
        [(14, 24, 256), (2, 12, 24, 256), (3, 4, 8, LANES)],
        [(2, 14, 24, 256), (288, LANES)],
    )(both)
    first = extended(level, 4, 4, 0)
    narrow, line = call(
        level_kernel, [(2, 10, 16, LANES), (1, LANES)], [(2, 12, 16, LANES)]
    )(first)
    gathered = gather_all(line)
    post_scratch = [
        (2, KY + 2, 8 + KX + 8, LANES), (2, 10, 16, LANES), (2, 8, 16, LANES), (2, 6, 16, LANES),
        (2, 12, 24, 256), (2, 10, 24, 256),
    ]
    precond, diag = call(
        functools.partial(precond_kernel, weights),
        [(2, 8, 16, 256), (KY, KX, LANES)],
        post_scratch,
        place,
    )(gathered, narrow, first, guess, both, inv)
    wide = extended(precond, 4, 4, 0)
    image, guess_q, level_q, sums = call(
        image_kernel,
        [(2, 14, 24, 256), (2, 12, 24, 256), (2, 4, 8, LANES), (6, 8, LANES)],
        [(2, 14, 24, 256), (288, LANES)],
    )(wide, both, inv)
    second = extended(level_q, 4, 4, 0)
    narrow_q, line_q = call(
        level_kernel_q, [(2, 10, 16, LANES), (1, LANES)], [(2, 12, 16, LANES)]
    )(second, first, sums)
    gathered_q = gather_all(line_q)
    return tuple(
        call(
            functools.partial(final_kernel, weights),
            [(2, 8, 16, 256)] * 3,
            post_scratch,
            place,
        )(gathered_q, diag, narrow_q, second, first, guess_q, image, both, inv, precond, right_side)
    )


def solution(mesh):
    placed = (P(None, "gx", "gy", None), P("gx", "gy", None))
    return jax.shard_map(
        local,
        mesh=mesh,
        in_specs=placed,
        out_specs=(P(None, "gx", "gy", None),) * 3,
        check_vma=False,
    )
```

```python
import functools

import jax
import jax.numpy as jnp
from jax import lax
from jax.experimental import pallas as pl
from jax.experimental.pallas import tpu as pltpu
from jax.sharding import PartitionSpec as P

KX = 16
KY = 16
KZ = 8
CSWEEPS = 4
OMEGA = 0.8
HIGH = lax.Precision.HIGHEST
F32 = jnp.float32
LANES = 128
SIDE_LANE = 16
OTHER_LANE = 48
DIAG_GROUP = 12
DIAG_LANE = 96
TOTAL_LANE = 104


def dot(a, b):
    return jnp.dot(a, b, precision=HIGH, preferred_element_type=F32)


def table_dot(a, table):
    table = table.astype(jnp.bfloat16)
    out = None
    for _ in range(3):
        part = a.astype(jnp.bfloat16)
        a = a - part.astype(F32)
        product = jnp.dot(part, table, preferred_element_type=F32)
        out = product if out is None else out + product
    return out


def iota(shape, dim):
    return lax.broadcasted_iota(jnp.int32, shape, dim)


def z_sides(row):
    depth = row.shape[-1]
    lane = iota(row.shape, 1)
    before = jnp.where(lane == 0, 0.0, pltpu.roll(row, 1, 1))
    after = jnp.where(lane == depth - 1, 0.0, pltpu.roll(row, depth - 1, 1))
    return before + after


def sides(ref, r, x):
    row = ref[r, x]
    rows = row.shape[0]
    along_y = pltpu.roll(row, 1, 0) + pltpu.roll(row, rows - 1, 0)
    return ref[r, x - 1] + ref[r, x + 1] + along_y + z_sides(row)


def sweep_rows(out, field, rhs, kappa, inverse, count, shift_rhs, shift_diag):
    for r in range(2):
        for x in range(count):
            image = (6.0 + kappa(x + shift_diag)) * field[r, x + 1] - sides(field, r, x + 1)
            step = inverse(x + shift_diag) * (rhs(r, x + shift_rhs) - image)
            out[r, x] = field[r, x + 1] + step


def inverse_of(kappa):
    return jnp.where(kappa > 0.0, OMEGA / (6.0 + kappa), 0.0)


def pair_table(wide, narrow):
    return (iota((wide, narrow), 0) // 2 == iota((wide, narrow), 1)).astype(F32)


def copy_table(narrow, wide):
    return (iota((narrow, wide), 0) == iota((narrow, wide), 1) // 2).astype(F32)


def fine_pre(wide, kappa, inv, zero, guess, sums, extra):
    for r in range(2):
        for x in range(14):
            zero[r, x] = inv(x) * wide[r, x]
    sweep_rows(guess, zero, lambda r, x: wide[r, x], kappa, inv, 12, 1, 1)
    left = []
    for r in range(2):
        rows = []
        for x in range(8):
            image = (6.0 + kappa(x + 3)) * guess[r, x + 2] - sides(guess, r, x + 2)
            rows.append(wide[r, x + 3] - image)
        left.append(rows)
    table = pair_table(256, LANES)
    pairs = [left[r][2 * x] + left[r][2 * x + 1] for r in range(2) for x in range(4)]
    if extra:
        pairs = pairs + [kappa(2 * x + 1) + kappa(2 * x + 2) for x in range(6)]
    sums[...] = jnp.zeros(sums.shape, F32)
    for i, pair in enumerate(pairs):
        sums[pl.ds(32 * i + 4, 24), :] = table_dot(pair, table)

    def level_row(i):
        pair = sums[pl.ds(32 * i, 16, stride=2), :] + sums[pl.ds(32 * i + 1, 16, stride=2), :]
        return pair * 0.25

    return left, level_row


def own_rows(shape, low, high):
    row = iota(shape, 0)
    return (row >= low) & (row < high)


def own_eight(row):
    return pltpu.roll(row, 12, 0)[0:8]


def gathered_line(vectors):
    row = iota((16, LANES), 0)
    stacked = jnp.zeros((16, LANES), F32)
    for group, vector in vectors.items():
        stacked = jnp.where(row == group, vector, stacked)
    table = iota((LANES, LANES), 0) // (LANES // KZ) == iota((LANES, LANES), 1) % KZ
    spread = table_dot(stacked, table.astype(F32))
    return jnp.sum(jnp.where(iota((16, LANES), 1) // KZ == row, spread, 0.0), axis=0, keepdims=True)


def level_pre(rhs, extra, guess, zero, first, last):
    linv = [inverse_of(extra(x)) for x in range(12)]
    for r in range(2):
        for x in range(12):
            zero[r, x] = linv[x] * rhs(r, x)
    sweep_rows(guess, zero, rhs, extra, lambda x: linv[x], 10, 1, 1)
    left = []
    for r in range(2):
        rows = []
        for x in range(first, last):
            image = (6.0 + extra(x)) * guess[r, x - 1] - sides(guess, r, x - 1)
            rows.append(rhs(r, x) - image)
        left.append(rows)
    return left


def total(rows):
    out = rows[0]
    for row in rows[1:]:
        out = out + row
    return out


def fine_kernel(place, both, inv, guess, level, line, zero, sums, zero_level, guess_level):
    for x in range(14):
        inv[x] = inverse_of(both[2, x])
    _, level_row = fine_pre(
        both, lambda x: both[2, x], lambda x: inv[x], zero, guess, sums, True
    )
    own = own_rows((16, LANES), 4, 12)
    nothing = jnp.zeros((16, LANES), F32)
    rhs = [[jnp.where(own, level_row(4 * r + x), 0.0) for x in range(4)] for r in range(2)]
    extra = [level_row(8 + x) for x in range(6)]
    for r in range(2):
        for x in range(4):
            level[r, x] = own_eight(rhs[r][x])
    for x in range(4):
        level[2, x] = own_eight(extra[x + 1])
    left = level_pre(
        lambda r, x: rhs[r][x - 4] if 4 <= x < 8 else nothing,
        lambda x: extra[x - 3] if 3 <= x < 9 else nothing,
        guess_level, zero_level, 2, 10,
    )
    row = iota((16, LANES), 0)
    odd = place[1] % 2
    other = (row < 4 * (1 - odd)) | (row >= 16 - 4 * odd)
    vectors = {}
    for r in range(2):
        for side, rows in enumerate((left[r][2:6], left[r][0:2], left[r][6:8])):
            column = total(rows)
            for far in range(2):
                part = jnp.where(other, column, 0.0) if far else jnp.where(other, 0.0, column)
                vectors[(3 * far + side) * 2 + r] = jnp.sum(part, axis=0, keepdims=True)
    diag_sum = jnp.where(own, total(extra[1:5]), 0.0)
    vectors[DIAG_GROUP] = jnp.sum(diag_sum, axis=0, keepdims=True)
    line[...] = gathered_line(vectors)


def level_kernel_q(level, first, sums, guess, line, zero):
    left = level_pre(lambda r, x: level[r, x], lambda x: first[2, x], guess, zero, 4, 8)
    own = own_rows((16, LANES), 4, 12)
    vectors = {}
    parts = [sums[place] for place in range(6)]
    for r in range(2):
        column = jnp.where(own, total(left[r]), 0.0)
        vectors[r] = jnp.sum(column, axis=0, keepdims=True)
        terms = [guess[r, x + 3] * (level[r, x + 4] + left[r][x]) for x in range(4)]
        terms = 4.0 * jnp.where(own, total(terms), 0.0)
        parts[4 + r] = parts[4 + r] + terms[0:8] + terms[8:16]
    out = gathered_line(vectors)
    lane = iota((1, LANES), 1)
    for place in range(6):
        value = jnp.sum(jnp.sum(parts[place], axis=0, keepdims=True), axis=1, keepdims=True)
        out = jnp.where(lane == TOTAL_LANE + place, value, out)
    line[...] = out


def fold(field):
    folded = field[0:8] + field[8:16] + field[16:24]
    return folded[:, :LANES] + folded[:, LANES:]


def image_kernel(wide, both, inv, image, guess, level, out, zero, sums):
    for r in range(2):
        for x in range(14):
            image[r, x] = (6.0 + both[2, x]) * wide[r, x + 1] - sides(wide, r, x + 1)
    left, level_row = fine_pre(
        image, lambda x: both[2, x], lambda x: inv[x], zero, guess, sums, False
    )
    for r in range(2):
        for x in range(4):
            level[r, x] = own_eight(level_row(4 * r + x))
    own = own_rows((24, 256), 4, 20)
    for r in range(2):
        rz = total([both[r, x + 3] * wide[r, x + 4] for x in range(8)])
        pq = total([image[r, x + 3] * wide[r, x + 4] for x in range(8)])
        en = total([guess[r, x + 2] * (image[r, x + 3] + left[r][x]) for x in range(8)])
        out[r] = fold(jnp.where(own, rz, 0.0))
        out[2 + r] = fold(jnp.where(own, pq, 0.0))
        out[4 + r] = fold(jnp.where(own, en, 0.0))


def coarse_rows(gathered):
    rows = [gathered[x] for x in range(KX)]
    lane = iota(rows[0].shape, 1)
    out = []
    for x in range(KX):
        row = rows[x]
        if x < KX - 1:
            row = row + pltpu.roll(rows[x + 1], LANES - SIDE_LANE, 1)
        if x > 0:
            row = row + pltpu.roll(rows[x - 1], LANES - 2 * SIDE_LANE, 1)
        out.append(jnp.where(lane < 2 * KZ, row, 0.0))
    return rows, out


def coarse_solve(rhs, diag, weights):
    weight_x, weight_y, weight_z = weights
    shape = rhs[0].shape
    row = iota(shape, 0)
    lane = iota(shape, 1) % KZ
    inverse = [OMEGA / d for d in diag]
    value = [i * b for i, b in zip(inverse, rhs)]
    nothing = jnp.zeros(shape, F32)
    for _ in range(CSWEEPS - 1):
        new = []
        for x in range(KX):
            v = value[x]
            below = value[x - 1] if x > 0 else nothing
            above = value[x + 1] if x < KX - 1 else nothing
            along_y = jnp.where(row == 0, 0.0, pltpu.roll(v, 1, 0))
            along_y = along_y + jnp.where(row == KY - 1, 0.0, pltpu.roll(v, shape[0] - 1, 0))
            along_z = jnp.where(lane == 0, 0.0, pltpu.roll(v, 1, 1))
            along_z = along_z + jnp.where(lane == KZ - 1, 0.0, pltpu.roll(v, LANES - 1, 1))
            image = diag[x] * v - (
                weight_x * (below + above) + weight_y * along_y + weight_z * along_z
            )
            new.append(v + inverse[x] * (rhs[x] - image))
        value = new
    return value


def coarse_diag_of(rows, weights):
    lane = iota(rows[0].shape, 1)
    base = 2.0 * (weights[0] + weights[1] + weights[2])
    out = []
    for row in rows:
        first = pltpu.roll(row, LANES - DIAG_LANE, 1)
        second = pltpu.roll(row, LANES - DIAG_LANE + KZ, 1)
        both = jnp.where(lane < KZ, first, jnp.where(lane < 2 * KZ, second, 0.0))
        out.append(base + both)
    return out


def up_blocks(place, value, spread, narrow, target):
    gx, gy = place[0], place[1]
    spread[...] = jnp.zeros(spread.shape, F32)
    stacked = jnp.concatenate(value, axis=0)
    lane_table = iota((LANES, LANES), 0)
    col = iota((LANES, LANES), 1) // (LANES // KZ)
    for r in range(2):
        wide = table_dot(stacked, (lane_table == r * KZ + col).astype(F32))
        for x in range(KX):
            spread[r, x + 1, pl.ds(8, KY), :] = wide[KY * x : KY * (x + 1)]
    odd = gy % 2
    low = gy // 2 + odd + 7
    row = iota((16, LANES), 0)
    limit = 4 + 8 * odd
    for r in range(2):
        for x in range(3):
            first = spread[r, gx + x, pl.ds(low, 1), :]
            second = spread[r, gx + x, pl.ds(low + 1, 1), :]
            tile = jnp.where(row < limit, first, second)
            for i in ((0, 1, 2), (3, 4, 5, 6), (7, 8, 9))[x]:
                target[r, i] = narrow[r, i] + tile


def post(place, value, spread, narrow, level_rhs, extra, guess, rhs, both, inv, s10, s8, s6, ups, f12, f10, out):
    up_blocks(place, value, spread, narrow, s10)
    linv = {x: inverse_of(extra(x)) for x in range(2, 10)}
    sweep_rows(s8, s10, level_rhs, extra, lambda x: linv[x], 8, 2, 2)
    sweep_rows(s6, s8, level_rhs, extra, lambda x: linv[x], 6, 3, 3)
    table_z = copy_table(LANES, 256)
    for r in range(2):
        for x in range(6):
            base = 32 * (6 * r + x)
            ups[pl.ds(base, 16, stride=2), :] = s6[r, x]
            ups[pl.ds(base + 1, 16, stride=2), :] = s6[r, x]
            wide = table_dot(ups[pl.ds(base + 4, 24), :], table_z)
            for i in range(2):
                f12[r, 2 * x + i] = guess[r, 2 * x + i] + wide
    kappa = lambda x: both[2, x]
    sweep_rows(f10, f12, rhs, kappa, lambda x: inv[x], 10, 2, 2)
    for r in range(2):
        for x in range(8):
            image = (6.0 + kappa(x + 3)) * f10[r, x + 1] - sides(f10, r, x + 1)
            out(r, x, f10[r, x + 1] + inv[x + 3] * (rhs(r, x + 3) - image))


def middle(row):
    return pltpu.roll(row, row.shape[0] - 4, 0)[0:16]


def precond_kernel(weights, place, gathered, level, guess, both, inv, precond, diag_out,
                   zero, narrow, spread, s10, s8, s6, ups, f12, f10):
    level_pre(lambda r, x: level[r, x], lambda x: level[2, x], narrow, zero, 4, 4)
    rows, rhs = coarse_rows(gathered)
    diag = coarse_diag_of(rows, weights)
    for x in range(KX):
        diag_out[x] = diag[x]
    value = coarse_solve(rhs, diag, weights)

    def out(r, x, row):
        precond[r, x] = middle(row)

    post(
        place, value, spread, narrow, lambda r, x: level[r, x], lambda x: level[2, x],
        guess, lambda r, x: both[r, x], both, inv, s10, s8, s6, ups, f12, f10, out,
    )


def final_kernel(weights, place, gathered, diag_in, narrow, level, first, guess, image, both, inv, precond, right,
                 solution_field, residual, direction, spread, s10, s8, s6, ups, f12, f10):
    rows, rhs = coarse_rows(gathered)
    diag = [diag_in[x] for x in range(KX)]
    value = coarse_solve(rhs, diag, weights)
    sums = jnp.sum(total(rows), axis=0, keepdims=True)
    product = jnp.sum(total([a * b for a, b in zip(rhs, value)]), axis=0, keepdims=True)
    line = iota(sums.shape, 1)

    def pick(row, low, high):
        return jnp.sum(jnp.where((line >= low) & (line < high), row, 0.0), axis=1, keepdims=True)

    alphas, betas = [], []
    for r in range(2):
        rz = pick(sums, TOTAL_LANE + r, TOTAL_LANE + r + 1)
        pq = pick(sums, TOTAL_LANE + 2 + r, TOTAL_LANE + 3 + r)
        energy = pick(sums, TOTAL_LANE + 4 + r, TOTAL_LANE + 5 + r)
        energy = energy + 4.0 * pick(product, r * KZ, (r + 1) * KZ)
        alpha = rz / pq
        alphas.append(alpha)
        betas.append(alpha * alpha * energy / rz - 1.0)

    def out(r, x, row):
        p = precond[r, x]
        solution_field[r, x] = alphas[r] * p
        residual[r, x] = right[r, x] - alphas[r] * middle(image[r, x + 3])
        direction[r, x] = p - alphas[r] * middle(row) + betas[r] * p

    post(
        place, value, spread, narrow, lambda r, x: level[r, x], lambda x: first[2, x],
        guess, lambda r, x: image[r, x], both, inv, s10, s8, s6, ups, f12, f10, out,
    )


def call(kernel, outs, scratch, place=None):
    vmem = pl.BlockSpec(memory_space=pltpu.VMEM)

    def run(*args):
        specs = [vmem] * len(args)
        if place is not None:
            args = (place,) + args
            specs = [pl.BlockSpec(memory_space=pltpu.SMEM)] + specs
        return pl.pallas_call(
            kernel,
            out_shape=[jax.ShapeDtypeStruct(shape, F32) for shape in outs],
            in_specs=specs,
            out_specs=[vmem] * len(outs),
            scratch_shapes=[pltpu.VMEM(shape, F32) for shape in scratch],
            compiler_params=pltpu.CompilerParams(vmem_limit_bytes=40 * 1024 * 1024),
        )(*args)

    return run


def extended(block, width_y, width_x, pad_y):
    count_y = lax.axis_size("gy")
    even = lax.axis_index("gy") % 2 == 0
    near_pairs = [(i, i + 1) for i in range(0, count_y, 2)]
    far_pairs = [(i, i + 1) for i in range(1, count_y - 1, 2)]
    near_pairs = near_pairs + [(b, a) for a, b in near_pairs]
    far_pairs = far_pairs + [(b, a) for a, b in far_pairs]
    low = block[:, :, :width_y]
    high = block[:, :, block.shape[2] - width_y :]
    far = lax.ppermute(jnp.where(even, low, high), "gy", far_pairs)
    near = lax.ppermute(jnp.where(even, high, low), "gy", near_pairs)
    parts = [jnp.where(even, far, near), block, jnp.where(even, near, far)]
    block = jnp.concatenate(parts, axis=2)
    if pad_y:
        block = jnp.pad(block, ((0, 0), (0, 0), (pad_y, pad_y), (0, 0)))
    count_x = lax.axis_size("gx")
    forward = [(i, i + 1) for i in range(count_x - 1)]
    backward = [(b, a) for a, b in forward]
    low = lax.ppermute(block[:, block.shape[1] - width_x :], "gx", forward)
    high = lax.ppermute(block[:, :width_x], "gx", backward)
    return jnp.concatenate([low, block, high], axis=1)


def gather_all(line):
    size_x = lax.axis_size("gx")
    size_y = lax.axis_size("gy")
    spread = jnp.broadcast_to(line[None], (size_y, 1, LANES))
    rows = lax.all_to_all(spread, "gy", 0, 0, tiled=True).reshape(KY, size_y // KY, LANES)
    even, odd = rows[:, 0], rows[:, 1]
    other = jnp.pad(even[1:], ((0, 1), (0, 0))) + jnp.pad(odd[:-1], ((1, 0), (0, 0)))
    other = jnp.pad(other[:, OTHER_LANE : 2 * OTHER_LANE], ((0, 0), (0, LANES - OTHER_LANE)))
    rows = even + odd + other
    spread = jnp.broadcast_to(rows[None], (size_x, KY, LANES))
    return lax.all_to_all(spread, "gx", 0, 0, tiled=True)


def local(right_side, diagonal):
    block_x = right_side.shape[1] * lax.axis_size("gx") // 2 // KX
    block_y = right_side.shape[2] * lax.axis_size("gy") // 2 // KY
    block_z = right_side.shape[3] // 2 // KZ
    weights = (float(block_y * block_z), float(block_x * block_z), float(block_x * block_y))
    place = jnp.stack([lax.axis_index("gx"), lax.axis_index("gy")]).astype(jnp.int32)

    both = extended(jnp.concatenate([right_side, diagonal[None]], axis=0), 3, 3, 1)
    inv, guess, level, line = call(
        fine_kernel,
        [(14, 24, 256), (2, 12, 24, 256), (3, 4, 8, LANES), (1, LANES)],
        [(2, 14, 24, 256), (448, LANES), (2, 12, 16, LANES), (2, 10, 16, LANES)],
        place,
    )(both)
    gathered = gather_all(line)
    first = extended(level, 4, 4, 0)
    post_scratch = [
        (2, KX + 2, 8 + KY + 8, LANES), (2, 10, 16, LANES), (2, 8, 16, LANES), (2, 6, 16, LANES),
        (384, LANES), (2, 12, 24, 256), (2, 10, 24, 256),
    ]
    precond, diag = call(
        functools.partial(precond_kernel, weights),
        [(2, 8, 16, 256), (KX, KY, LANES)],
        [(2, 12, 16, LANES), (2, 10, 16, LANES)] + post_scratch,
        place,
    )(gathered, first, guess, both, inv)
    wide = extended(precond, 4, 4, 0)
    image, guess_q, level_q, sums = call(
        image_kernel,
        [(2, 14, 24, 256), (2, 12, 24, 256), (2, 4, 8, LANES), (6, 8, LANES)],
        [(2, 14, 24, 256), (256, LANES)],
    )(wide, both, inv)
    second = extended(level_q, 4, 4, 0)
    narrow_q, line_q = call(
        level_kernel_q, [(2, 10, 16, LANES), (1, LANES)], [(2, 12, 16, LANES)]
    )(second, first, sums)
    gathered_q = gather_all(line_q)
    return tuple(
        call(
            functools.partial(final_kernel, weights),
            [(2, 8, 16, 256)] * 3,
            post_scratch,
            place,
        )(gathered_q, diag, narrow_q, second, first, guess_q, image, both, inv, precond, right_side)
    )


def solution(mesh):
    placed = (P(None, "gx", "gy", None), P("gx", "gy", None))
    return jax.shard_map(
        local,
        mesh=mesh,
        in_specs=placed,
        out_specs=(P(None, "gx", "gy", None),) * 3,
        check_vma=False,
    )
```

```python
import functools

import jax
import jax.numpy as jnp
from jax import lax
from jax.experimental import pallas as pl
from jax.experimental.pallas import tpu as pltpu
from jax.sharding import PartitionSpec as P

KX = 16
KY = 16
KZ = 8
CSWEEPS = 4
OMEGA = 0.8
HIGH = lax.Precision.HIGHEST
F32 = jnp.float32
LANES = 128
SIDE_LANE = 16
OTHER_LANE = 48
DIAG_GROUP = 12
DIAG_LANE = 96
TOTAL_LANE = 104


def dot(a, b):
    return jnp.dot(a, b, precision=HIGH, preferred_element_type=F32)


def table_dot(a, table):
    table = table.astype(jnp.bfloat16)
    out = None
    for _ in range(3):
        part = a.astype(jnp.bfloat16)
        a = a - part.astype(F32)
        product = jnp.dot(part, table, preferred_element_type=F32)
        out = product if out is None else out + product
    return out


def iota(shape, dim):
    return lax.broadcasted_iota(jnp.int32, shape, dim)


def z_sides(row):
    depth = row.shape[-1]
    lane = iota(row.shape, 1)
    before = jnp.where(lane == 0, 0.0, pltpu.roll(row, 1, 1))
    after = jnp.where(lane == depth - 1, 0.0, pltpu.roll(row, depth - 1, 1))
    return before + after


def sides(ref, r, x):
    row = ref[r, x]
    rows = row.shape[0]
    along_y = pltpu.roll(row, 1, 0) + pltpu.roll(row, rows - 1, 0)
    return ref[r, x - 1] + ref[r, x + 1] + along_y + z_sides(row)


def sweep_rows(out, field, rhs, kappa, inverse, count, shift_rhs, shift_diag):
    for r in range(2):
        for x in range(count):
            image = (6.0 + kappa(x + shift_diag)) * field[r, x + 1] - sides(field, r, x + 1)
            step = inverse(x + shift_diag) * (rhs(r, x + shift_rhs) - image)
            out[r, x] = field[r, x + 1] + step


def inverse_of(kappa):
    return jnp.where(kappa > 0.0, OMEGA / (6.0 + kappa), 0.0)


def pair_table(wide, narrow):
    return (iota((wide, narrow), 0) // 2 == iota((wide, narrow), 1)).astype(F32)


def copy_table(narrow, wide):
    return (iota((narrow, wide), 0) == iota((narrow, wide), 1) // 2).astype(F32)


def fine_pre(wide, kappa, inv, zero, guess, sums):
    for r in range(2):
        for x in range(14):
            zero[r, x] = inv(x) * wide[r, x]
    sweep_rows(guess, zero, lambda r, x: wide[r, x], kappa, inv, 12, 1, 1)
    left = []
    for r in range(2):
        rows = []
        for x in range(8):
            image = (6.0 + kappa(x + 3)) * guess[r, x + 2] - sides(guess, r, x + 2)
            rows.append(wide[r, x + 3] - image)
        left.append(rows)
    pairs = [left[r][2 * x] + left[r][2 * x + 1] for r in range(2) for x in range(4)]
    return level_rows(pairs + [kappa(2 * x + 1) + kappa(2 * x + 2) for x in range(6)], sums)


def level_rows(pairs, sums):
    table = pair_table(256, LANES)
    sums[...] = jnp.zeros(sums.shape, F32)
    for i, pair in enumerate(pairs):
        sums[pl.ds(32 * i + 4, 24), :] = table_dot(pair, table)

    def level_row(i):
        pair = sums[pl.ds(32 * i, 16, stride=2), :] + sums[pl.ds(32 * i + 1, 16, stride=2), :]
        return pair * 0.25

    return level_row


def own_rows(shape, low, high):
    row = iota(shape, 0)
    return (row >= low) & (row < high)


def own_eight(row):
    return pltpu.roll(row, 12, 0)[0:8]


def gathered_line(vectors):
    row = iota((16, LANES), 0)
    stacked = jnp.zeros((16, LANES), F32)
    for group, vector in vectors.items():
        stacked = jnp.where(row == group, vector, stacked)
    table = iota((LANES, LANES), 0) // (LANES // KZ) == iota((LANES, LANES), 1) % KZ
    spread = table_dot(stacked, table.astype(F32))
    return jnp.sum(jnp.where(iota((16, LANES), 1) // KZ == row, spread, 0.0), axis=0, keepdims=True)


def level_pre(rhs, extra, guess, zero, first, last):
    linv = [inverse_of(extra(x)) for x in range(12)]
    for r in range(2):
        for x in range(12):
            zero[r, x] = linv[x] * rhs(r, x)
    sweep_rows(guess, zero, rhs, extra, lambda x: linv[x], 10, 1, 1)
    left = []
    for r in range(2):
        rows = []
        for x in range(first, last):
            image = (6.0 + extra(x)) * guess[r, x - 1] - sides(guess, r, x - 1)
            rows.append(rhs(r, x) - image)
        left.append(rows)
    return left


def total(rows):
    out = rows[0]
    for row in rows[1:]:
        out = out + row
    return out


def fine_kernel(place, both, inv, guess, level, line, zero, sums, zero_level, guess_level):
    for x in range(14):
        inv[x] = inverse_of(both[2, x])
    level_row = fine_pre(both, lambda x: both[2, x], lambda x: inv[x], zero, guess, sums)
    own = own_rows((16, LANES), 4, 12)
    nothing = jnp.zeros((16, LANES), F32)
    rhs = [[jnp.where(own, level_row(4 * r + x), 0.0) for x in range(4)] for r in range(2)]
    extra = [level_row(8 + x) for x in range(6)]
    for r in range(2):
        for x in range(4):
            level[r, x] = own_eight(rhs[r][x])
    for x in range(4):
        level[2, x] = own_eight(extra[x + 1])
    left = level_pre(
        lambda r, x: rhs[r][x - 4] if 4 <= x < 8 else nothing,
        lambda x: extra[x - 3] if 3 <= x < 9 else nothing,
        guess_level, zero_level, 2, 10,
    )
    row = iota((16, LANES), 0)
    odd = place[1] % 2
    other = (row < 4 * (1 - odd)) | (row >= 16 - 4 * odd)
    vectors = {}
    for r in range(2):
        for side, rows in enumerate((left[r][2:6], left[r][0:2], left[r][6:8])):
            column = total(rows)
            for far in range(2):
                part = jnp.where(other, column, 0.0) if far else jnp.where(other, 0.0, column)
                vectors[(3 * far + side) * 2 + r] = jnp.sum(part, axis=0, keepdims=True)
    diag_sum = jnp.where(own, total(extra[1:5]), 0.0)
    vectors[DIAG_GROUP] = jnp.sum(diag_sum, axis=0, keepdims=True)
    line[...] = gathered_line(vectors)


def fold(field):
    folded = field[0:8] + field[8:16] + field[16:24]
    return folded[:, :LANES] + folded[:, LANES:]


def image_kernel(wide, level, first, both, inv, image, guess, narrow, line, zero, zero_level):
    for r in range(2):
        for x in range(14):
            image[r, x] = (6.0 + both[2, x]) * wide[r, x + 1] - sides(wide, r, x + 1)
            zero[r, x] = inv[x] * image[r, x]
    kappa = lambda x: both[2, x]
    sweep_rows(guess, zero, lambda r, x: image[r, x], kappa, lambda x: inv[x], 12, 1, 1)
    own = own_rows((24, 256), 4, 20)
    own_level = own_rows((16, LANES), 4, 12)
    extra = lambda x: first[2, x + 2]
    linv = [inverse_of(extra(x)) for x in range(8)]
    for r in range(2):
        for x in range(8):
            zero_level[r, x] = linv[x] * level[r, x]
    level_rhs = lambda r, x: level[r, x]
    sweep_rows(narrow, zero_level, level_rhs, extra, lambda x: linv[x], 6, 1, 1)
    vectors = {}
    totals = []
    for r in range(2):
        rz = total([both[r, x + 3] * wide[r, x + 4] for x in range(8)])
        pq = total([image[r, x + 3] * wide[r, x + 4] for x in range(8)])
        energy = None
        for x in range(8):
            back = (6.0 + both[2, x + 3]) * guess[r, x + 2] - sides(guess, r, x + 2)
            term = guess[r, x + 2] * (2.0 * image[r, x + 3] - back)
            energy = term if energy is None else energy + term
        energy = fold(jnp.where(own, energy, 0.0))
        column = None
        for x in range(4):
            back = (6.0 + extra(x + 2)) * narrow[r, x + 1] - sides(narrow, r, x + 1)
            left = level[r, x + 2] - back
            column = left if column is None else column + left
            term = narrow[r, x + 1] * (level[r, x + 2] + left)
            term = 4.0 * jnp.where(own_level, term, 0.0)
            energy = energy + term[0:8] + term[8:16]
        vectors[r] = jnp.sum(jnp.where(own_level, column, 0.0), axis=0, keepdims=True)
        totals.append((TOTAL_LANE + r, fold(jnp.where(own, rz, 0.0))))
        totals.append((TOTAL_LANE + 2 + r, fold(jnp.where(own, pq, 0.0))))
        totals.append((TOTAL_LANE + 4 + r, energy))
    out = gathered_line(vectors)
    lane = iota((1, LANES), 1)
    for place, part in totals:
        value = jnp.sum(jnp.sum(part, axis=0, keepdims=True), axis=1, keepdims=True)
        out = jnp.where(lane == place, value, out)
    line[...] = out


def coarse_rows(gathered):
    rows = [gathered[x] for x in range(KX)]
    lane = iota(rows[0].shape, 1)
    out = []
    for x in range(KX):
        row = rows[x]
        if x < KX - 1:
            row = row + pltpu.roll(rows[x + 1], LANES - SIDE_LANE, 1)
        if x > 0:
            row = row + pltpu.roll(rows[x - 1], LANES - 2 * SIDE_LANE, 1)
        out.append(jnp.where(lane < 2 * KZ, row, 0.0))
    return rows, out


def coarse_solve(rhs, diag, weights):
    weight_x, weight_y, weight_z = weights
    shape = rhs[0].shape
    row = iota(shape, 0)
    lane = iota(shape, 1) % KZ
    inverse = [OMEGA / d for d in diag]
    value = [i * b for i, b in zip(inverse, rhs)]
    nothing = jnp.zeros(shape, F32)
    for _ in range(CSWEEPS - 1):
        new = []
        for x in range(KX):
            v = value[x]
            below = value[x - 1] if x > 0 else nothing
            above = value[x + 1] if x < KX - 1 else nothing
            along_y = jnp.where(row == 0, 0.0, pltpu.roll(v, 1, 0))
            along_y = along_y + jnp.where(row == KY - 1, 0.0, pltpu.roll(v, shape[0] - 1, 0))
            along_z = jnp.where(lane == 0, 0.0, pltpu.roll(v, 1, 1))
            along_z = along_z + jnp.where(lane == KZ - 1, 0.0, pltpu.roll(v, LANES - 1, 1))
            image = diag[x] * v - (
                weight_x * (below + above) + weight_y * along_y + weight_z * along_z
            )
            new.append(v + inverse[x] * (rhs[x] - image))
        value = new
    return value


def coarse_diag_of(rows, weights):
    lane = iota(rows[0].shape, 1)
    base = 2.0 * (weights[0] + weights[1] + weights[2])
    out = []
    for row in rows:
        first = pltpu.roll(row, LANES - DIAG_LANE, 1)
        second = pltpu.roll(row, LANES - DIAG_LANE + KZ, 1)
        both = jnp.where(lane < KZ, first, jnp.where(lane < 2 * KZ, second, 0.0))
        out.append(base + both)
    return out


def up_blocks(place, value, spread, narrow, target):
    gx, gy = place[0], place[1]
    spread[...] = jnp.zeros(spread.shape, F32)
    stacked = jnp.concatenate(value, axis=0)
    lane_table = iota((LANES, LANES), 0)
    col = iota((LANES, LANES), 1) // (LANES // KZ)
    for r in range(2):
        wide = table_dot(stacked, (lane_table == r * KZ + col).astype(F32))
        for x in range(KX):
            spread[r, x + 1, pl.ds(8, KY), :] = wide[KY * x : KY * (x + 1)]
    odd = gy % 2
    low = gy // 2 + odd + 7
    row = iota((16, LANES), 0)
    limit = 4 + 8 * odd
    for r in range(2):
        for x in range(3):
            first = spread[r, gx + x, pl.ds(low, 1), :]
            second = spread[r, gx + x, pl.ds(low + 1, 1), :]
            tile = jnp.where(row < limit, first, second)
            for i in ((0, 1, 2), (3, 4, 5, 6), (7, 8, 9))[x]:
                target[r, i] = narrow[r, i] + tile


def post(place, value, spread, narrow, level_rhs, extra, guess, rhs, both, inv, s10, s8, s6, ups, f12, f10, out):
    up_blocks(place, value, spread, narrow, s10)
    linv = {x: inverse_of(extra(x)) for x in range(2, 10)}
    sweep_rows(s8, s10, level_rhs, extra, lambda x: linv[x], 8, 2, 2)
    sweep_rows(s6, s8, level_rhs, extra, lambda x: linv[x], 6, 3, 3)
    table_z = copy_table(LANES, 256)
    for r in range(2):
        for x in range(6):
            base = 32 * (6 * r + x)
            ups[pl.ds(base, 16, stride=2), :] = s6[r, x]
            ups[pl.ds(base + 1, 16, stride=2), :] = s6[r, x]
            wide = table_dot(ups[pl.ds(base + 4, 24), :], table_z)
            for i in range(2):
                f12[r, 2 * x + i] = guess[r, 2 * x + i] + wide
    kappa = lambda x: both[2, x]
    sweep_rows(f10, f12, rhs, kappa, lambda x: inv[x], 10, 2, 2)
    for r in range(2):
        for x in range(8):
            image = (6.0 + kappa(x + 3)) * f10[r, x + 1] - sides(f10, r, x + 1)
            out(r, x, f10[r, x + 1] + inv[x + 3] * (rhs(r, x + 3) - image))


def middle(row):
    return pltpu.roll(row, row.shape[0] - 4, 0)[0:16]


def share(alone, kappa, inv, image, zero, guess, sums):
    nothing = jnp.zeros((24, 256), F32)
    for r in range(2):
        for x in range(14):
            if 2 <= x < 12:
                image[r, x] = (6.0 + kappa(x)) * alone[r, x + 1] - sides(alone, r, x + 1)
                zero[r, x] = inv(x) * image[r, x]
            else:
                image[r, x] = nothing
                zero[r, x] = nothing
        for x in (0, 1, 14, 15):
            guess[r, x] = nothing
        for x in range(2, 14):
            back = (6.0 + kappa(x - 1)) * zero[r, x - 1] - sides(zero, r, x - 1)
            guess[r, x] = zero[r, x - 1] + inv(x - 1) * (image[r, x - 1] - back)
    pairs = []
    for r in range(2):
        rows = []
        for x in range(14):
            back = (6.0 + kappa(x)) * guess[r, x + 1] - sides(guess, r, x + 1)
            rows.append(image[r, x] - back)
        pairs = pairs + [rows[0]]
        pairs = pairs + [rows[2 * x + 1] + rows[2 * x + 2] for x in range(6)] + [rows[13]]
    return level_rows(pairs, sums)


def precond_kernel(weights, place, gathered, level, guess, both, inv,
                   precond, diag_out, part, low, high,
                   zero_level, narrow, alone, image, zero, guess_alone, sums,
                   spread, s10, s8, s6, ups, f12, f10):
    level_pre(lambda r, x: level[r, x], lambda x: level[2, x], narrow, zero_level, 4, 4)
    rows, rhs = coarse_rows(gathered)
    diag = coarse_diag_of(rows, weights)
    for x in range(KX):
        diag_out[x] = diag[x]
    value = coarse_solve(rhs, diag, weights)
    own = own_rows((24, 256), 4, 20)
    top = iota((8, LANES), 0) < 4
    for r in range(2):
        for x in (0, 1, 2, 3, 12, 13, 14, 15):
            alone[r, x] = jnp.zeros((24, 256), F32)

    def out(r, x, row):
        own_part = middle(row)
        precond[r, x] = own_part
        alone[r, x + 4] = jnp.where(own, row, 0.0)
        left, right = own_part[:, :LANES], own_part[:, LANES:]
        low[r, x, 0:8, :] = jnp.where(top, left[0:8], pltpu.roll(right[0:8], 4, 0))
        high[r, x, 0:8, :] = jnp.where(top, pltpu.roll(left[8:16], 4, 0), right[8:16])

    post(
        place, value, spread, narrow, lambda r, x: level[r, x], lambda x: level[2, x],
        guess, lambda r, x: both[r, x], both, inv, s10, s8, s6, ups, f12, f10, out,
    )
    level_row = share(
        alone, lambda x: both[2, x], lambda x: inv[x], image, zero, guess_alone, sums
    )
    for r in range(2):
        for x in range(8):
            row = level_row(8 * r + x)
            part[r, x] = row
            low[r, x, 8:16, :] = pltpu.roll(row, 14, 0)[0:8]
            high[r, x, 8:16, :] = row[8:16]


def final_kernel(weights, place, gathered, diag_in, narrow, level, first, guess, image, both, inv, precond, right,
                 solution_field, residual, direction, spread, s10, s8, s6, ups, f12, f10):
    rows, rhs = coarse_rows(gathered)
    diag = [diag_in[x] for x in range(KX)]
    value = coarse_solve(rhs, diag, weights)
    sums = jnp.sum(total(rows), axis=0, keepdims=True)
    product = jnp.sum(total([a * b for a, b in zip(rhs, value)]), axis=0, keepdims=True)
    line = iota(sums.shape, 1)

    def pick(row, low, high):
        return jnp.sum(jnp.where((line >= low) & (line < high), row, 0.0), axis=1, keepdims=True)

    alphas, betas = [], []
    for r in range(2):
        rz = pick(sums, TOTAL_LANE + r, TOTAL_LANE + r + 1)
        pq = pick(sums, TOTAL_LANE + 2 + r, TOTAL_LANE + 3 + r)
        energy = pick(sums, TOTAL_LANE + 4 + r, TOTAL_LANE + 5 + r)
        energy = energy + 4.0 * pick(product, r * KZ, (r + 1) * KZ)
        alpha = rz / pq
        alphas.append(alpha)
        betas.append(alpha * alpha * energy / rz - 1.0)

    def out(r, x, row):
        p = precond[r, x]
        solution_field[r, x] = alphas[r] * p
        residual[r, x] = right[r, x] - alphas[r] * middle(image[r, x + 3])
        direction[r, x] = p - alphas[r] * middle(row) + betas[r] * p

    post(
        place, value, spread, narrow, lambda r, x: level[r, x - 2], lambda x: first[2, x],
        guess, lambda r, x: image[r, x], both, inv, s10, s8, s6, ups, f12, f10, out,
    )


def call(kernel, outs, scratch, place=None):
    vmem = pl.BlockSpec(memory_space=pltpu.VMEM)

    def run(*args):
        specs = [vmem] * len(args)
        if place is not None:
            args = (place,) + args
            specs = [pl.BlockSpec(memory_space=pltpu.SMEM)] + specs
        return pl.pallas_call(
            kernel,
            out_shape=[jax.ShapeDtypeStruct(shape, F32) for shape in outs],
            in_specs=specs,
            out_specs=[vmem] * len(outs),
            scratch_shapes=[pltpu.VMEM(shape, F32) for shape in scratch],
            compiler_params=pltpu.CompilerParams(vmem_limit_bytes=40 * 1024 * 1024),
        )(*args)

    return run


def swap_y(low, high):
    count = lax.axis_size("gy")
    even = lax.axis_index("gy") % 2 == 0
    near_pairs = [(i, i + 1) for i in range(0, count, 2)]
    far_pairs = [(i, i + 1) for i in range(1, count - 1, 2)]
    near_pairs = near_pairs + [(b, a) for a, b in near_pairs]
    far_pairs = far_pairs + [(b, a) for a, b in far_pairs]
    far = lax.ppermute(jnp.where(even, low, high), "gy", far_pairs)
    near = lax.ppermute(jnp.where(even, high, low), "gy", near_pairs)
    return jnp.where(even, far, near), jnp.where(even, near, far)


def swap_x(low, high):
    count = lax.axis_size("gx")
    forward = [(i, i + 1) for i in range(count - 1)]
    backward = [(b, a) for a, b in forward]
    return lax.ppermute(high, "gx", forward), lax.ppermute(low, "gx", backward)


def extended(block, width_y, width_x, pad_y):
    low, high = swap_y(block[:, :, :width_y], block[:, :, block.shape[2] - width_y :])
    block = jnp.concatenate([low, block, high], axis=2)
    if pad_y:
        block = jnp.pad(block, ((0, 0), (0, 0), (pad_y, pad_y), (0, 0)))
    low, high = swap_x(block[:, :width_x], block[:, block.shape[1] - width_x :])
    return jnp.concatenate([low, block, high], axis=1)


def halves_to_rows(block):
    return jnp.concatenate([block[..., :LANES], block[..., LANES:]], axis=2)


def rows_to_halves(block):
    rows = block.shape[2] // 2
    return jnp.concatenate([block[:, :, :rows], block[:, :, rows:]], axis=3)


def exchange_shares(precond, part, low, high):
    low, high = swap_y(low, high)
    wide = jnp.concatenate([rows_to_halves(low[:, :, :8]), precond, rows_to_halves(high[:, :, :8])], axis=2)
    part = part + jnp.pad(low[:, :, 8:14], ((0, 0), (0, 0), (0, 10), (0, 0)))
    part = part + jnp.pad(high[:, :, 8:14], ((0, 0), (0, 0), (10, 0), (0, 0)))
    low = jnp.concatenate([halves_to_rows(wide[:, :4]), part[:, :4]], axis=2)
    high = jnp.concatenate([halves_to_rows(wide[:, 4:]), part[:, 4:]], axis=2)
    low, high = swap_x(low, high)
    wide = jnp.concatenate([rows_to_halves(low[:, :, :48]), wide, rows_to_halves(high[:, :, :48])], axis=1)
    part = jnp.concatenate([part[:, :4] + low[:, :, 48:], part[:, 4:] + high[:, :, 48:]], axis=1)
    return wide, part


def gather_all(line):
    size_x = lax.axis_size("gx")
    size_y = lax.axis_size("gy")
    spread = jnp.broadcast_to(line[None], (size_y, 1, LANES))
    rows = lax.all_to_all(spread, "gy", 0, 0, tiled=True).reshape(KY, size_y // KY, LANES)
    even, odd = rows[:, 0], rows[:, 1]
    other = jnp.pad(even[1:], ((0, 1), (0, 0))) + jnp.pad(odd[:-1], ((1, 0), (0, 0)))
    other = jnp.pad(other[:, OTHER_LANE : 2 * OTHER_LANE], ((0, 0), (0, LANES - OTHER_LANE)))
    rows = even + odd + other
    spread = jnp.broadcast_to(rows[None], (size_x, KY, LANES))
    return lax.all_to_all(spread, "gx", 0, 0, tiled=True)


def local(right_side, diagonal):
    block_x = right_side.shape[1] * lax.axis_size("gx") // 2 // KX
    block_y = right_side.shape[2] * lax.axis_size("gy") // 2 // KY
    block_z = right_side.shape[3] // 2 // KZ
    weights = (float(block_y * block_z), float(block_x * block_z), float(block_x * block_y))
    place = jnp.stack([lax.axis_index("gx"), lax.axis_index("gy")]).astype(jnp.int32)

    both = extended(jnp.concatenate([right_side, diagonal[None]], axis=0), 3, 3, 1)
    inv, guess, level, line = call(
        fine_kernel,
        [(14, 24, 256), (2, 12, 24, 256), (3, 4, 8, LANES), (1, LANES)],
        [(2, 14, 24, 256), (448, LANES), (2, 12, 16, LANES), (2, 10, 16, LANES)],
        place,
    )(both)
    gathered = gather_all(line)
    first = extended(level, 4, 4, 0)
    post_scratch = [
        (2, KX + 2, 8 + KY + 8, LANES), (2, 10, 16, LANES), (2, 8, 16, LANES), (2, 6, 16, LANES),
        (384, LANES), (2, 12, 24, 256), (2, 10, 24, 256),
    ]
    precond, diag, part, low, high = call(
        functools.partial(precond_kernel, weights),
        [(2, 8, 16, 256), (KX, KY, LANES), (2, 8, 16, LANES), (2, 8, 16, LANES), (2, 8, 16, LANES)],
        [
            (2, 12, 16, LANES), (2, 10, 16, LANES), (2, 16, 24, 256), (2, 14, 24, 256),
            (2, 14, 24, 256), (2, 16, 24, 256), (512, LANES),
        ] + post_scratch,
        place,
    )(gathered, first, guess, both, inv)
    wide, level_q = exchange_shares(precond, part, low, high)
    image, guess_q, inner, line_q = call(
        image_kernel,
        [(2, 14, 24, 256), (2, 12, 24, 256), (2, 6, 16, LANES), (1, LANES)],
        [(2, 14, 24, 256), (2, 8, 16, LANES)],
    )(wide, level_q, first, both, inv)
    gathered_q = gather_all(line_q)
    low, high = swap_x(inner[:, 2:4], inner[:, 2:4])
    narrow_q = jnp.concatenate([low, inner, high], axis=1)
    return tuple(
        call(
            functools.partial(final_kernel, weights),
            [(2, 8, 16, 256)] * 3,
            post_scratch,
            place,
        )(gathered_q, diag, narrow_q, level_q, first, guess_q, image, both, inv, precond, right_side)
    )


def solution(mesh):
    placed = (P(None, "gx", "gy", None), P("gx", "gy", None))
    return jax.shard_map(
        local,
        mesh=mesh,
        in_specs=placed,
        out_specs=(P(None, "gx", "gy", None),) * 3,
        check_vma=False,
    )
```

```python
import functools

import jax
import jax.numpy as jnp
from jax import lax
from jax.experimental import pallas as pl
from jax.experimental.pallas import tpu as pltpu
from jax.sharding import PartitionSpec as P

KX = 16
KY = 16
KZ = 8
CSWEEPS = 4
OMEGA = 0.8
HIGH = lax.Precision.HIGHEST
F32 = jnp.float32
LANES = 128
SIDE_LANE = 16
OTHER_LANE = 48
DIAG_GROUP = 12
DIAG_LANE = 96
TOTAL_LANE = 104


def dot(a, b):
    return jnp.dot(a, b, precision=HIGH, preferred_element_type=F32)


def table_dot(a, table):
    table = table.astype(jnp.bfloat16)
    out = None
    for _ in range(3):
        part = a.astype(jnp.bfloat16)
        a = a - part.astype(F32)
        product = jnp.dot(part, table, preferred_element_type=F32)
        out = product if out is None else out + product
    return out


def iota(shape, dim):
    return lax.broadcasted_iota(jnp.int32, shape, dim)


def z_sides(row):
    depth = row.shape[-1]
    lane = iota(row.shape, 1)
    before = jnp.where(lane == 0, 0.0, pltpu.roll(row, 1, 1))
    after = jnp.where(lane == depth - 1, 0.0, pltpu.roll(row, depth - 1, 1))
    return before + after


def sides(ref, r, x):
    row = ref[r, x]
    rows = row.shape[0]
    along_y = pltpu.roll(row, 1, 0) + pltpu.roll(row, rows - 1, 0)
    return ref[r, x - 1] + ref[r, x + 1] + along_y + z_sides(row)


def sweep_rows(out, field, rhs, kappa, inverse, count, shift_rhs, shift_diag):
    for r in range(2):
        for x in range(count):
            image = (6.0 + kappa(x + shift_diag)) * field[r, x + 1] - sides(field, r, x + 1)
            step = inverse(x + shift_diag) * (rhs(r, x + shift_rhs) - image)
            out[r, x] = field[r, x + 1] + step


def inverse_of(kappa):
    return jnp.where(kappa > 0.0, OMEGA / (6.0 + kappa), 0.0)


def pair_table(wide, narrow):
    return (iota((wide, narrow), 0) // 2 == iota((wide, narrow), 1)).astype(F32)


def copy_table(narrow, wide):
    return (iota((narrow, wide), 0) == iota((narrow, wide), 1) // 2).astype(F32)


def fine_pre(wide, kappa, inv, zero, guess, sums):
    for r in range(2):
        for x in range(14):
            zero[r, x] = inv(x) * wide[r, x]
    sweep_rows(guess, zero, lambda r, x: wide[r, x], kappa, inv, 12, 1, 1)
    left = []
    for r in range(2):
        rows = []
        for x in range(8):
            image = (6.0 + kappa(x + 3)) * guess[r, x + 2] - sides(guess, r, x + 2)
            rows.append(wide[r, x + 3] - image)
        left.append(rows)
    pairs = [left[r][2 * x] + left[r][2 * x + 1] for r in range(2) for x in range(4)]
    return level_rows(pairs + [kappa(2 * x + 1) + kappa(2 * x + 2) for x in range(6)], sums)


def level_rows(pairs, sums):
    table = pair_table(256, LANES)
    sums[...] = jnp.zeros(sums.shape, F32)
    for i, pair in enumerate(pairs):
        sums[pl.ds(32 * i + 4, 24), :] = table_dot(pair, table)

    def level_row(i):
        pair = sums[pl.ds(32 * i, 16, stride=2), :] + sums[pl.ds(32 * i + 1, 16, stride=2), :]
        return pair * 0.25

    return level_row


def own_rows(shape, low, high):
    row = iota(shape, 0)
    return (row >= low) & (row < high)


def own_eight(row):
    return pltpu.roll(row, 12, 0)[0:8]


def gathered_line(vectors):
    row = iota((16, LANES), 0)
    stacked = jnp.zeros((16, LANES), F32)
    for group, vector in vectors.items():
        stacked = jnp.where(row == group, vector, stacked)
    table = iota((LANES, LANES), 0) // (LANES // KZ) == iota((LANES, LANES), 1) % KZ
    spread = table_dot(stacked, table.astype(F32))
    return jnp.sum(jnp.where(iota((16, LANES), 1) // KZ == row, spread, 0.0), axis=0, keepdims=True)


def level_pre(rhs, extra, guess, zero, first, last):
    linv = [inverse_of(extra(x)) for x in range(12)]
    for r in range(2):
        for x in range(12):
            zero[r, x] = linv[x] * rhs(r, x)
    sweep_rows(guess, zero, rhs, extra, lambda x: linv[x], 10, 1, 1)
    left = []
    for r in range(2):
        rows = []
        for x in range(first, last):
            image = (6.0 + extra(x)) * guess[r, x - 1] - sides(guess, r, x - 1)
            rows.append(rhs(r, x) - image)
        left.append(rows)
    return left


def total(rows):
    out = rows[0]
    for row in rows[1:]:
        out = out + row
    return out


def fine_kernel(place, both, inv, guess, level, line, zero, sums, zero_level, guess_level):
    for x in range(14):
        inv[x] = inverse_of(both[2, x])
    level_row = fine_pre(both, lambda x: both[2, x], lambda x: inv[x], zero, guess, sums)
    own = own_rows((16, LANES), 4, 12)
    nothing = jnp.zeros((16, LANES), F32)
    rhs = [[jnp.where(own, level_row(4 * r + x), 0.0) for x in range(4)] for r in range(2)]
    extra = [level_row(8 + x) for x in range(6)]
    for r in range(2):
        for x in range(4):
            level[r, x] = own_eight(rhs[r][x])
    for x in range(4):
        level[2, x] = own_eight(extra[x + 1])
    left = level_pre(
        lambda r, x: rhs[r][x - 4] if 4 <= x < 8 else nothing,
        lambda x: extra[x - 3] if 3 <= x < 9 else nothing,
        guess_level, zero_level, 2, 10,
    )
    row = iota((16, LANES), 0)
    odd = place[1] % 2
    other = (row < 4 * (1 - odd)) | (row >= 16 - 4 * odd)
    vectors = {}
    for r in range(2):
        for side, rows in enumerate((left[r][2:6], left[r][0:2], left[r][6:8])):
            column = total(rows)
            for far in range(2):
                part = jnp.where(other, column, 0.0) if far else jnp.where(other, 0.0, column)
                vectors[(3 * far + side) * 2 + r] = jnp.sum(part, axis=0, keepdims=True)
    diag_sum = jnp.where(own, total(extra[1:5]), 0.0)
    vectors[DIAG_GROUP] = jnp.sum(diag_sum, axis=0, keepdims=True)
    line[...] = gathered_line(vectors)


def fold(field):
    folded = field[0:8] + field[8:16] + field[16:24]
    return folded[:, :LANES] + folded[:, LANES:]


def image_kernel(wide, level, first, both, inv, image, guess, narrow, line, zero, zero_level):
    for r in range(2):
        for x in range(14):
            image[r, x] = (6.0 + both[2, x]) * wide[r, x + 1] - sides(wide, r, x + 1)
            zero[r, x] = inv[x] * image[r, x]
    kappa = lambda x: both[2, x]
    sweep_rows(guess, zero, lambda r, x: image[r, x], kappa, lambda x: inv[x], 12, 1, 1)
    own = own_rows((24, 256), 4, 20)
    own_level = own_rows((16, LANES), 4, 12)
    extra = lambda x: first[2, x + 2]
    linv = [inverse_of(extra(x)) for x in range(8)]
    for r in range(2):
        for x in range(8):
            zero_level[r, x] = linv[x] * level[r, x]
    level_rhs = lambda r, x: level[r, x]
    sweep_rows(narrow, zero_level, level_rhs, extra, lambda x: linv[x], 6, 1, 1)
    vectors = {}
    totals = []
    for r in range(2):
        rz = total([both[r, x + 3] * wide[r, x + 4] for x in range(8)])
        pq = total([image[r, x + 3] * wide[r, x + 4] for x in range(8)])
        energy = None
        for x in range(8):
            back = (6.0 + both[2, x + 3]) * guess[r, x + 2] - sides(guess, r, x + 2)
            term = guess[r, x + 2] * (2.0 * image[r, x + 3] - back)
            energy = term if energy is None else energy + term
        energy = fold(jnp.where(own, energy, 0.0))
        column = None
        for x in range(4):
            back = (6.0 + extra(x + 2)) * narrow[r, x + 1] - sides(narrow, r, x + 1)
            left = level[r, x + 2] - back
            column = left if column is None else column + left
            term = narrow[r, x + 1] * (level[r, x + 2] + left)
            term = 4.0 * jnp.where(own_level, term, 0.0)
            energy = energy + term[0:8] + term[8:16]
        vectors[r] = jnp.sum(jnp.where(own_level, column, 0.0), axis=0, keepdims=True)
        totals.append((TOTAL_LANE + r, fold(jnp.where(own, rz, 0.0))))
        totals.append((TOTAL_LANE + 2 + r, fold(jnp.where(own, pq, 0.0))))
        totals.append((TOTAL_LANE + 4 + r, energy))
    out = gathered_line(vectors)
    lane = iota((1, LANES), 1)
    for place, part in totals:
        value = jnp.sum(jnp.sum(part, axis=0, keepdims=True), axis=1, keepdims=True)
        out = jnp.where(lane == place, value, out)
    line[...] = out


def coarse_rows(gathered):
    rows = [gathered[x] for x in range(KX)]
    lane = iota(rows[0].shape, 1)
    out = []
    for x in range(KX):
        row = rows[x]
        if x < KX - 1:
            row = row + pltpu.roll(rows[x + 1], LANES - SIDE_LANE, 1)
        if x > 0:
            row = row + pltpu.roll(rows[x - 1], LANES - 2 * SIDE_LANE, 1)
        out.append(jnp.where(lane < 2 * KZ, row, 0.0))
    return rows, out


def coarse_solve(rhs, diag, weights):
    weight_x, weight_y, weight_z = weights
    shape = rhs[0].shape
    row = iota(shape, 0)
    lane = iota(shape, 1) % KZ
    inverse = [OMEGA / d for d in diag]
    value = [i * b for i, b in zip(inverse, rhs)]
    nothing = jnp.zeros(shape, F32)
    for _ in range(CSWEEPS - 1):
        new = []
        for x in range(KX):
            v = value[x]
            below = value[x - 1] if x > 0 else nothing
            above = value[x + 1] if x < KX - 1 else nothing
            along_y = jnp.where(row == 0, 0.0, pltpu.roll(v, 1, 0))
            along_y = along_y + jnp.where(row == KY - 1, 0.0, pltpu.roll(v, shape[0] - 1, 0))
            along_z = jnp.where(lane == 0, 0.0, pltpu.roll(v, 1, 1))
            along_z = along_z + jnp.where(lane == KZ - 1, 0.0, pltpu.roll(v, LANES - 1, 1))
            image = diag[x] * v - (
                weight_x * (below + above) + weight_y * along_y + weight_z * along_z
            )
            new.append(v + inverse[x] * (rhs[x] - image))
        value = new
    return value


def coarse_diag_of(rows, weights):
    lane = iota(rows[0].shape, 1)
    base = 2.0 * (weights[0] + weights[1] + weights[2])
    out = []
    for row in rows:
        first = pltpu.roll(row, LANES - DIAG_LANE, 1)
        second = pltpu.roll(row, LANES - DIAG_LANE + KZ, 1)
        both = jnp.where(lane < KZ, first, jnp.where(lane < 2 * KZ, second, 0.0))
        out.append(base + both)
    return out


def up_blocks(place, value, spread, narrow, target):
    gx, gy = place[0], place[1]
    spread[...] = jnp.zeros(spread.shape, F32)
    stacked = jnp.concatenate(value, axis=0)
    lane_table = iota((LANES, LANES), 0)
    col = iota((LANES, LANES), 1) // (LANES // KZ)
    for r in range(2):
        wide = table_dot(stacked, (lane_table == r * KZ + col).astype(F32))
        for x in range(KX):
            spread[r, x + 1, pl.ds(8, KY), :] = wide[KY * x : KY * (x + 1)]
    odd = gy % 2
    low = gy // 2 + odd + 7
    row = iota((16, LANES), 0)
    limit = 4 + 8 * odd
    for r in range(2):
        for x in range(3):
            first = spread[r, gx + x, pl.ds(low, 1), :]
            second = spread[r, gx + x, pl.ds(low + 1, 1), :]
            tile = jnp.where(row < limit, first, second)
            for i in ((0, 1, 2), (3, 4, 5, 6), (7, 8, 9))[x]:
                target[r, i] = narrow[r, i] + tile


def post(place, value, spread, narrow, level_rhs, extra, guess, rhs, both, inv, s10, s8, s6, ups, f12, f10, out):
    up_blocks(place, value, spread, narrow, s10)
    linv = {x: inverse_of(extra(x)) for x in range(2, 10)}
    sweep_rows(s8, s10, level_rhs, extra, lambda x: linv[x], 8, 2, 2)
    sweep_rows(s6, s8, level_rhs, extra, lambda x: linv[x], 6, 3, 3)
    table_z = copy_table(LANES, 256)
    for r in range(2):
        for x in range(6):
            base = 32 * (6 * r + x)
            ups[pl.ds(base, 16, stride=2), :] = s6[r, x]
            ups[pl.ds(base + 1, 16, stride=2), :] = s6[r, x]
            wide = table_dot(ups[pl.ds(base + 4, 24), :], table_z)
            for i in range(2):
                f12[r, 2 * x + i] = guess[r, 2 * x + i] + wide
    kappa = lambda x: both[2, x]
    sweep_rows(f10, f12, rhs, kappa, lambda x: inv[x], 10, 2, 2)
    for r in range(2):
        for x in range(8):
            image = (6.0 + kappa(x + 3)) * f10[r, x + 1] - sides(f10, r, x + 1)
            out(r, x, f10[r, x + 1] + inv[x + 3] * (rhs(r, x + 3) - image))


def middle(row):
    return pltpu.roll(row, row.shape[0] - 4, 0)[0:16]


def share(alone, kappa, inv, image, zero, guess, sums):
    nothing = jnp.zeros((24, 256), F32)
    for r in range(2):
        for x in range(14):
            if 2 <= x < 12:
                image[r, x] = (6.0 + kappa(x)) * alone[r, x + 1] - sides(alone, r, x + 1)
                zero[r, x] = inv(x) * image[r, x]
            else:
                image[r, x] = nothing
                zero[r, x] = nothing
        for x in (0, 1, 14, 15):
            guess[r, x] = nothing
        for x in range(2, 14):
            back = (6.0 + kappa(x - 1)) * zero[r, x - 1] - sides(zero, r, x - 1)
            guess[r, x] = zero[r, x - 1] + inv(x - 1) * (image[r, x - 1] - back)
    pairs = []
    for r in range(2):
        rows = []
        for x in range(14):
            back = (6.0 + kappa(x)) * guess[r, x + 1] - sides(guess, r, x + 1)
            rows.append(image[r, x] - back)
        pairs = pairs + [rows[0]]
        pairs = pairs + [rows[2 * x + 1] + rows[2 * x + 2] for x in range(6)] + [rows[13]]
    return level_rows(pairs, sums)


def precond_kernel(weights, place, gathered, level, guess, both, inv,
                   precond, diag_out, part, low, high,
                   zero_level, narrow, alone, image, zero, guess_alone, sums,
                   spread, s10, s8, s6, ups, f12, f10):
    level_pre(lambda r, x: level[r, x], lambda x: level[2, x], narrow, zero_level, 4, 4)
    rows, rhs = coarse_rows(gathered)
    diag = coarse_diag_of(rows, weights)
    for x in range(KX):
        diag_out[x] = diag[x]
    value = coarse_solve(rhs, diag, weights)
    own = own_rows((24, 256), 4, 20)
    top = iota((8, LANES), 0) < 4
    for r in range(2):
        for x in (0, 1, 2, 3, 12, 13, 14, 15):
            alone[r, x] = jnp.zeros((24, 256), F32)

    def out(r, x, row):
        own_part = middle(row)
        precond[r, x] = own_part
        alone[r, x + 4] = jnp.where(own, row, 0.0)
        left, right = own_part[:, :LANES], own_part[:, LANES:]
        low[r, x, 0:8, :] = jnp.where(top, left[0:8], pltpu.roll(right[0:8], 4, 0))
        high[r, x, 0:8, :] = jnp.where(top, pltpu.roll(left[8:16], 4, 0), right[8:16])

    post(
        place, value, spread, narrow, lambda r, x: level[r, x], lambda x: level[2, x],
        guess, lambda r, x: both[r, x], both, inv, s10, s8, s6, ups, f12, f10, out,
    )
    level_row = share(
        alone, lambda x: both[2, x], lambda x: inv[x], image, zero, guess_alone, sums
    )
    for r in range(2):
        for x in range(8):
            row = level_row(8 * r + x)
            part[r, x] = row
            low[r, x, 8:16, :] = pltpu.roll(row, 14, 0)[0:8]
            high[r, x, 8:16, :] = row[8:16]


def final_kernel(weights, place, gathered, diag_in, narrow, level, first, guess, image, both, inv, precond, right,
                 solution_field, residual, direction, spread, s10, s8, s6, ups, f12, f10):
    rows, rhs = coarse_rows(gathered)
    diag = [diag_in[x] for x in range(KX)]
    value = coarse_solve(rhs, diag, weights)
    sums = jnp.sum(total(rows), axis=0, keepdims=True)
    product = jnp.sum(total([a * b for a, b in zip(rhs, value)]), axis=0, keepdims=True)
    line = iota(sums.shape, 1)

    def pick(row, low, high):
        return jnp.sum(jnp.where((line >= low) & (line < high), row, 0.0), axis=1, keepdims=True)

    alphas, betas = [], []
    for r in range(2):
        rz = pick(sums, TOTAL_LANE + r, TOTAL_LANE + r + 1)
        pq = pick(sums, TOTAL_LANE + 2 + r, TOTAL_LANE + 3 + r)
        energy = pick(sums, TOTAL_LANE + 4 + r, TOTAL_LANE + 5 + r)
        energy = energy + 4.0 * pick(product, r * KZ, (r + 1) * KZ)
        alpha = rz / pq
        alphas.append(alpha)
        betas.append(alpha * alpha * energy / rz - 1.0)

    def out(r, x, row):
        p = precond[r, x]
        solution_field[r, x] = alphas[r] * p
        residual[r, x] = right[r, x] - alphas[r] * middle(image[r, x + 3])
        direction[r, x] = p - alphas[r] * middle(row) + betas[r] * p

    post(
        place, value, spread, narrow, lambda r, x: level[r, x - 2], lambda x: first[2, x],
        guess, lambda r, x: image[r, x], both, inv, s10, s8, s6, ups, f12, f10, out,
    )


def call(kernel, outs, scratch, place=None):
    vmem = pl.BlockSpec(memory_space=pltpu.VMEM)

    def run(*args):
        specs = [vmem] * len(args)
        if place is not None:
            args = (place,) + args
            specs = [pl.BlockSpec(memory_space=pltpu.SMEM)] + specs
        return pl.pallas_call(
            kernel,
            out_shape=[jax.ShapeDtypeStruct(shape, F32) for shape in outs],
            in_specs=specs,
            out_specs=[vmem] * len(outs),
            scratch_shapes=[pltpu.VMEM(shape, F32) for shape in scratch],
            compiler_params=pltpu.CompilerParams(vmem_limit_bytes=16 * 1024 * 1024),
        )(*args)

    return run


def swap_y(low, high):
    count = lax.axis_size("gy")
    even = lax.axis_index("gy") % 2 == 0
    near_pairs = [(i, i + 1) for i in range(0, count, 2)]
    far_pairs = [(i, i + 1) for i in range(1, count - 1, 2)]
    near_pairs = near_pairs + [(b, a) for a, b in near_pairs]
    far_pairs = far_pairs + [(b, a) for a, b in far_pairs]
    far = lax.ppermute(jnp.where(even, low, high), "gy", far_pairs)
    near = lax.ppermute(jnp.where(even, high, low), "gy", near_pairs)
    return jnp.where(even, far, near), jnp.where(even, near, far)


def swap_x(low, high):
    count = lax.axis_size("gx")
    forward = [(i, i + 1) for i in range(count - 1)]
    backward = [(b, a) for a, b in forward]
    return lax.ppermute(high, "gx", forward), lax.ppermute(low, "gx", backward)


def extended(block, width_y, width_x, pad_y):
    low, high = swap_y(block[:, :, :width_y], block[:, :, block.shape[2] - width_y :])
    block = jnp.concatenate([low, block, high], axis=2)
    if pad_y:
        block = jnp.pad(block, ((0, 0), (0, 0), (pad_y, pad_y), (0, 0)))
    low, high = swap_x(block[:, :width_x], block[:, block.shape[1] - width_x :])
    return jnp.concatenate([low, block, high], axis=1)


def halves_to_rows(block):
    return jnp.concatenate([block[..., :LANES], block[..., LANES:]], axis=2)


def rows_to_halves(block):
    rows = block.shape[2] // 2
    return jnp.concatenate([block[:, :, :rows], block[:, :, rows:]], axis=3)


def exchange_shares(precond, part, low, high):
    low, high = swap_y(low, high)
    wide = jnp.concatenate([rows_to_halves(low[:, :, :8]), precond, rows_to_halves(high[:, :, :8])], axis=2)
    part = part + jnp.pad(low[:, :, 8:14], ((0, 0), (0, 0), (0, 10), (0, 0)))
    part = part + jnp.pad(high[:, :, 8:14], ((0, 0), (0, 0), (10, 0), (0, 0)))
    low = jnp.concatenate([halves_to_rows(wide[:, :4]), part[:, :4]], axis=2)
    high = jnp.concatenate([halves_to_rows(wide[:, 4:]), part[:, 4:]], axis=2)
    low, high = swap_x(low, high)
    wide = jnp.concatenate([rows_to_halves(low[:, :, :48]), wide, rows_to_halves(high[:, :, :48])], axis=1)
    part = jnp.concatenate([part[:, :4] + low[:, :, 48:], part[:, 4:] + high[:, :, 48:]], axis=1)
    return wide, part


def gather_all(line, beside):
    size_x = lax.axis_size("gx")
    size_y = lax.axis_size("gy")
    spread = jnp.broadcast_to(line[None], (size_y, 1, LANES))
    rows = lax.all_to_all(spread, "gy", 0, 0, tiled=True).reshape(KY, size_y // KY, LANES)
    even, odd = rows[:, 0], rows[:, 1]
    other = jnp.pad(even[1:], ((0, 1), (0, 0))) + jnp.pad(odd[:-1], ((1, 0), (0, 0)))
    other = jnp.pad(other[:, OTHER_LANE : 2 * OTHER_LANE], ((0, 0), (0, LANES - OTHER_LANE)))
    rows, beside = lax.optimization_barrier((even + odd + other, beside))
    spread = jnp.broadcast_to(rows[None], (size_x, KY, LANES))
    return lax.all_to_all(spread, "gx", 0, 0, tiled=True), beside


def local(right_side, diagonal):
    block_x = right_side.shape[1] * lax.axis_size("gx") // 2 // KX
    block_y = right_side.shape[2] * lax.axis_size("gy") // 2 // KY
    block_z = right_side.shape[3] // 2 // KZ
    weights = (float(block_y * block_z), float(block_x * block_z), float(block_x * block_y))
    place = jnp.stack([lax.axis_index("gx"), lax.axis_index("gy")]).astype(jnp.int32)

    both = extended(jnp.concatenate([right_side, diagonal[None]], axis=0), 3, 3, 1)
    inv, guess, level, line = call(
        fine_kernel,
        [(14, 24, 256), (2, 12, 24, 256), (3, 4, 8, LANES), (1, LANES)],
        [(2, 14, 24, 256), (448, LANES), (2, 12, 16, LANES), (2, 10, 16, LANES)],
        place,
    )(both)
    gathered, first = gather_all(line, extended(level, 4, 4, 0))
    post_scratch = [
        (2, KX + 2, 8 + KY + 8, LANES), (2, 10, 16, LANES), (2, 8, 16, LANES), (2, 6, 16, LANES),
        (384, LANES), (2, 12, 24, 256), (2, 10, 24, 256),
    ]
    precond, diag, part, low, high = call(
        functools.partial(precond_kernel, weights),
        [(2, 8, 16, 256), (KX, KY, LANES), (2, 8, 16, LANES), (2, 8, 16, LANES), (2, 8, 16, LANES)],
        [
            (2, 12, 16, LANES), (2, 10, 16, LANES), (2, 16, 24, 256), (2, 14, 24, 256),
            (2, 14, 24, 256), (2, 16, 24, 256), (512, LANES),
        ] + post_scratch,
        place,
    )(gathered, first, guess, both, inv)
    wide, level_q = exchange_shares(precond, part, low, high)
    image, guess_q, inner, line_q = call(
        image_kernel,
        [(2, 14, 24, 256), (2, 12, 24, 256), (2, 6, 16, LANES), (1, LANES)],
        [(2, 14, 24, 256), (2, 8, 16, LANES)],
    )(wide, level_q, first, both, inv)
    low, high = swap_x(inner[:, 2:4], inner[:, 2:4])
    gathered_q, narrow_q = gather_all(line_q, jnp.concatenate([low, inner, high], axis=1))
    return tuple(
        call(
            functools.partial(final_kernel, weights),
            [(2, 8, 16, 256)] * 3,
            post_scratch,
            place,
        )(gathered_q, diag, narrow_q, level_q, first, guess_q, image, both, inv, precond, right_side)
    )


def solution(mesh):
    placed = (P(None, "gx", "gy", None), P("gx", "gy", None))
    return jax.shard_map(
        local,
        mesh=mesh,
        in_specs=placed,
        out_specs=(P(None, "gx", "gy", None),) * 3,
        check_vma=False,
    )
```

```python
import functools

import jax
import jax.numpy as jnp
from jax import lax
from jax.experimental import pallas as pl
from jax.experimental.pallas import tpu as pltpu
from jax.sharding import PartitionSpec as P

KX = 16
KY = 16
KZ = 8
CSWEEPS = 4
OMEGA = 0.8
HIGH = lax.Precision.HIGHEST
F32 = jnp.float32
LANES = 128
SIDE_LANE = 16
OTHER_LANE = 48
DIAG_GROUP = 12
DIAG_LANE = 96
TOTAL_LANE = 104


def dot(a, b):
    return jnp.dot(a, b, precision=HIGH, preferred_element_type=F32)


def table_dot(a, table):
    table = table.astype(jnp.bfloat16)
    out = None
    for _ in range(3):
        part = a.astype(jnp.bfloat16)
        a = a - part.astype(F32)
        product = jnp.dot(part, table, preferred_element_type=F32)
        out = product if out is None else out + product
    return out


def iota(shape, dim):
    return lax.broadcasted_iota(jnp.int32, shape, dim)


def z_sides(row):
    depth = row.shape[-1]
    lane = iota(row.shape, 1)
    before = jnp.where(lane == 0, 0.0, pltpu.roll(row, 1, 1))
    after = jnp.where(lane == depth - 1, 0.0, pltpu.roll(row, depth - 1, 1))
    return before + after


def sides(ref, r, x):
    row = ref[r, x]
    rows = row.shape[0]
    along_y = pltpu.roll(row, 1, 0) + pltpu.roll(row, rows - 1, 0)
    return ref[r, x - 1] + ref[r, x + 1] + along_y + z_sides(row)


def swept(field, rhs, inverse, r, x):
    return (1.0 - OMEGA) * field[r, x] + inverse * (rhs + sides(field, r, x))


def sweep_rows(out, field, rhs, inverse, count, shift):
    for r in range(2):
        for x in range(count):
            out[r, x] = swept(field, rhs(r, x + shift), inverse(x + shift), r, x + 1)


def inverse_of(kappa):
    return jnp.where(kappa > 0.0, OMEGA / (6.0 + kappa), 0.0)


def pair_table(wide, narrow):
    return (iota((wide, narrow), 0) // 2 == iota((wide, narrow), 1)).astype(F32)


def copy_table(narrow, wide):
    return (iota((narrow, wide), 0) == iota((narrow, wide), 1) // 2).astype(F32)


def fine_pre(wide, kappa, inv, zero, guess, sums):
    for r in range(2):
        for x in range(14):
            zero[r, x] = inv(x) * wide[r, x]
    sweep_rows(guess, zero, lambda r, x: wide[r, x], inv, 12, 1)
    left = []
    for r in range(2):
        rows = []
        for x in range(8):
            image = (6.0 + kappa(x + 3)) * guess[r, x + 2] - sides(guess, r, x + 2)
            rows.append(wide[r, x + 3] - image)
        left.append(rows)
    pairs = [left[r][2 * x] + left[r][2 * x + 1] for r in range(2) for x in range(4)]
    return level_rows(pairs + [kappa(2 * x + 1) + kappa(2 * x + 2) for x in range(6)], sums)


def level_rows(pairs, sums):
    table = pair_table(256, LANES)
    sums[...] = jnp.zeros(sums.shape, F32)
    for i, pair in enumerate(pairs):
        sums[pl.ds(32 * i + 4, 24), :] = table_dot(pair, table)

    def level_row(i):
        pair = sums[pl.ds(32 * i, 16, stride=2), :] + sums[pl.ds(32 * i + 1, 16, stride=2), :]
        return pair * 0.25

    return level_row


def own_rows(shape, low, high):
    row = iota(shape, 0)
    return (row >= low) & (row < high)


def own_eight(row):
    return pltpu.roll(row, 12, 0)[0:8]


def gathered_line(vectors):
    row = iota((16, LANES), 0)
    stacked = jnp.zeros((16, LANES), F32)
    for group, vector in vectors.items():
        stacked = jnp.where(row == group, vector, stacked)
    table = iota((LANES, LANES), 0) // (LANES // KZ) == iota((LANES, LANES), 1) % KZ
    spread = table_dot(stacked, table.astype(F32))
    return jnp.sum(jnp.where(iota((16, LANES), 1) // KZ == row, spread, 0.0), axis=0, keepdims=True)


def level_pre(rhs, extra, guess, zero, first, last):
    linv = [inverse_of(extra(x)) for x in range(12)]
    for r in range(2):
        for x in range(12):
            zero[r, x] = linv[x] * rhs(r, x)
    sweep_rows(guess, zero, rhs, lambda x: linv[x], 10, 1)
    left = []
    for r in range(2):
        rows = []
        for x in range(first, last):
            image = (6.0 + extra(x)) * guess[r, x - 1] - sides(guess, r, x - 1)
            rows.append(rhs(r, x) - image)
        left.append(rows)
    return left


def total(rows):
    out = rows[0]
    for row in rows[1:]:
        out = out + row
    return out


def fine_kernel(place, both, inv, guess, level, line, zero, sums, zero_level, guess_level):
    for x in range(14):
        inv[x] = inverse_of(both[2, x])
    level_row = fine_pre(both, lambda x: both[2, x], lambda x: inv[x], zero, guess, sums)
    own = own_rows((16, LANES), 4, 12)
    nothing = jnp.zeros((16, LANES), F32)
    rhs = [[jnp.where(own, level_row(4 * r + x), 0.0) for x in range(4)] for r in range(2)]
    extra = [level_row(8 + x) for x in range(6)]
    for r in range(2):
        for x in range(4):
            level[r, x] = own_eight(rhs[r][x])
    for x in range(4):
        level[2, x] = own_eight(extra[x + 1])
    left = level_pre(
        lambda r, x: rhs[r][x - 4] if 4 <= x < 8 else nothing,
        lambda x: extra[x - 3] if 3 <= x < 9 else nothing,
        guess_level, zero_level, 2, 10,
    )
    row = iota((16, LANES), 0)
    odd = place[1] % 2
    other = (row < 4 * (1 - odd)) | (row >= 16 - 4 * odd)
    vectors = {}
    for r in range(2):
        for side, rows in enumerate((left[r][2:6], left[r][0:2], left[r][6:8])):
            column = total(rows)
            for far in range(2):
                part = jnp.where(other, column, 0.0) if far else jnp.where(other, 0.0, column)
                vectors[(3 * far + side) * 2 + r] = jnp.sum(part, axis=0, keepdims=True)
    diag_sum = jnp.where(own, total(extra[1:5]), 0.0)
    vectors[DIAG_GROUP] = jnp.sum(diag_sum, axis=0, keepdims=True)
    line[...] = jnp.broadcast_to(gathered_line(vectors)[None], line.shape)


def pack_kernel(place, level, far, near):
    even = place[1] % 2 == 0
    top = iota((8, LANES), 0) < 4
    for c in range(3):
        for i in range(2):
            one, two = level[c, 2 * i], level[c, 2 * i + 1]
            low = jnp.where(top, one, pltpu.roll(two, 4, 0))
            high = jnp.where(top, pltpu.roll(one, 4, 0), two)
            far[c, i] = jnp.where(even, low, high)
            near[c, i] = jnp.where(even, high, low)


def fold(field):
    folded = field[0:8] + field[8:16] + field[16:24]
    return folded[:, :LANES] + folded[:, LANES:]


def image_kernel(wide, level, first, both, inv, image, narrow, line, zero, guess, zero_level):
    for r in range(2):
        for x in range(14):
            image[r, x] = (6.0 + both[2, x]) * wide[r, x + 1] - sides(wide, r, x + 1)
            zero[r, x] = inv[x] * image[r, x]
    sweep_rows(guess, zero, lambda r, x: image[r, x], lambda x: inv[x], 12, 1)
    own = own_rows((24, 256), 4, 20)
    own_level = own_rows((16, LANES), 4, 12)
    extra = lambda x: first[2, x + 2]
    linv = [inverse_of(extra(x)) for x in range(8)]
    for r in range(2):
        for x in range(8):
            zero_level[r, x] = linv[x] * level[r, x]
    level_rhs = lambda r, x: level[r, x]
    sweep_rows(narrow, zero_level, level_rhs, lambda x: linv[x], 6, 1)
    vectors = {}
    totals = []
    for r in range(2):
        rz = total([both[r, x + 3] * wide[r, x + 4] for x in range(8)])
        pq = total([image[r, x + 3] * wide[r, x + 4] for x in range(8)])
        energy = None
        for x in range(8):
            back = (6.0 + both[2, x + 3]) * guess[r, x + 2] - sides(guess, r, x + 2)
            term = guess[r, x + 2] * (2.0 * image[r, x + 3] - back)
            energy = term if energy is None else energy + term
        energy = fold(jnp.where(own, energy, 0.0))
        column = None
        for x in range(4):
            back = (6.0 + extra(x + 2)) * narrow[r, x + 1] - sides(narrow, r, x + 1)
            left = level[r, x + 2] - back
            column = left if column is None else column + left
            term = narrow[r, x + 1] * (level[r, x + 2] + left)
            term = 4.0 * jnp.where(own_level, term, 0.0)
            energy = energy + term[0:8] + term[8:16]
        vectors[r] = jnp.sum(jnp.where(own_level, column, 0.0), axis=0, keepdims=True)
        totals.append((TOTAL_LANE + r, fold(jnp.where(own, rz, 0.0))))
        totals.append((TOTAL_LANE + 2 + r, fold(jnp.where(own, pq, 0.0))))
        totals.append((TOTAL_LANE + 4 + r, energy))
    out = gathered_line(vectors)
    lane = iota((1, LANES), 1)
    for place, part in totals:
        value = jnp.sum(jnp.sum(part, axis=0, keepdims=True), axis=1, keepdims=True)
        out = jnp.where(lane == place, value, out)
    line[...] = jnp.broadcast_to(out[None], line.shape)


def coarse_rows(gathered):
    rows = [gathered[x] for x in range(KX)]
    lane = iota(rows[0].shape, 1)
    out = []
    for x in range(KX):
        row = rows[x]
        if x < KX - 1:
            row = row + pltpu.roll(rows[x + 1], LANES - SIDE_LANE, 1)
        if x > 0:
            row = row + pltpu.roll(rows[x - 1], LANES - 2 * SIDE_LANE, 1)
        out.append(jnp.where(lane < 2 * KZ, row, 0.0))
    return rows, out


def coarse_solve(rhs, diag, weights):
    weight_x, weight_y, weight_z = weights
    shape = rhs[0].shape
    row = iota(shape, 0)
    lane = iota(shape, 1) % KZ
    inverse = [OMEGA / d for d in diag]
    value = [i * b for i, b in zip(inverse, rhs)]
    nothing = jnp.zeros(shape, F32)
    for _ in range(CSWEEPS - 1):
        new = []
        for x in range(KX):
            v = value[x]
            below = value[x - 1] if x > 0 else nothing
            above = value[x + 1] if x < KX - 1 else nothing
            along_y = jnp.where(row == 0, 0.0, pltpu.roll(v, 1, 0))
            along_y = along_y + jnp.where(row == KY - 1, 0.0, pltpu.roll(v, shape[0] - 1, 0))
            along_z = jnp.where(lane == 0, 0.0, pltpu.roll(v, 1, 1))
            along_z = along_z + jnp.where(lane == KZ - 1, 0.0, pltpu.roll(v, LANES - 1, 1))
            image = diag[x] * v - (
                weight_x * (below + above) + weight_y * along_y + weight_z * along_z
            )
            new.append(v + inverse[x] * (rhs[x] - image))
        value = new
    return value


def coarse_diag_of(rows, weights):
    lane = iota(rows[0].shape, 1)
    base = 2.0 * (weights[0] + weights[1] + weights[2])
    out = []
    for row in rows:
        first = pltpu.roll(row, LANES - DIAG_LANE, 1)
        second = pltpu.roll(row, LANES - DIAG_LANE + KZ, 1)
        both = jnp.where(lane < KZ, first, jnp.where(lane < 2 * KZ, second, 0.0))
        out.append(base + both)
    return out


def up_blocks(place, value, spread, narrow, target):
    gx, gy = place[0], place[1]
    spread[...] = jnp.zeros(spread.shape, F32)
    stacked = jnp.concatenate(value, axis=0)
    lane_table = iota((LANES, LANES), 0)
    col = iota((LANES, LANES), 1) // (LANES // KZ)
    for r in range(2):
        wide = table_dot(stacked, (lane_table == r * KZ + col).astype(F32))
        for x in range(KX):
            spread[r, x + 1, pl.ds(8, KY), :] = wide[KY * x : KY * (x + 1)]
    odd = gy % 2
    low = gy // 2 + odd + 7
    row = iota((16, LANES), 0)
    limit = 4 + 8 * odd
    for r in range(2):
        for x in range(3):
            first = spread[r, gx + x, pl.ds(low, 1), :]
            second = spread[r, gx + x, pl.ds(low + 1, 1), :]
            tile = jnp.where(row < limit, first, second)
            for i in ((0, 1, 2), (3, 4, 5, 6), (7, 8, 9))[x]:
                target[r, i] = narrow[r, i] + tile


def post(place, value, spread, narrow, level_rhs, extra, guess, rhs, inv, s10, s8, s6, ups, f12, f10, out):
    up_blocks(place, value, spread, narrow, s10)
    linv = {x: inverse_of(extra(x)) for x in range(2, 10)}
    sweep_rows(s8, s10, level_rhs, lambda x: linv[x], 8, 2)
    sweep_rows(s6, s8, level_rhs, lambda x: linv[x], 6, 3)
    table_z = copy_table(LANES, 256)
    for r in range(2):
        for x in range(6):
            base = 32 * (6 * r + x)
            ups[pl.ds(base, 16, stride=2), :] = s6[r, x]
            ups[pl.ds(base + 1, 16, stride=2), :] = s6[r, x]
            wide = table_dot(ups[pl.ds(base + 4, 24), :], table_z)
            for i in range(2):
                f12[r, 2 * x + i] = guess[r, 2 * x + i] + wide
    sweep_rows(f10, f12, rhs, lambda x: inv[x], 10, 2)
    for r in range(2):
        for x in range(8):
            out(r, x, swept(f10, rhs(r, x + 3), inv[x + 3], r, x + 1))


def middle(row):
    return pltpu.roll(row, row.shape[0] - 4, 0)[0:16]


def share(alone, kappa, inv, image, zero, guess, sums):
    nothing = jnp.zeros((24, 256), F32)
    for r in range(2):
        for x in range(14):
            if 2 <= x < 12:
                image[r, x] = (6.0 + kappa(x)) * alone[r, x + 1] - sides(alone, r, x + 1)
                zero[r, x] = inv(x) * image[r, x]
            else:
                image[r, x] = nothing
                zero[r, x] = nothing
        for x in (0, 1, 14, 15):
            guess[r, x] = nothing
        for x in range(2, 14):
            guess[r, x] = swept(zero, image[r, x - 1], inv(x - 1), r, x - 1)
    pairs = []
    for r in range(2):
        rows = []
        for x in range(14):
            back = (6.0 + kappa(x)) * guess[r, x + 1] - sides(guess, r, x + 1)
            rows.append(image[r, x] - back)
        pairs = pairs + [rows[0]]
        pairs = pairs + [rows[2 * x + 1] + rows[2 * x + 2] for x in range(6)] + [rows[13]]
    return level_rows(pairs, sums)


def precond_kernel(weights, place, gathered, level, guess, both, inv,
                   precond, diag_out, part, low, high,
                   zero_level, narrow, alone, image, zero, guess_alone, sums,
                   spread, s10, s8, s6, ups, f12, f10):
    level_pre(lambda r, x: level[r, x], lambda x: level[2, x], narrow, zero_level, 4, 4)
    rows, rhs = coarse_rows(gathered)
    diag = coarse_diag_of(rows, weights)
    for x in range(KX):
        diag_out[x] = diag[x]
    value = coarse_solve(rhs, diag, weights)
    own = own_rows((24, 256), 4, 20)
    top = iota((8, LANES), 0) < 4
    for r in range(2):
        for x in (0, 1, 2, 3, 12, 13, 14, 15):
            alone[r, x] = jnp.zeros((24, 256), F32)

    def out(r, x, row):
        own_part = middle(row)
        precond[r, x] = own_part
        alone[r, x + 4] = jnp.where(own, row, 0.0)
        left, right = own_part[:, :LANES], own_part[:, LANES:]
        low[r, x, 0:8, :] = jnp.where(top, left[0:8], pltpu.roll(right[0:8], 4, 0))
        high[r, x, 0:8, :] = jnp.where(top, pltpu.roll(left[8:16], 4, 0), right[8:16])

    post(
        place, value, spread, narrow, lambda r, x: level[r, x], lambda x: level[2, x],
        guess, lambda r, x: both[r, x], inv, s10, s8, s6, ups, f12, f10, out,
    )
    level_row = share(
        alone, lambda x: both[2, x], lambda x: inv[x], image, zero, guess_alone, sums
    )
    for r in range(2):
        for x in range(8):
            row = level_row(8 * r + x)
            part[r, x] = row
            low[r, x, 8:16, :] = pltpu.roll(row, 14, 0)[0:8]
            high[r, x, 8:16, :] = row[8:16]


def final_kernel(weights, place, gathered, diag_in, narrow, level, first, image, inv, precond, right,
                 solution_field, residual, direction, zero, guess, spread, s10, s8, s6, ups, f12, f10):
    for r in range(2):
        for x in range(14):
            zero[r, x] = inv[x] * image[r, x]
    sweep_rows(guess, zero, lambda r, x: image[r, x], lambda x: inv[x], 12, 1)
    rows, rhs = coarse_rows(gathered)
    diag = [diag_in[x] for x in range(KX)]
    value = coarse_solve(rhs, diag, weights)
    sums = jnp.sum(total(rows), axis=0, keepdims=True)
    product = jnp.sum(total([a * b for a, b in zip(rhs, value)]), axis=0, keepdims=True)
    line = iota(sums.shape, 1)

    def pick(row, low, high):
        return jnp.sum(jnp.where((line >= low) & (line < high), row, 0.0), axis=1, keepdims=True)

    alphas, betas = [], []
    for r in range(2):
        rz = pick(sums, TOTAL_LANE + r, TOTAL_LANE + r + 1)
        pq = pick(sums, TOTAL_LANE + 2 + r, TOTAL_LANE + 3 + r)
        energy = pick(sums, TOTAL_LANE + 4 + r, TOTAL_LANE + 5 + r)
        energy = energy + 4.0 * pick(product, r * KZ, (r + 1) * KZ)
        alpha = rz / pq
        alphas.append(alpha)
        betas.append(alpha * alpha * energy / rz - 1.0)

    def out(r, x, row):
        p = precond[r, x]
        solution_field[r, x] = alphas[r] * p
        residual[r, x] = right[r, x] - alphas[r] * middle(image[r, x + 3])
        direction[r, x] = p - alphas[r] * middle(row) + betas[r] * p

    post(
        place, value, spread, narrow, lambda r, x: level[r, x - 2], lambda x: first[2, x],
        guess, lambda r, x: image[r, x], inv, s10, s8, s6, ups, f12, f10, out,
    )


def call(kernel, outs, scratch, place=None, cost=None):
    vmem = pl.BlockSpec(memory_space=pltpu.VMEM)

    def run(*args):
        specs = [vmem] * len(args)
        if place is not None:
            args = (place,) + args
            specs = [pl.BlockSpec(memory_space=pltpu.SMEM)] + specs
        return pl.pallas_call(
            kernel,
            out_shape=[jax.ShapeDtypeStruct(shape, F32) for shape in outs],
            in_specs=specs,
            out_specs=[vmem] * len(outs),
            scratch_shapes=[pltpu.VMEM(shape, F32) for shape in scratch],
            cost_estimate=cost,
            compiler_params=pltpu.CompilerParams(vmem_limit_bytes=16 * 1024 * 1024),
        )(*args)

    return run


def swap_y(low, high, packed=False):
    count = lax.axis_size("gy")
    even = lax.axis_index("gy") % 2 == 0
    near_pairs = [(i, i + 1) for i in range(0, count, 2)]
    far_pairs = [(i, i + 1) for i in range(1, count - 1, 2)]
    near_pairs = near_pairs + [(b, a) for a, b in near_pairs]
    far_pairs = far_pairs + [(b, a) for a, b in far_pairs]
    far, near = (low, high) if packed else (jnp.where(even, low, high), jnp.where(even, high, low))
    far = lax.ppermute(far, "gy", far_pairs)
    near = lax.ppermute(near, "gy", near_pairs)
    return jnp.where(even, far, near), jnp.where(even, near, far)


def swap_x(low, high):
    count = lax.axis_size("gx")
    forward = [(i, i + 1) for i in range(count - 1)]
    backward = [(b, a) for a, b in forward]
    return lax.ppermute(high, "gx", forward), lax.ppermute(low, "gx", backward)


def extended_x(block, width):
    low, high = swap_x(block[:, :width], block[:, block.shape[1] - width :])
    return jnp.concatenate([low, block, high], axis=1)


def extended(block):
    low, high = swap_y(block[:, :, :3], block[:, :, block.shape[2] - 3 :])
    block = jnp.concatenate([low, block, high], axis=2)
    return extended_x(jnp.pad(block, ((0, 0), (0, 0), (1, 1), (0, 0))), 3)


def extended_level(level, place):
    cost = pl.CostEstimate(flops=0, bytes_accessed=16 * 1024 * 1024, transcendentals=0)
    far, near = call(pack_kernel, [(3, 2, 8, LANES)] * 2, [], place, cost)(level)
    low, high = swap_y(far, near, True)
    shape = (3, 4, 4, LANES)
    return extended_x(jnp.concatenate([low.reshape(shape), level, high.reshape(shape)], axis=2), 4)


def halves_to_rows(block):
    return jnp.concatenate([block[..., :LANES], block[..., LANES:]], axis=2)


def rows_to_halves(block):
    rows = block.shape[2] // 2
    return jnp.concatenate([block[:, :, :rows], block[:, :, rows:]], axis=3)


def exchange_shares(precond, part, low, high):
    low, high = swap_y(low, high)
    wide = jnp.concatenate([rows_to_halves(low[:, :, :8]), precond, rows_to_halves(high[:, :, :8])], axis=2)
    part = part + jnp.pad(low[:, :, 8:14], ((0, 0), (0, 0), (0, 10), (0, 0)))
    part = part + jnp.pad(high[:, :, 8:14], ((0, 0), (0, 0), (10, 0), (0, 0)))
    low = jnp.concatenate([halves_to_rows(wide[:, :4]), part[:, :4]], axis=2)
    high = jnp.concatenate([halves_to_rows(wide[:, 4:]), part[:, 4:]], axis=2)
    low, high = swap_x(low, high)
    wide = jnp.concatenate([rows_to_halves(low[:, :, :48]), wide, rows_to_halves(high[:, :, :48])], axis=1)
    part = jnp.concatenate([part[:, :4] + low[:, :, 48:], part[:, 4:] + high[:, :, 48:]], axis=1)
    return wide, part


def gather_all(line, beside=None):
    size_x = lax.axis_size("gx")
    size_y = lax.axis_size("gy")
    rows = lax.all_to_all(line, "gy", 0, 0, tiled=True).reshape(KY, size_y // KY, LANES)
    even, odd = rows[:, 0], rows[:, 1]
    other = jnp.pad(even[1:], ((0, 1), (0, 0))) + jnp.pad(odd[:-1], ((1, 0), (0, 0)))
    other = jnp.pad(other[:, OTHER_LANE : 2 * OTHER_LANE], ((0, 0), (0, LANES - OTHER_LANE)))
    rows = even + odd + other
    if beside is not None:
        rows, beside = lax.optimization_barrier((rows, beside))
    spread = jnp.broadcast_to(rows[None], (size_x, KY, LANES))
    return lax.all_to_all(spread, "gx", 0, 0, tiled=True), beside


def local(right_side, diagonal):
    block_x = right_side.shape[1] * lax.axis_size("gx") // 2 // KX
    block_y = right_side.shape[2] * lax.axis_size("gy") // 2 // KY
    block_z = right_side.shape[3] // 2 // KZ
    size_y = lax.axis_size("gy")
    weights = (float(block_y * block_z), float(block_x * block_z), float(block_x * block_y))
    place = jnp.stack([lax.axis_index("gx"), lax.axis_index("gy")]).astype(jnp.int32)

    both = extended(jnp.concatenate([right_side, diagonal[None]], axis=0))
    inv, guess, level, line = call(
        fine_kernel,
        [(14, 24, 256), (2, 12, 24, 256), (3, 4, 8, LANES), (size_y, 1, LANES)],
        [(2, 14, 24, 256), (448, LANES), (2, 12, 16, LANES), (2, 10, 16, LANES)],
        place,
    )(both)
    gathered, _ = gather_all(line)
    first = extended_level(level, place)
    post_scratch = [
        (2, KX + 2, 8 + KY + 8, LANES), (2, 10, 16, LANES), (2, 8, 16, LANES), (2, 6, 16, LANES),
        (384, LANES), (2, 12, 24, 256), (2, 10, 24, 256),
    ]
    precond, diag, part, low, high = call(
        functools.partial(precond_kernel, weights),
        [(2, 8, 16, 256), (KX, KY, LANES), (2, 8, 16, LANES), (2, 8, 16, LANES), (2, 8, 16, LANES)],
        [
            (2, 12, 16, LANES), (2, 10, 16, LANES), (2, 16, 24, 256), (2, 14, 24, 256),
            (2, 14, 24, 256), (2, 16, 24, 256), (512, LANES),
        ] + post_scratch,
        place,
    )(gathered, first, guess, both, inv)
    wide, level_q = exchange_shares(precond, part, low, high)
    image, inner, line_q = call(
        image_kernel,
        [(2, 14, 24, 256), (2, 6, 16, LANES), (size_y, 1, LANES)],
        [(2, 14, 24, 256), (2, 12, 24, 256), (2, 8, 16, LANES)],
    )(wide, level_q, first, both, inv)
    low, high = swap_x(inner[:, 2:4], inner[:, 2:4])
    gathered_q, narrow_q = gather_all(line_q, jnp.concatenate([low, inner, high], axis=1))
    return tuple(
        call(
            functools.partial(final_kernel, weights),
            [(2, 8, 16, 256)] * 3,
            [(2, 14, 24, 256), (2, 12, 24, 256)] + post_scratch,
            place,
        )(gathered_q, diag, narrow_q, level_q, first, image, inv, precond, right_side)
    )


def solution(mesh):
    placed = (P(None, "gx", "gy", None), P("gx", "gy", None))
    return jax.shard_map(
        local,
        mesh=mesh,
        in_specs=placed,
        out_specs=(P(None, "gx", "gy", None),) * 3,
        check_vma=False,
    )
```

```python
import functools

import jax
import jax.numpy as jnp
from jax import lax
from jax.experimental import pallas as pl
from jax.experimental.pallas import tpu as pltpu
from jax.sharding import PartitionSpec as P

KX = 16
KY = 16
KZ = 8
CSWEEPS = 4
OMEGA = 0.8
HIGH = lax.Precision.HIGHEST
F32 = jnp.float32
LANES = 128
SIDE_LANE = 16
OTHER_LANE = 48
DIAG_GROUP = 12
DIAG_LANE = 96
TOTAL_LANE = 104


def dot(a, b):
    return jnp.dot(a, b, precision=HIGH, preferred_element_type=F32)


def table_dot(a, table):
    parts = []
    for _ in range(3):
        part = a.astype(jnp.bfloat16).astype(F32)
        a = a - part
        parts.append(part)
    rows = a.shape[0]
    stacked = jnp.concatenate(parts, axis=0).astype(jnp.bfloat16)
    product = jnp.dot(stacked, table.astype(jnp.bfloat16), preferred_element_type=F32)
    return product[:rows] + product[rows : 2 * rows] + product[2 * rows :]


def iota(shape, dim):
    return lax.broadcasted_iota(jnp.int32, shape, dim)


def z_sides(row):
    depth = row.shape[-1]
    lane = iota(row.shape, 1)
    before = jnp.where(lane == 0, 0.0, pltpu.roll(row, 1, 1))
    after = jnp.where(lane == depth - 1, 0.0, pltpu.roll(row, depth - 1, 1))
    return before + after


def sides(ref, r, x):
    row = ref[r, x]
    rows = row.shape[0]
    along_y = pltpu.roll(row, 1, 0) + pltpu.roll(row, rows - 1, 0)
    return ref[r, x - 1] + ref[r, x + 1] + along_y + z_sides(row)


def swept(field, rhs, inverse, r, x):
    return (1.0 - OMEGA) * field[r, x] + inverse * (rhs + sides(field, r, x))


def sweep_rows(out, field, rhs, inverse, count, shift):
    for r in range(2):
        for x in range(count):
            out[r, x] = swept(field, rhs(r, x + shift), inverse(x + shift), r, x + 1)


def inverse_of(kappa):
    return jnp.where(kappa > 0.0, OMEGA / (6.0 + kappa), 0.0)


def pair_table(wide, narrow):
    return (iota((wide, narrow), 0) // 2 == iota((wide, narrow), 1)).astype(F32)


def copy_table(narrow, wide):
    return (iota((narrow, wide), 0) == iota((narrow, wide), 1) // 2).astype(F32)


def fine_pre(wide, kappa, inv, zero, guess, sums):
    for r in range(2):
        for x in range(14):
            zero[r, x] = inv(x) * wide[r, x]
    sweep_rows(guess, zero, lambda r, x: wide[r, x], inv, 12, 1)
    left = []
    for r in range(2):
        rows = []
        for x in range(8):
            image = (6.0 + kappa(x + 3)) * guess[r, x + 2] - sides(guess, r, x + 2)
            rows.append(wide[r, x + 3] - image)
        left.append(rows)
    pairs = [left[r][2 * x] + left[r][2 * x + 1] for r in range(2) for x in range(4)]
    return level_rows(pairs + [kappa(2 * x + 1) + kappa(2 * x + 2) for x in range(6)], sums)


def level_rows(pairs, sums):
    table = pair_table(256, LANES)
    sums[...] = jnp.zeros(sums.shape, F32)
    product = table_dot(jnp.concatenate(pairs, axis=0), table)
    for i in range(len(pairs)):
        sums[pl.ds(32 * i + 4, 24), :] = product[24 * i : 24 * (i + 1)]

    def level_row(i):
        pair = sums[pl.ds(32 * i, 16, stride=2), :] + sums[pl.ds(32 * i + 1, 16, stride=2), :]
        return pair * 0.25

    return level_row


def own_rows(shape, low, high):
    row = iota(shape, 0)
    return (row >= low) & (row < high)


def own_eight(row):
    return pltpu.roll(row, 12, 0)[0:8]


def gathered_line(vectors):
    row = iota((16, LANES), 0)
    stacked = jnp.zeros((16, LANES), F32)
    for group, vector in vectors.items():
        stacked = jnp.where(row == group, vector, stacked)
    table = iota((LANES, LANES), 0) // (LANES // KZ) == iota((LANES, LANES), 1) % KZ
    spread = table_dot(stacked, table.astype(F32))
    return jnp.sum(jnp.where(iota((16, LANES), 1) // KZ == row, spread, 0.0), axis=0, keepdims=True)


def level_pre(rhs, extra, guess, zero, first, last):
    linv = [inverse_of(extra(x)) for x in range(12)]
    for r in range(2):
        for x in range(12):
            zero[r, x] = linv[x] * rhs(r, x)
    sweep_rows(guess, zero, rhs, lambda x: linv[x], 10, 1)
    left = []
    for r in range(2):
        rows = []
        for x in range(first, last):
            image = (6.0 + extra(x)) * guess[r, x - 1] - sides(guess, r, x - 1)
            rows.append(rhs(r, x) - image)
        left.append(rows)
    return left


def total(rows):
    out = rows[0]
    for row in rows[1:]:
        out = out + row
    return out


def fine_kernel(place, both, inv, guess, level, line, zero, sums, zero_level, guess_level):
    for x in range(14):
        inv[x] = inverse_of(both[2, x])
    level_row = fine_pre(both, lambda x: both[2, x], lambda x: inv[x], zero, guess, sums)
    own = own_rows((16, LANES), 4, 12)
    nothing = jnp.zeros((16, LANES), F32)
    rhs = [[jnp.where(own, level_row(4 * r + x), 0.0) for x in range(4)] for r in range(2)]
    extra = [level_row(8 + x) for x in range(6)]
    for r in range(2):
        for x in range(4):
            level[r, x] = own_eight(rhs[r][x])
    for x in range(4):
        level[2, x] = own_eight(extra[x + 1])
    left = level_pre(
        lambda r, x: rhs[r][x - 4] if 4 <= x < 8 else nothing,
        lambda x: extra[x - 3] if 3 <= x < 9 else nothing,
        guess_level, zero_level, 2, 10,
    )
    row = iota((16, LANES), 0)
    odd = place[1] % 2
    other = (row < 4 * (1 - odd)) | (row >= 16 - 4 * odd)
    vectors = {}
    for r in range(2):
        for side, rows in enumerate((left[r][2:6], left[r][0:2], left[r][6:8])):
            column = total(rows)
            for far in range(2):
                part = jnp.where(other, column, 0.0) if far else jnp.where(other, 0.0, column)
                vectors[(3 * far + side) * 2 + r] = jnp.sum(part, axis=0, keepdims=True)
    diag_sum = jnp.where(own, total(extra[1:5]), 0.0)
    vectors[DIAG_GROUP] = jnp.sum(diag_sum, axis=0, keepdims=True)
    line[...] = jnp.broadcast_to(gathered_line(vectors), line.shape)


def pack_kernel(place, level, far, near):
    even = place[1] % 2 == 0
    top = iota((8, LANES), 0) < 4
    for c in range(3):
        for i in range(2):
            one, two = level[c, 2 * i], level[c, 2 * i + 1]
            low = jnp.where(top, one, pltpu.roll(two, 4, 0))
            high = jnp.where(top, pltpu.roll(one, 4, 0), two)
            far[c, i] = jnp.where(even, low, high)
            near[c, i] = jnp.where(even, high, low)


def fold(field):
    folded = field[0:8] + field[8:16] + field[16:24]
    return folded[:, :LANES] + folded[:, LANES:]


def image_kernel(wide, level, first, both, inv, image, narrow, line, zero, guess, zero_level):
    for r in range(2):
        for x in range(14):
            image[r, x] = (6.0 + both[2, x]) * wide[r, x + 1] - sides(wide, r, x + 1)
            zero[r, x] = inv[x] * image[r, x]
    sweep_rows(guess, zero, lambda r, x: image[r, x], lambda x: inv[x], 12, 1)
    own = own_rows((24, 256), 4, 20)
    own_level = own_rows((16, LANES), 4, 12)
    extra = lambda x: first[2, x + 2]
    linv = [inverse_of(extra(x)) for x in range(8)]
    for r in range(2):
        for x in range(8):
            zero_level[r, x] = linv[x] * level[r, x]
    level_rhs = lambda r, x: level[r, x]
    sweep_rows(narrow, zero_level, level_rhs, lambda x: linv[x], 6, 1)
    vectors = {}
    totals = []
    for r in range(2):
        rz = total([both[r, x + 3] * wide[r, x + 4] for x in range(8)])
        pq = total([image[r, x + 3] * wide[r, x + 4] for x in range(8)])
        energy = None
        for x in range(8):
            back = (6.0 + both[2, x + 3]) * guess[r, x + 2] - sides(guess, r, x + 2)
            term = guess[r, x + 2] * (2.0 * image[r, x + 3] - back)
            energy = term if energy is None else energy + term
        energy = fold(jnp.where(own, energy, 0.0))
        column = None
        for x in range(4):
            back = (6.0 + extra(x + 2)) * narrow[r, x + 1] - sides(narrow, r, x + 1)
            left = level[r, x + 2] - back
            column = left if column is None else column + left
            term = narrow[r, x + 1] * (level[r, x + 2] + left)
            term = 4.0 * jnp.where(own_level, term, 0.0)
            energy = energy + term[0:8] + term[8:16]
        vectors[r] = jnp.sum(jnp.where(own_level, column, 0.0), axis=0, keepdims=True)
        totals.append((TOTAL_LANE + r, fold(jnp.where(own, rz, 0.0))))
        totals.append((TOTAL_LANE + 2 + r, fold(jnp.where(own, pq, 0.0))))
        totals.append((TOTAL_LANE + 4 + r, energy))
    out = gathered_line(vectors)
    lane = iota((1, LANES), 1)
    for place, part in totals:
        value = jnp.sum(jnp.sum(part, axis=0, keepdims=True), axis=1, keepdims=True)
        out = jnp.where(lane == place, value, out)
    line[...] = jnp.broadcast_to(out, line.shape)


def coarse_rows(gathered):
    rows = [gathered[x] for x in range(KX)]
    lane = iota(rows[0].shape, 1)
    out = []
    for x in range(KX):
        row = rows[x]
        if x < KX - 1:
            row = row + pltpu.roll(rows[x + 1], LANES - SIDE_LANE, 1)
        if x > 0:
            row = row + pltpu.roll(rows[x - 1], LANES - 2 * SIDE_LANE, 1)
        out.append(jnp.where(lane < 2 * KZ, row, 0.0))
    return rows, out


def coarse_solve(rhs, diag, weights):
    weight_x, weight_y, weight_z = weights
    shape = rhs[0].shape
    row = iota(shape, 0)
    lane = iota(shape, 1) % KZ
    inverse = [OMEGA / d for d in diag]
    value = [i * b for i, b in zip(inverse, rhs)]
    nothing = jnp.zeros(shape, F32)
    for _ in range(CSWEEPS - 1):
        new = []
        for x in range(KX):
            v = value[x]
            below = value[x - 1] if x > 0 else nothing
            above = value[x + 1] if x < KX - 1 else nothing
            along_y = jnp.where(row == 0, 0.0, pltpu.roll(v, 1, 0))
            along_y = along_y + jnp.where(row == KY - 1, 0.0, pltpu.roll(v, shape[0] - 1, 0))
            along_z = jnp.where(lane == 0, 0.0, pltpu.roll(v, 1, 1))
            along_z = along_z + jnp.where(lane == KZ - 1, 0.0, pltpu.roll(v, LANES - 1, 1))
            image = diag[x] * v - (
                weight_x * (below + above) + weight_y * along_y + weight_z * along_z
            )
            new.append(v + inverse[x] * (rhs[x] - image))
        value = new
    return value


def coarse_diag_of(rows, weights):
    lane = iota(rows[0].shape, 1)
    base = 2.0 * (weights[0] + weights[1] + weights[2])
    out = []
    for row in rows:
        first = pltpu.roll(row, LANES - DIAG_LANE, 1)
        second = pltpu.roll(row, LANES - DIAG_LANE + KZ, 1)
        both = jnp.where(lane < KZ, first, jnp.where(lane < 2 * KZ, second, 0.0))
        out.append(base + both)
    return out


def up_blocks(place, value, spread, narrow, target):
    gx, gy = place[0], place[1]
    spread[...] = jnp.zeros(spread.shape, F32)
    stacked = jnp.concatenate(value, axis=0)
    lane_table = iota((LANES, LANES), 0)
    col = iota((LANES, LANES), 1) // (LANES // KZ)
    for r in range(2):
        wide = table_dot(stacked, (lane_table == r * KZ + col).astype(F32))
        for x in range(KX):
            spread[r, x + 1, pl.ds(8, KY), :] = wide[KY * x : KY * (x + 1)]
    odd = gy % 2
    low = gy // 2 + odd + 7
    row = iota((16, LANES), 0)
    limit = 4 + 8 * odd
    for r in range(2):
        for x in range(3):
            first = spread[r, gx + x, pl.ds(low, 1), :]
            second = spread[r, gx + x, pl.ds(low + 1, 1), :]
            tile = jnp.where(row < limit, first, second)
            for i in ((0, 1, 2), (3, 4, 5, 6), (7, 8, 9))[x]:
                target[r, i] = narrow[r, i] + tile


def post(place, value, spread, narrow, level_rhs, extra, guess, rhs, inv, s10, s8, s6, ups, f12, f10, out):
    up_blocks(place, value, spread, narrow, s10)
    linv = {x: inverse_of(extra(x)) for x in range(2, 10)}
    sweep_rows(s8, s10, level_rhs, lambda x: linv[x], 8, 2)
    sweep_rows(s6, s8, level_rhs, lambda x: linv[x], 6, 3)
    table_z = copy_table(LANES, 256)
    for r in range(2):
        for x in range(6):
            base = 32 * (6 * r + x)
            ups[pl.ds(base, 16, stride=2), :] = s6[r, x]
            ups[pl.ds(base + 1, 16, stride=2), :] = s6[r, x]
    rows = [ups[pl.ds(32 * i + 4, 24), :] for i in range(12)]
    product = table_dot(jnp.concatenate(rows, axis=0), table_z)
    for r in range(2):
        for x in range(12):
            i = 6 * r + x // 2
            f12[r, x] = guess[r, x] + product[24 * i : 24 * (i + 1)]
    sweep_rows(f10, f12, rhs, lambda x: inv[x], 10, 2)
    for r in range(2):
        for x in range(8):
            out(r, x, swept(f10, rhs(r, x + 3), inv[x + 3], r, x + 1))


def middle(row):
    return pltpu.roll(row, row.shape[0] - 4, 0)[0:16]


def share(alone, kappa, inv, image, zero, guess, sums):
    nothing = jnp.zeros((24, 256), F32)
    for r in range(2):
        for x in range(14):
            if 2 <= x < 12:
                image[r, x] = (6.0 + kappa(x)) * alone[r, x + 1] - sides(alone, r, x + 1)
                zero[r, x] = inv(x) * image[r, x]
            else:
                image[r, x] = nothing
                zero[r, x] = nothing
        for x in (0, 1, 14, 15):
            guess[r, x] = nothing
        for x in range(2, 14):
            guess[r, x] = swept(zero, image[r, x - 1], inv(x - 1), r, x - 1)
    pairs = []
    for r in range(2):
        rows = []
        for x in range(14):
            back = (6.0 + kappa(x)) * guess[r, x + 1] - sides(guess, r, x + 1)
            rows.append(image[r, x] - back)
        pairs = pairs + [rows[0]]
        pairs = pairs + [rows[2 * x + 1] + rows[2 * x + 2] for x in range(6)] + [rows[13]]
    return level_rows(pairs, sums)


def precond_kernel(weights, place, gathered, level, guess, both, inv,
                   precond, diag_out, part, low, high,
                   zero_level, narrow, alone, image, zero, guess_alone, sums,
                   spread, s10, s8, s6, ups, f12, f10):
    level_pre(lambda r, x: level[r, x], lambda x: level[2, x], narrow, zero_level, 4, 4)
    rows, rhs = coarse_rows(gathered)
    diag = coarse_diag_of(rows, weights)
    for x in range(KX):
        diag_out[x] = diag[x]
    value = coarse_solve(rhs, diag, weights)
    own = own_rows((24, 256), 4, 20)
    top = iota((8, LANES), 0) < 4
    for r in range(2):
        for x in (0, 1, 2, 3, 12, 13, 14, 15):
            alone[r, x] = jnp.zeros((24, 256), F32)

    def out(r, x, row):
        own_part = middle(row)
        precond[r, x] = own_part
        alone[r, x + 4] = jnp.where(own, row, 0.0)
        left, right = own_part[:, :LANES], own_part[:, LANES:]
        low[r, x, 0:8, :] = jnp.where(top, left[0:8], pltpu.roll(right[0:8], 4, 0))
        high[r, x, 0:8, :] = jnp.where(top, pltpu.roll(left[8:16], 4, 0), right[8:16])

    post(
        place, value, spread, narrow, lambda r, x: level[r, x], lambda x: level[2, x],
        guess, lambda r, x: both[r, x], inv, s10, s8, s6, ups, f12, f10, out,
    )
    level_row = share(
        alone, lambda x: both[2, x], lambda x: inv[x], image, zero, guess_alone, sums
    )
    for r in range(2):
        for x in range(8):
            row = level_row(8 * r + x)
            part[r, x] = row
            low[r, x, 8:16, :] = pltpu.roll(row, 14, 0)[0:8]
            high[r, x, 8:16, :] = row[8:16]


def final_kernel(weights, place, gathered, diag_in, narrow, level, first, image, inv, precond, right,
                 solution_field, residual, direction, zero, guess, spread, s10, s8, s6, ups, f12, f10):
    for r in range(2):
        for x in range(14):
            zero[r, x] = inv[x] * image[r, x]
    sweep_rows(guess, zero, lambda r, x: image[r, x], lambda x: inv[x], 12, 1)
    rows, rhs = coarse_rows(gathered)
    diag = [diag_in[x] for x in range(KX)]
    value = coarse_solve(rhs, diag, weights)
    sums = jnp.sum(total(rows), axis=0, keepdims=True)
    product = jnp.sum(total([a * b for a, b in zip(rhs, value)]), axis=0, keepdims=True)
    line = iota(sums.shape, 1)

    def pick(row, low, high):
        return jnp.sum(jnp.where((line >= low) & (line < high), row, 0.0), axis=1, keepdims=True)

    alphas, betas = [], []
    for r in range(2):
        rz = pick(sums, TOTAL_LANE + r, TOTAL_LANE + r + 1)
        pq = pick(sums, TOTAL_LANE + 2 + r, TOTAL_LANE + 3 + r)
        energy = pick(sums, TOTAL_LANE + 4 + r, TOTAL_LANE + 5 + r)
        energy = energy + 4.0 * pick(product, r * KZ, (r + 1) * KZ)
        alpha = rz / pq
        alphas.append(alpha)
        betas.append(alpha * alpha * energy / rz - 1.0)

    def out(r, x, row):
        p = precond[r, x]
        solution_field[r, x] = alphas[r] * p
        residual[r, x] = right[r, x] - alphas[r] * middle(image[r, x + 3])
        direction[r, x] = p - alphas[r] * middle(row) + betas[r] * p

    post(
        place, value, spread, narrow, lambda r, x: level[r, x - 2], lambda x: first[2, x],
        guess, lambda r, x: image[r, x], inv, s10, s8, s6, ups, f12, f10, out,
    )


def call(kernel, outs, scratch, place=None):
    vmem = pl.BlockSpec(memory_space=pltpu.VMEM)

    def run(*args):
        specs = [vmem] * len(args)
        if place is not None:
            args = (place,) + args
            specs = [pl.BlockSpec(memory_space=pltpu.SMEM)] + specs
        return pl.pallas_call(
            kernel,
            out_shape=[jax.ShapeDtypeStruct(shape, F32) for shape in outs],
            in_specs=specs,
            out_specs=[vmem] * len(outs),
            scratch_shapes=[pltpu.VMEM(shape, F32) for shape in scratch],
            compiler_params=pltpu.CompilerParams(vmem_limit_bytes=16 * 1024 * 1024),
        )(*args)

    return run


def swap_y(low, high, packed=False):
    count = lax.axis_size("gy")
    even = lax.axis_index("gy") % 2 == 0
    near_pairs = [(i, i + 1) for i in range(0, count, 2)]
    far_pairs = [(i, i + 1) for i in range(1, count - 1, 2)]
    near_pairs = near_pairs + [(b, a) for a, b in near_pairs]
    far_pairs = far_pairs + [(b, a) for a, b in far_pairs]
    far, near = (low, high) if packed else (jnp.where(even, low, high), jnp.where(even, high, low))
    far = lax.ppermute(far, "gy", far_pairs)
    near = lax.ppermute(near, "gy", near_pairs)
    return jnp.where(even, far, near), jnp.where(even, near, far)


def swap_x(low, high):
    count = lax.axis_size("gx")
    forward = [(i, i + 1) for i in range(count - 1)]
    backward = [(b, a) for a, b in forward]
    return lax.ppermute(high, "gx", forward), lax.ppermute(low, "gx", backward)


def extended_x(block, width):
    low, high = swap_x(block[:, :width], block[:, block.shape[1] - width :])
    return jnp.concatenate([low, block, high], axis=1)


def extended(block):
    low, high = swap_y(block[:, :, :3], block[:, :, block.shape[2] - 3 :])
    block = jnp.concatenate([low, block, high], axis=2)
    return extended_x(jnp.pad(block, ((0, 0), (0, 0), (1, 1), (0, 0))), 3)


def extended_level(level, place):
    far, near = call(pack_kernel, [(3, 2, 8, LANES)] * 2, [], place)(level)
    low, high = swap_y(far, near, True)
    shape = (3, 4, 4, LANES)
    return extended_x(jnp.concatenate([low.reshape(shape), level, high.reshape(shape)], axis=2), 4)


def halves_to_rows(block):
    return jnp.concatenate([block[..., :LANES], block[..., LANES:]], axis=2)


def rows_to_halves(block):
    rows = block.shape[2] // 2
    return jnp.concatenate([block[:, :, :rows], block[:, :, rows:]], axis=3)


def exchange_shares(precond, part, low, high):
    low, high = swap_y(low, high)
    wide = jnp.concatenate([rows_to_halves(low[:, :, :8]), precond, rows_to_halves(high[:, :, :8])], axis=2)
    part = part + jnp.pad(low[:, :, 8:14], ((0, 0), (0, 0), (0, 10), (0, 0)))
    part = part + jnp.pad(high[:, :, 8:14], ((0, 0), (0, 0), (10, 0), (0, 0)))
    low = jnp.concatenate([halves_to_rows(wide[:, :4]), part[:, :4]], axis=2)
    high = jnp.concatenate([halves_to_rows(wide[:, 4:]), part[:, 4:]], axis=2)
    low, high = swap_x(low, high)
    wide = jnp.concatenate([rows_to_halves(low[:, :, :48]), wide, rows_to_halves(high[:, :, :48])], axis=1)
    part = jnp.concatenate([part[:, :4] + low[:, :, 48:], part[:, 4:] + high[:, :, 48:]], axis=1)
    return wide, part


def gather_all(line, beside=None):
    size_x = lax.axis_size("gx")
    size_y = lax.axis_size("gy")
    rows = lax.all_to_all(line, "gy", 0, 0, tiled=True).reshape(KY, size_y // KY, LANES)
    even, odd = rows[:, 0], rows[:, 1]
    other = jnp.pad(even[1:], ((0, 1), (0, 0))) + jnp.pad(odd[:-1], ((1, 0), (0, 0)))
    other = jnp.pad(other[:, OTHER_LANE : 2 * OTHER_LANE], ((0, 0), (0, LANES - OTHER_LANE)))
    rows = even + odd + other
    if beside is not None:
        rows, beside = lax.optimization_barrier((rows, beside))
    spread = jnp.broadcast_to(rows[None], (size_x, KY, LANES))
    return lax.all_to_all(spread, "gx", 0, 0, tiled=True), beside


def local(right_side, diagonal):
    block_x = right_side.shape[1] * lax.axis_size("gx") // 2 // KX
    block_y = right_side.shape[2] * lax.axis_size("gy") // 2 // KY
    block_z = right_side.shape[3] // 2 // KZ
    size_y = lax.axis_size("gy")
    weights = (float(block_y * block_z), float(block_x * block_z), float(block_x * block_y))
    place = jnp.stack([lax.axis_index("gx"), lax.axis_index("gy")]).astype(jnp.int32)

    both = extended(jnp.concatenate([right_side, diagonal[None]], axis=0))
    inv, guess, level, line = call(
        fine_kernel,
        [(14, 24, 256), (2, 12, 24, 256), (3, 4, 8, LANES), (size_y, LANES)],
        [(2, 14, 24, 256), (448, LANES), (2, 12, 16, LANES), (2, 10, 16, LANES)],
        place,
    )(both)
    gathered, _ = gather_all(line)
    first = extended_level(level, place)
    post_scratch = [
        (2, KX + 2, 8 + KY + 8, LANES), (2, 10, 16, LANES), (2, 8, 16, LANES), (2, 6, 16, LANES),
        (384, LANES), (2, 12, 24, 256), (2, 10, 24, 256),
    ]
    precond, diag, part, low, high = call(
        functools.partial(precond_kernel, weights),
        [(2, 8, 16, 256), (KX, KY, LANES), (2, 8, 16, LANES), (2, 8, 16, LANES), (2, 8, 16, LANES)],
        [
            (2, 12, 16, LANES), (2, 10, 16, LANES), (2, 16, 24, 256), (2, 14, 24, 256),
            (2, 14, 24, 256), (2, 16, 24, 256), (512, LANES),
        ] + post_scratch,
        place,
    )(gathered, first, guess, both, inv)
    wide, level_q = exchange_shares(precond, part, low, high)
    image, inner, line_q = call(
        image_kernel,
        [(2, 14, 24, 256), (2, 6, 16, LANES), (size_y, LANES)],
        [(2, 14, 24, 256), (2, 12, 24, 256), (2, 8, 16, LANES)],
    )(wide, level_q, first, both, inv)
    low, high = swap_x(inner[:, 2:4], inner[:, 2:4])
    gathered_q, narrow_q = gather_all(line_q, jnp.concatenate([low, inner, high], axis=1))
    return tuple(
        call(
            functools.partial(final_kernel, weights),
            [(2, 8, 16, 256)] * 3,
            [(2, 14, 24, 256), (2, 12, 24, 256)] + post_scratch,
            place,
        )(gathered_q, diag, narrow_q, level_q, first, image, inv, precond, right_side)
    )


def solution(mesh):
    placed = (P(None, "gx", "gy", None), P("gx", "gy", None))
    return jax.shard_map(
        local,
        mesh=mesh,
        in_specs=placed,
        out_specs=(P(None, "gx", "gy", None),) * 3,
        check_vma=False,
    )
```

```python
import functools

import jax
import jax.numpy as jnp
from jax import lax
from jax.experimental import pallas as pl
from jax.experimental.pallas import tpu as pltpu
from jax.sharding import PartitionSpec as P

KX = 16
KY = 16
KZ = 8
CSWEEPS = 4
OMEGA = 0.8
HIGH = lax.Precision.HIGHEST
F32 = jnp.float32
LANES = 128
SIDE_LANE = 16
OTHER_LANE = 48
DIAG_GROUP = 12
DIAG_LANE = 96
TOTAL_LANE = 104


def dot(a, b):
    return jnp.dot(a, b, precision=HIGH, preferred_element_type=F32)


def table_dot(a, table):
    parts = []
    for _ in range(3):
        part = a.astype(jnp.bfloat16).astype(F32)
        a = a - part
        parts.append(part)
    rows = a.shape[0]
    stacked = jnp.concatenate(parts, axis=0).astype(jnp.bfloat16)
    product = jnp.dot(stacked, table.astype(jnp.bfloat16), preferred_element_type=F32)
    return product[:rows] + product[rows : 2 * rows] + product[2 * rows :]


def iota(shape, dim):
    return lax.broadcasted_iota(jnp.int32, shape, dim)


def z_sides(row):
    depth = row.shape[-1]
    lane = iota(row.shape, 1)
    before = jnp.where(lane == 0, 0.0, pltpu.roll(row, 1, 1))
    after = jnp.where(lane == depth - 1, 0.0, pltpu.roll(row, depth - 1, 1))
    return before + after


def sides(ref, r, x):
    row = ref[r, x]
    rows = row.shape[0]
    along_y = pltpu.roll(row, 1, 0) + pltpu.roll(row, rows - 1, 0)
    return ref[r, x - 1] + ref[r, x + 1] + along_y + z_sides(row)


def swept(field, rhs, inverse, r, x):
    return (1.0 - OMEGA) * field[r, x] + inverse * (rhs + sides(field, r, x))


def sweep_rows(out, field, rhs, inverse, count, shift):
    for r in range(2):
        for x in range(count):
            out[r, x] = swept(field, rhs(r, x + shift), inverse(x + shift), r, x + 1)


def inverse_of(kappa):
    return jnp.where(kappa > 0.0, OMEGA / (6.0 + kappa), 0.0)


def pair_table(wide, narrow):
    return (iota((wide, narrow), 0) // 2 == iota((wide, narrow), 1)).astype(F32)


def copy_table(narrow, wide):
    return (iota((narrow, wide), 0) == iota((narrow, wide), 1) // 2).astype(F32)


def fine_pre(wide, kappa, inv, zero, guess, sums):
    for r in range(2):
        for x in range(14):
            zero[r, x] = inv(x) * wide[r, x]
    sweep_rows(guess, zero, lambda r, x: wide[r, x], inv, 12, 1)
    left = []
    for r in range(2):
        rows = []
        for x in range(8):
            image = (6.0 + kappa(x + 3)) * guess[r, x + 2] - sides(guess, r, x + 2)
            rows.append(wide[r, x + 3] - image)
        left.append(rows)
    pairs = [left[r][2 * x] + left[r][2 * x + 1] for r in range(2) for x in range(4)]
    return level_rows(pairs + [kappa(2 * x + 1) + kappa(2 * x + 2) for x in range(6)], sums)


def level_rows(pairs, sums):
    table = pair_table(256, LANES)
    sums[...] = jnp.zeros(sums.shape, F32)
    product = table_dot(jnp.concatenate(pairs, axis=0), table)
    for i in range(len(pairs)):
        sums[pl.ds(32 * i + 4, 24), :] = product[24 * i : 24 * (i + 1)]

    def level_row(i):
        pair = sums[pl.ds(32 * i, 16, stride=2), :] + sums[pl.ds(32 * i + 1, 16, stride=2), :]
        return pair * 0.25

    return level_row


def own_rows(shape, low, high):
    row = iota(shape, 0)
    return (row >= low) & (row < high)


def own_eight(row):
    return pltpu.roll(row, 12, 0)[0:8]


def gathered_line(vectors):
    row = iota((16, LANES), 0)
    stacked = jnp.zeros((16, LANES), F32)
    for group, vector in vectors.items():
        stacked = jnp.where(row == group, vector, stacked)
    table = iota((LANES, LANES), 0) // (LANES // KZ) == iota((LANES, LANES), 1) % KZ
    spread = table_dot(stacked, table.astype(F32))
    return jnp.sum(jnp.where(iota((16, LANES), 1) // KZ == row, spread, 0.0), axis=0, keepdims=True)


def level_pre(rhs, extra, guess, zero, first, last):
    linv = [inverse_of(extra(x)) for x in range(12)]
    for r in range(2):
        for x in range(12):
            zero[r, x] = linv[x] * rhs(r, x)
    sweep_rows(guess, zero, rhs, lambda x: linv[x], 10, 1)
    left = []
    for r in range(2):
        rows = []
        for x in range(first, last):
            image = (6.0 + extra(x)) * guess[r, x - 1] - sides(guess, r, x - 1)
            rows.append(rhs(r, x) - image)
        left.append(rows)
    return left


def total(rows):
    out = rows[0]
    for row in rows[1:]:
        out = out + row
    return out


def fine_kernel(place, both, inv, guess, level, line, zero, sums, zero_level, guess_level):
    for x in range(14):
        inv[x] = inverse_of(both[2, x])
    level_row = fine_pre(both, lambda x: both[2, x], lambda x: inv[x], zero, guess, sums)
    own = own_rows((16, LANES), 4, 12)
    nothing = jnp.zeros((16, LANES), F32)
    rhs = [[jnp.where(own, level_row(4 * r + x), 0.0) for x in range(4)] for r in range(2)]
    extra = [level_row(8 + x) for x in range(6)]
    for r in range(2):
        for x in range(4):
            level[r, x] = own_eight(rhs[r][x])
    for x in range(4):
        level[2, x] = own_eight(extra[x + 1])
    left = level_pre(
        lambda r, x: rhs[r][x - 4] if 4 <= x < 8 else nothing,
        lambda x: extra[x - 3] if 3 <= x < 9 else nothing,
        guess_level, zero_level, 2, 10,
    )
    row = iota((16, LANES), 0)
    odd = place[1] % 2
    other = (row < 4 * (1 - odd)) | (row >= 16 - 4 * odd)
    vectors = {}
    for r in range(2):
        for side, rows in enumerate((left[r][2:6], left[r][0:2], left[r][6:8])):
            column = total(rows)
            for far in range(2):
                part = jnp.where(other, column, 0.0) if far else jnp.where(other, 0.0, column)
                vectors[(3 * far + side) * 2 + r] = jnp.sum(part, axis=0, keepdims=True)
    diag_sum = jnp.where(own, total(extra[1:5]), 0.0)
    vectors[DIAG_GROUP] = jnp.sum(diag_sum, axis=0, keepdims=True)
    line[...] = jnp.broadcast_to(gathered_line(vectors), line.shape)


def fold(field):
    folded = field[0:8] + field[8:16] + field[16:24]
    return folded[:, :LANES] + folded[:, LANES:]


def image_kernel(wide, level, first, both, inv, image, narrow, line, zero, guess, zero_level):
    for r in range(2):
        for x in range(14):
            image[r, x] = (6.0 + both[2, x]) * wide[r, x + 1] - sides(wide, r, x + 1)
            zero[r, x] = inv[x] * image[r, x]
    sweep_rows(guess, zero, lambda r, x: image[r, x], lambda x: inv[x], 12, 1)
    own = own_rows((24, 256), 4, 20)
    own_level = own_rows((16, LANES), 4, 12)
    extra = lambda x: first[2, x + 2]
    linv = [inverse_of(extra(x)) for x in range(8)]
    for r in range(2):
        for x in range(8):
            zero_level[r, x] = linv[x] * level[r, x]
    level_rhs = lambda r, x: level[r, x]
    sweep_rows(narrow, zero_level, level_rhs, lambda x: linv[x], 6, 1)
    vectors = {}
    totals = []
    for r in range(2):
        rz = total([both[r, x + 3] * wide[r, x + 4] for x in range(8)])
        pq = total([image[r, x + 3] * wide[r, x + 4] for x in range(8)])
        energy = None
        for x in range(8):
            back = (6.0 + both[2, x + 3]) * guess[r, x + 2] - sides(guess, r, x + 2)
            term = guess[r, x + 2] * (2.0 * image[r, x + 3] - back)
            energy = term if energy is None else energy + term
        energy = fold(jnp.where(own, energy, 0.0))
        column = None
        for x in range(4):
            back = (6.0 + extra(x + 2)) * narrow[r, x + 1] - sides(narrow, r, x + 1)
            left = level[r, x + 2] - back
            column = left if column is None else column + left
            term = narrow[r, x + 1] * (level[r, x + 2] + left)
            term = 4.0 * jnp.where(own_level, term, 0.0)
            energy = energy + term[0:8] + term[8:16]
        vectors[r] = jnp.sum(jnp.where(own_level, column, 0.0), axis=0, keepdims=True)
        totals.append((TOTAL_LANE + r, fold(jnp.where(own, rz, 0.0))))
        totals.append((TOTAL_LANE + 2 + r, fold(jnp.where(own, pq, 0.0))))
        totals.append((TOTAL_LANE + 4 + r, energy))
    out = gathered_line(vectors)
    lane = iota((1, LANES), 1)
    for place, part in totals:
        value = jnp.sum(jnp.sum(part, axis=0, keepdims=True), axis=1, keepdims=True)
        out = jnp.where(lane == place, value, out)
    line[...] = jnp.broadcast_to(out, line.shape)


def coarse_rows(gathered):
    rows = [gathered[x] for x in range(KX)]
    lane = iota(rows[0].shape, 1)
    out = []
    for x in range(KX):
        row = rows[x]
        if x < KX - 1:
            row = row + pltpu.roll(rows[x + 1], LANES - SIDE_LANE, 1)
        if x > 0:
            row = row + pltpu.roll(rows[x - 1], LANES - 2 * SIDE_LANE, 1)
        out.append(jnp.where(lane < 2 * KZ, row, 0.0))
    return rows, out


def coarse_solve(rhs, diag, weights):
    weight_x, weight_y, weight_z = weights
    shape = rhs[0].shape
    row = iota(shape, 0)
    lane = iota(shape, 1) % KZ
    inverse = [OMEGA / d for d in diag]
    value = [i * b for i, b in zip(inverse, rhs)]
    nothing = jnp.zeros(shape, F32)
    for _ in range(CSWEEPS - 1):
        new = []
        for x in range(KX):
            v = value[x]
            below = value[x - 1] if x > 0 else nothing
            above = value[x + 1] if x < KX - 1 else nothing
            along_y = jnp.where(row == 0, 0.0, pltpu.roll(v, 1, 0))
            along_y = along_y + jnp.where(row == KY - 1, 0.0, pltpu.roll(v, shape[0] - 1, 0))
            along_z = jnp.where(lane == 0, 0.0, pltpu.roll(v, 1, 1))
            along_z = along_z + jnp.where(lane == KZ - 1, 0.0, pltpu.roll(v, LANES - 1, 1))
            image = diag[x] * v - (
                weight_x * (below + above) + weight_y * along_y + weight_z * along_z
            )
            new.append(v + inverse[x] * (rhs[x] - image))
        value = new
    return value


def coarse_diag_of(rows, weights):
    lane = iota(rows[0].shape, 1)
    base = 2.0 * (weights[0] + weights[1] + weights[2])
    out = []
    for row in rows:
        first = pltpu.roll(row, LANES - DIAG_LANE, 1)
        second = pltpu.roll(row, LANES - DIAG_LANE + KZ, 1)
        both = jnp.where(lane < KZ, first, jnp.where(lane < 2 * KZ, second, 0.0))
        out.append(base + both)
    return out


def up_blocks(place, value, spread, narrow, target):
    gx, gy = place[0], place[1]
    spread[...] = jnp.zeros(spread.shape, F32)
    stacked = jnp.concatenate(value, axis=0)
    lane_table = iota((LANES, LANES), 0)
    col = iota((LANES, LANES), 1) // (LANES // KZ)
    for r in range(2):
        wide = table_dot(stacked, (lane_table == r * KZ + col).astype(F32))
        for x in range(KX):
            spread[r, x + 1, pl.ds(8, KY), :] = wide[KY * x : KY * (x + 1)]
    odd = gy % 2
    low = gy // 2 + odd + 7
    row = iota((16, LANES), 0)
    limit = 4 + 8 * odd
    for r in range(2):
        for x in range(3):
            first = spread[r, gx + x, pl.ds(low, 1), :]
            second = spread[r, gx + x, pl.ds(low + 1, 1), :]
            tile = jnp.where(row < limit, first, second)
            for i in ((0, 1, 2), (3, 4, 5, 6), (7, 8, 9))[x]:
                target[r, i] = narrow[r, i] + tile


def post(place, value, spread, narrow, level_rhs, extra, guess, rhs, inv, s10, s8, s6, ups, f12, f10, out):
    up_blocks(place, value, spread, narrow, s10)
    linv = {x: inverse_of(extra(x)) for x in range(2, 10)}
    sweep_rows(s8, s10, level_rhs, lambda x: linv[x], 8, 2)
    sweep_rows(s6, s8, level_rhs, lambda x: linv[x], 6, 3)
    table_z = copy_table(LANES, 256)
    for r in range(2):
        for x in range(6):
            base = 32 * (6 * r + x)
            ups[pl.ds(base, 16, stride=2), :] = s6[r, x]
            ups[pl.ds(base + 1, 16, stride=2), :] = s6[r, x]
    rows = [ups[pl.ds(32 * i + 4, 24), :] for i in range(12)]
    product = table_dot(jnp.concatenate(rows, axis=0), table_z)
    for r in range(2):
        for x in range(12):
            i = 6 * r + x // 2
            f12[r, x] = guess[r, x] + product[24 * i : 24 * (i + 1)]
    sweep_rows(f10, f12, rhs, lambda x: inv[x], 10, 2)
    for r in range(2):
        for x in range(8):
            out(r, x, swept(f10, rhs(r, x + 3), inv[x + 3], r, x + 1))


def middle(row):
    return pltpu.roll(row, row.shape[0] - 4, 0)[0:16]


def share(alone, kappa, inv, image, zero, guess, sums):
    nothing = jnp.zeros((24, 256), F32)
    for r in range(2):
        for x in range(14):
            if 2 <= x < 12:
                image[r, x] = (6.0 + kappa(x)) * alone[r, x + 1] - sides(alone, r, x + 1)
                zero[r, x] = inv(x) * image[r, x]
            else:
                image[r, x] = nothing
                zero[r, x] = nothing
        for x in (0, 1, 14, 15):
            guess[r, x] = nothing
        for x in range(2, 14):
            guess[r, x] = swept(zero, image[r, x - 1], inv(x - 1), r, x - 1)
    pairs = []
    for r in range(2):
        rows = []
        for x in range(14):
            back = (6.0 + kappa(x)) * guess[r, x + 1] - sides(guess, r, x + 1)
            rows.append(image[r, x] - back)
        pairs = pairs + [rows[0]]
        pairs = pairs + [rows[2 * x + 1] + rows[2 * x + 2] for x in range(6)] + [rows[13]]
    return level_rows(pairs, sums)


def precond_kernel(weights, place, gathered, level, guess, both, inv,
                   precond, diag_out, part, low, high,
                   zero_level, narrow, alone, image, zero, guess_alone, sums,
                   spread, s10, s8, s6, ups, f12, f10):
    level_pre(lambda r, x: level[r, x], lambda x: level[2, x], narrow, zero_level, 4, 4)
    rows, rhs = coarse_rows(gathered)
    diag = coarse_diag_of(rows, weights)
    for x in range(KX):
        diag_out[x] = diag[x]
    value = coarse_solve(rhs, diag, weights)
    own = own_rows((24, 256), 4, 20)
    top = iota((8, LANES), 0) < 4
    for r in range(2):
        for x in (0, 1, 2, 3, 12, 13, 14, 15):
            alone[r, x] = jnp.zeros((24, 256), F32)

    def out(r, x, row):
        own_part = middle(row)
        precond[r, x] = own_part
        alone[r, x + 4] = jnp.where(own, row, 0.0)
        left, right = own_part[:, :LANES], own_part[:, LANES:]
        low[r, x, 0:8, :] = jnp.where(top, left[0:8], pltpu.roll(right[0:8], 4, 0))
        high[r, x, 0:8, :] = jnp.where(top, pltpu.roll(left[8:16], 4, 0), right[8:16])

    post(
        place, value, spread, narrow, lambda r, x: level[r, x], lambda x: level[2, x],
        guess, lambda r, x: both[r, x], inv, s10, s8, s6, ups, f12, f10, out,
    )
    level_row = share(
        alone, lambda x: both[2, x], lambda x: inv[x], image, zero, guess_alone, sums
    )
    for r in range(2):
        for x in range(8):
            row = level_row(8 * r + x)
            part[r, x] = row
            low[r, x, 8:16, :] = pltpu.roll(row, 14, 0)[0:8]
            high[r, x, 8:16, :] = row[8:16]


def final_kernel(weights, place, gathered, diag_in, narrow, level, first, image, inv, precond, right,
                 solution_field, residual, direction, zero, guess, spread, s10, s8, s6, ups, f12, f10):
    for r in range(2):
        for x in range(14):
            zero[r, x] = inv[x] * image[r, x]
    sweep_rows(guess, zero, lambda r, x: image[r, x], lambda x: inv[x], 12, 1)
    rows, rhs = coarse_rows(gathered)
    diag = [diag_in[x] for x in range(KX)]
    value = coarse_solve(rhs, diag, weights)
    sums = jnp.sum(total(rows), axis=0, keepdims=True)
    product = jnp.sum(total([a * b for a, b in zip(rhs, value)]), axis=0, keepdims=True)
    line = iota(sums.shape, 1)

    def pick(row, low, high):
        return jnp.sum(jnp.where((line >= low) & (line < high), row, 0.0), axis=1, keepdims=True)

    alphas, betas = [], []
    for r in range(2):
        rz = pick(sums, TOTAL_LANE + r, TOTAL_LANE + r + 1)
        pq = pick(sums, TOTAL_LANE + 2 + r, TOTAL_LANE + 3 + r)
        energy = pick(sums, TOTAL_LANE + 4 + r, TOTAL_LANE + 5 + r)
        energy = energy + 4.0 * pick(product, r * KZ, (r + 1) * KZ)
        alpha = rz / pq
        alphas.append(alpha)
        betas.append(alpha * alpha * energy / rz - 1.0)

    def out(r, x, row):
        p = precond[r, x]
        solution_field[r, x] = alphas[r] * p
        residual[r, x] = right[r, x] - alphas[r] * middle(image[r, x + 3])
        direction[r, x] = p - alphas[r] * middle(row) + betas[r] * p

    post(
        place, value, spread, narrow, lambda r, x: level[r, x - 2], lambda x: first[2, x],
        guess, lambda r, x: image[r, x], inv, s10, s8, s6, ups, f12, f10, out,
    )


def call(kernel, outs, scratch, place=None):
    vmem = pl.BlockSpec(memory_space=pltpu.VMEM)

    def run(*args):
        specs = [vmem] * len(args)
        if place is not None:
            args = (place,) + args
            specs = [pl.BlockSpec(memory_space=pltpu.SMEM)] + specs
        return pl.pallas_call(
            kernel,
            out_shape=[jax.ShapeDtypeStruct(shape, F32) for shape in outs],
            in_specs=specs,
            out_specs=[vmem] * len(outs),
            scratch_shapes=[pltpu.VMEM(shape, F32) for shape in scratch],
            compiler_params=pltpu.CompilerParams(vmem_limit_bytes=16 * 1024 * 1024),
        )(*args)

    return run


def swap_y(low, high):
    count = lax.axis_size("gy")
    even = lax.axis_index("gy") % 2 == 0
    near_pairs = [(i, i + 1) for i in range(0, count, 2)]
    far_pairs = [(i, i + 1) for i in range(1, count - 1, 2)]
    near_pairs = near_pairs + [(b, a) for a, b in near_pairs]
    far_pairs = far_pairs + [(b, a) for a, b in far_pairs]
    far = lax.ppermute(jnp.where(even, low, high), "gy", far_pairs)
    near = lax.ppermute(jnp.where(even, high, low), "gy", near_pairs)
    return jnp.where(even, far, near), jnp.where(even, near, far)


def swap_x(low, high):
    count = lax.axis_size("gx")
    forward = [(i, i + 1) for i in range(count - 1)]
    backward = [(b, a) for a, b in forward]
    return lax.ppermute(high, "gx", forward), lax.ppermute(low, "gx", backward)


def extended_x(block, width):
    low, high = swap_x(block[:, :width], block[:, block.shape[1] - width :])
    return jnp.concatenate([low, block, high], axis=1)


def extended(block):
    low, high = swap_y(block[:, :, :3], block[:, :, block.shape[2] - 3 :])
    block = jnp.concatenate([low, block, high], axis=2)
    return extended_x(jnp.pad(block, ((0, 0), (0, 0), (1, 1), (0, 0))), 3)


def extended_level(level):
    low, high = swap_y(level[:, :, :4], level[:, :, 4:])
    return extended_x(jnp.concatenate([low, level, high], axis=2), 4)


def halves_to_rows(block):
    return jnp.concatenate([block[..., :LANES], block[..., LANES:]], axis=2)


def rows_to_halves(block):
    rows = block.shape[2] // 2
    return jnp.concatenate([block[:, :, :rows], block[:, :, rows:]], axis=3)


def exchange_shares(precond, part, low, high):
    low, high = swap_y(low, high)
    wide = jnp.concatenate([rows_to_halves(low[:, :, :8]), precond, rows_to_halves(high[:, :, :8])], axis=2)
    part = part + jnp.pad(low[:, :, 8:14], ((0, 0), (0, 0), (0, 10), (0, 0)))
    part = part + jnp.pad(high[:, :, 8:14], ((0, 0), (0, 0), (10, 0), (0, 0)))
    low = jnp.concatenate([halves_to_rows(wide[:, :4]), part[:, :4]], axis=2)
    high = jnp.concatenate([halves_to_rows(wide[:, 4:]), part[:, 4:]], axis=2)
    low, high = swap_x(low, high)
    wide = jnp.concatenate([rows_to_halves(low[:, :, :48]), wide, rows_to_halves(high[:, :, :48])], axis=1)
    part = jnp.concatenate([part[:, :4] + low[:, :, 48:], part[:, 4:] + high[:, :, 48:]], axis=1)
    return wide, part


def gather_all(line, beside):
    size_x = lax.axis_size("gx")
    size_y = lax.axis_size("gy")
    rows = lax.all_to_all(line, "gy", 0, 0, tiled=True).reshape(KY, size_y // KY, LANES)
    even, odd = rows[:, 0], rows[:, 1]
    other = jnp.pad(even[1:], ((0, 1), (0, 0))) + jnp.pad(odd[:-1], ((1, 0), (0, 0)))
    other = jnp.pad(other[:, OTHER_LANE : 2 * OTHER_LANE], ((0, 0), (0, LANES - OTHER_LANE)))
    rows, beside = lax.optimization_barrier((even + odd + other, beside))
    spread = jnp.broadcast_to(rows[None], (size_x, KY, LANES))
    return lax.all_to_all(spread, "gx", 0, 0, tiled=True), beside


def local(right_side, diagonal):
    block_x = right_side.shape[1] * lax.axis_size("gx") // 2 // KX
    block_y = right_side.shape[2] * lax.axis_size("gy") // 2 // KY
    block_z = right_side.shape[3] // 2 // KZ
    size_y = lax.axis_size("gy")
    weights = (float(block_y * block_z), float(block_x * block_z), float(block_x * block_y))
    place = jnp.stack([lax.axis_index("gx"), lax.axis_index("gy")]).astype(jnp.int32)

    both = extended(jnp.concatenate([right_side, diagonal[None]], axis=0))
    inv, guess, level, line = call(
        fine_kernel,
        [(14, 24, 256), (2, 12, 24, 256), (3, 4, 8, LANES), (size_y, LANES)],
        [(2, 14, 24, 256), (448, LANES), (2, 12, 16, LANES), (2, 10, 16, LANES)],
        place,
    )(both)
    gathered, first = gather_all(line, extended_level(level))
    post_scratch = [
        (2, KX + 2, 8 + KY + 8, LANES), (2, 10, 16, LANES), (2, 8, 16, LANES), (2, 6, 16, LANES),
        (384, LANES), (2, 12, 24, 256), (2, 10, 24, 256),
    ]
    precond, diag, part, low, high = call(
        functools.partial(precond_kernel, weights),
        [(2, 8, 16, 256), (KX, KY, LANES), (2, 8, 16, LANES), (2, 8, 16, LANES), (2, 8, 16, LANES)],
        [
            (2, 12, 16, LANES), (2, 10, 16, LANES), (2, 16, 24, 256), (2, 14, 24, 256),
            (2, 14, 24, 256), (2, 16, 24, 256), (512, LANES),
        ] + post_scratch,
        place,
    )(gathered, first, guess, both, inv)
    wide, level_q = exchange_shares(precond, part, low, high)
    image, inner, line_q = call(
        image_kernel,
        [(2, 14, 24, 256), (2, 6, 16, LANES), (size_y, LANES)],
        [(2, 14, 24, 256), (2, 12, 24, 256), (2, 8, 16, LANES)],
    )(wide, level_q, first, both, inv)
    low, high = swap_x(inner[:, 2:4], inner[:, 2:4])
    gathered_q, narrow_q = gather_all(line_q, jnp.concatenate([low, inner, high], axis=1))
    return tuple(
        call(
            functools.partial(final_kernel, weights),
            [(2, 8, 16, 256)] * 3,
            [(2, 14, 24, 256), (2, 12, 24, 256)] + post_scratch,
            place,
        )(gathered_q, diag, narrow_q, level_q, first, image, inv, precond, right_side)
    )


def solution(mesh):
    placed = (P(None, "gx", "gy", None), P("gx", "gy", None))
    return jax.shard_map(
        local,
        mesh=mesh,
        in_specs=placed,
        out_specs=(P(None, "gx", "gy", None),) * 3,
        check_vma=False,
    )
```

```python
import functools

import jax
import jax.numpy as jnp
from jax import lax
from jax.experimental import pallas as pl
from jax.experimental.pallas import tpu as pltpu
from jax.sharding import PartitionSpec as P

KX = 16
KY = 16
KZ = 8
CSWEEPS = 4
OMEGA = 0.8
HIGH = lax.Precision.HIGHEST
F32 = jnp.float32
LANES = 128
SIDE_LANE = 16
OTHER_LANE = 48
DIAG_GROUP = 12
DIAG_LANE = 96
TOTAL_LANE = 104


def dot(a, b):
    return jnp.dot(a, b, precision=HIGH, preferred_element_type=F32)


def table_dot(a, table):
    parts = []
    for _ in range(3):
        part = a.astype(jnp.bfloat16).astype(F32)
        a = a - part
        parts.append(part)
    rows = a.shape[0]
    stacked = jnp.concatenate(parts, axis=0).astype(jnp.bfloat16)
    product = jnp.dot(stacked, table.astype(jnp.bfloat16), preferred_element_type=F32)
    return product[:rows] + product[rows : 2 * rows] + product[2 * rows :]


def iota(shape, dim):
    return lax.broadcasted_iota(jnp.int32, shape, dim)


def z_sides(row):
    depth = row.shape[-1]
    lane = iota(row.shape, 1)
    before = jnp.where(lane == 0, 0.0, pltpu.roll(row, 1, 1))
    after = jnp.where(lane == depth - 1, 0.0, pltpu.roll(row, depth - 1, 1))
    return before + after


def sides(ref, r, x):
    row = ref[r, x]
    rows = row.shape[0]
    along_y = pltpu.roll(row, 1, 0) + pltpu.roll(row, rows - 1, 0)
    return ref[r, x - 1] + ref[r, x + 1] + along_y + z_sides(row)


def swept(field, rhs, inverse, r, x):
    return (1.0 - OMEGA) * field[r, x] + inverse * (rhs + sides(field, r, x))


def sweep_rows(out, field, rhs, inverse, count, shift):
    for r in range(2):
        for x in range(count):
            out[r, x] = swept(field, rhs(r, x + shift), inverse(x + shift), r, x + 1)


def inverse_of(kappa):
    return jnp.where(kappa > 0.0, OMEGA / (6.0 + kappa), 0.0)


def pair_table(wide, narrow):
    return (iota((wide, narrow), 0) // 2 == iota((wide, narrow), 1)).astype(F32)


def copy_table(narrow, wide):
    return (iota((narrow, wide), 0) == iota((narrow, wide), 1) // 2).astype(F32)


def fine_pre(wide, kappa, inv, zero, guess, sums):
    for r in range(2):
        for x in range(14):
            zero[r, x] = inv(x) * wide[r, x]
    sweep_rows(guess, zero, lambda r, x: wide[r, x], inv, 12, 1)
    left = []
    for r in range(2):
        rows = []
        for x in range(8):
            image = (6.0 + kappa(x + 3)) * guess[r, x + 2] - sides(guess, r, x + 2)
            rows.append(wide[r, x + 3] - image)
        left.append(rows)
    pairs = [left[r][2 * x] + left[r][2 * x + 1] for r in range(2) for x in range(4)]
    return level_rows(pairs + [kappa(2 * x + 1) + kappa(2 * x + 2) for x in range(6)], sums)


def level_rows(pairs, sums):
    table = pair_table(256, LANES)
    sums[...] = jnp.zeros(sums.shape, F32)
    product = table_dot(jnp.concatenate(pairs, axis=0), table)
    for i in range(len(pairs)):
        sums[pl.ds(32 * i + 4, 24), :] = product[24 * i : 24 * (i + 1)]

    def level_row(i):
        pair = sums[pl.ds(32 * i, 16, stride=2), :] + sums[pl.ds(32 * i + 1, 16, stride=2), :]
        return pair * 0.25

    return level_row


def own_rows(shape, low, high):
    row = iota(shape, 0)
    return (row >= low) & (row < high)


def own_eight(row):
    return pltpu.roll(row, 12, 0)[0:8]


def gathered_line(vectors):
    row = iota((16, LANES), 0)
    stacked = jnp.zeros((16, LANES), F32)
    for group, vector in vectors.items():
        stacked = jnp.where(row == group, vector, stacked)
    table = iota((LANES, LANES), 0) // (LANES // KZ) == iota((LANES, LANES), 1) % KZ
    spread = table_dot(stacked, table.astype(F32))
    return jnp.sum(jnp.where(iota((16, LANES), 1) // KZ == row, spread, 0.0), axis=0, keepdims=True)


def level_pre(rhs, extra, guess, zero, first, last):
    linv = [inverse_of(extra(x)) for x in range(12)]
    for r in range(2):
        for x in range(12):
            zero[r, x] = linv[x] * rhs(r, x)
    sweep_rows(guess, zero, rhs, lambda x: linv[x], 10, 1)
    left = []
    for r in range(2):
        rows = []
        for x in range(first, last):
            image = (6.0 + extra(x)) * guess[r, x - 1] - sides(guess, r, x - 1)
            rows.append(rhs(r, x) - image)
        left.append(rows)
    return left


def total(rows):
    out = rows[0]
    for row in rows[1:]:
        out = out + row
    return out


def fine_kernel(place, both, inv, guess, level, line, zero, sums, zero_level, guess_level):
    for x in range(14):
        inv[x] = inverse_of(both[2, x])
    level_row = fine_pre(both, lambda x: both[2, x], lambda x: inv[x], zero, guess, sums)
    own = own_rows((16, LANES), 4, 12)
    nothing = jnp.zeros((16, LANES), F32)
    rhs = [[jnp.where(own, level_row(4 * r + x), 0.0) for x in range(4)] for r in range(2)]
    extra = [level_row(8 + x) for x in range(6)]
    for r in range(2):
        for x in range(4):
            level[r, x] = own_eight(rhs[r][x])
    for x in range(4):
        level[2, x] = own_eight(extra[x + 1])
    left = level_pre(
        lambda r, x: rhs[r][x - 4] if 4 <= x < 8 else nothing,
        lambda x: extra[x - 3] if 3 <= x < 9 else nothing,
        guess_level, zero_level, 2, 10,
    )
    row = iota((16, LANES), 0)
    odd = place[1] % 2
    other = (row < 4 * (1 - odd)) | (row >= 16 - 4 * odd)
    vectors = {}
    for r in range(2):
        for side, rows in enumerate((left[r][2:6], left[r][0:2], left[r][6:8])):
            column = total(rows)
            for far in range(2):
                part = jnp.where(other, column, 0.0) if far else jnp.where(other, 0.0, column)
                vectors[(3 * far + side) * 2 + r] = jnp.sum(part, axis=0, keepdims=True)
    diag_sum = jnp.where(own, total(extra[1:5]), 0.0)
    vectors[DIAG_GROUP] = jnp.sum(diag_sum, axis=0, keepdims=True)
    line[...] = jnp.broadcast_to(gathered_line(vectors), line.shape)


def fold(field):
    folded = field[0:8] + field[8:16] + field[16:24]
    return folded[:, :LANES] + folded[:, LANES:]


def image_kernel(wide, level, first, both, inv, image, narrow, line, zero, guess, zero_level):
    for r in range(2):
        for x in range(14):
            image[r, x] = (6.0 + both[2, x]) * wide[r, x + 1] - sides(wide, r, x + 1)
            zero[r, x] = inv[x] * image[r, x]
    sweep_rows(guess, zero, lambda r, x: image[r, x], lambda x: inv[x], 12, 1)
    own = own_rows((24, 256), 4, 20)
    own_level = own_rows((16, LANES), 4, 12)
    extra = lambda x: first[2, x + 2]
    linv = [inverse_of(extra(x)) for x in range(8)]
    for r in range(2):
        for x in range(8):
            zero_level[r, x] = linv[x] * level[r, x]
    level_rhs = lambda r, x: level[r, x]
    sweep_rows(narrow, zero_level, level_rhs, lambda x: linv[x], 6, 1)
    vectors = {}
    totals = []
    for r in range(2):
        rz = total([both[r, x + 3] * wide[r, x + 4] for x in range(8)])
        pq = total([image[r, x + 3] * wide[r, x + 4] for x in range(8)])
        energy = None
        for x in range(8):
            back = (6.0 + both[2, x + 3]) * guess[r, x + 2] - sides(guess, r, x + 2)
            term = guess[r, x + 2] * (2.0 * image[r, x + 3] - back)
            energy = term if energy is None else energy + term
        energy = fold(jnp.where(own, energy, 0.0))
        column = None
        for x in range(4):
            back = (6.0 + extra(x + 2)) * narrow[r, x + 1] - sides(narrow, r, x + 1)
            left = level[r, x + 2] - back
            column = left if column is None else column + left
            term = narrow[r, x + 1] * (level[r, x + 2] + left)
            term = 4.0 * jnp.where(own_level, term, 0.0)
            energy = energy + term[0:8] + term[8:16]
        vectors[r] = jnp.sum(jnp.where(own_level, column, 0.0), axis=0, keepdims=True)
        totals.append((TOTAL_LANE + r, fold(jnp.where(own, rz, 0.0))))
        totals.append((TOTAL_LANE + 2 + r, fold(jnp.where(own, pq, 0.0))))
        totals.append((TOTAL_LANE + 4 + r, energy))
    out = gathered_line(vectors)
    lane = iota((1, LANES), 1)
    for place, part in totals:
        value = jnp.sum(jnp.sum(part, axis=0, keepdims=True), axis=1, keepdims=True)
        out = jnp.where(lane == place, value, out)
    line[...] = jnp.broadcast_to(out, line.shape)


def coarse_rows(gathered):
    rows = [gathered[x] for x in range(KX)]
    lane = iota(rows[0].shape, 1)
    out = []
    for x in range(KX):
        row = rows[x]
        if x < KX - 1:
            row = row + pltpu.roll(rows[x + 1], LANES - SIDE_LANE, 1)
        if x > 0:
            row = row + pltpu.roll(rows[x - 1], LANES - 2 * SIDE_LANE, 1)
        out.append(jnp.where(lane < 2 * KZ, row, 0.0))
    return rows, out


def coarse_solve(rhs, diag, weights):
    weight_x, weight_y, weight_z = weights
    shape = rhs[0].shape
    row = iota(shape, 0)
    lane = iota(shape, 1) % KZ
    inverse = [OMEGA / d for d in diag]
    value = [i * b for i, b in zip(inverse, rhs)]
    nothing = jnp.zeros(shape, F32)
    for _ in range(CSWEEPS - 1):
        new = []
        for x in range(KX):
            v = value[x]
            below = value[x - 1] if x > 0 else nothing
            above = value[x + 1] if x < KX - 1 else nothing
            along_y = jnp.where(row == 0, 0.0, pltpu.roll(v, 1, 0))
            along_y = along_y + jnp.where(row == KY - 1, 0.0, pltpu.roll(v, shape[0] - 1, 0))
            along_z = jnp.where(lane == 0, 0.0, pltpu.roll(v, 1, 1))
            along_z = along_z + jnp.where(lane == KZ - 1, 0.0, pltpu.roll(v, LANES - 1, 1))
            image = diag[x] * v - (
                weight_x * (below + above) + weight_y * along_y + weight_z * along_z
            )
            new.append(v + inverse[x] * (rhs[x] - image))
        value = new
    return value


def coarse_diag_of(rows, weights):
    lane = iota(rows[0].shape, 1)
    base = 2.0 * (weights[0] + weights[1] + weights[2])
    out = []
    for row in rows:
        first = pltpu.roll(row, LANES - DIAG_LANE, 1)
        second = pltpu.roll(row, LANES - DIAG_LANE + KZ, 1)
        both = jnp.where(lane < KZ, first, jnp.where(lane < 2 * KZ, second, 0.0))
        out.append(base + both)
    return out


def up_blocks(place, value, spread, narrow, target):
    gx, gy = place[0], place[1]
    spread[...] = jnp.zeros(spread.shape, F32)
    stacked = jnp.concatenate(value, axis=0)
    lane_table = iota((LANES, LANES), 0)
    col = iota((LANES, LANES), 1) // (LANES // KZ)
    for r in range(2):
        wide = table_dot(stacked, (lane_table == r * KZ + col).astype(F32))
        for x in range(KX):
            spread[r, x + 1, pl.ds(8, KY), :] = wide[KY * x : KY * (x + 1)]
    odd = gy % 2
    low = gy // 2 + odd + 7
    row = iota((16, LANES), 0)
    limit = 4 + 8 * odd
    for r in range(2):
        for x in range(3):
            first = spread[r, gx + x, pl.ds(low, 1), :]
            second = spread[r, gx + x, pl.ds(low + 1, 1), :]
            tile = jnp.where(row < limit, first, second)
            for i in ((0, 1, 2), (3, 4, 5, 6), (7, 8, 9))[x]:
                target[r, i] = narrow[r, i] + tile


def post(place, value, spread, narrow, level_rhs, extra, guess, rhs, inv, s10, s8, s6, ups, f12, f10, out):
    up_blocks(place, value, spread, narrow, s10)
    linv = {x: inverse_of(extra(x)) for x in range(2, 10)}
    sweep_rows(s8, s10, level_rhs, lambda x: linv[x], 8, 2)
    sweep_rows(s6, s8, level_rhs, lambda x: linv[x], 6, 3)
    table_z = copy_table(LANES, 256)
    for r in range(2):
        for x in range(6):
            base = 32 * (6 * r + x)
            ups[pl.ds(base, 16, stride=2), :] = s6[r, x]
            ups[pl.ds(base + 1, 16, stride=2), :] = s6[r, x]
    rows = [ups[pl.ds(32 * i + 4, 24), :] for i in range(12)]
    product = table_dot(jnp.concatenate(rows, axis=0), table_z)
    for r in range(2):
        for x in range(12):
            i = 6 * r + x // 2
            f12[r, x] = guess[r, x] + product[24 * i : 24 * (i + 1)]
    sweep_rows(f10, f12, rhs, lambda x: inv[x], 10, 2)
    for r in range(2):
        for x in range(8):
            out(r, x, swept(f10, rhs(r, x + 3), inv[x + 3], r, x + 1))


def middle(row):
    return pltpu.roll(row, row.shape[0] - 4, 0)[0:16]


def share(alone, kappa, inv, image, zero, guess, sums):
    nothing = jnp.zeros((24, 256), F32)
    for r in range(2):
        for x in range(14):
            if 2 <= x < 12:
                image[r, x] = (6.0 + kappa(x)) * alone[r, x + 1] - sides(alone, r, x + 1)
                zero[r, x] = inv(x) * image[r, x]
            else:
                image[r, x] = nothing
                zero[r, x] = nothing
        for x in (0, 1, 14, 15):
            guess[r, x] = nothing
        for x in range(2, 14):
            guess[r, x] = swept(zero, image[r, x - 1], inv(x - 1), r, x - 1)
    pairs = []
    for r in range(2):
        rows = []
        for x in range(14):
            back = (6.0 + kappa(x)) * guess[r, x + 1] - sides(guess, r, x + 1)
            rows.append(image[r, x] - back)
        pairs = pairs + [rows[0]]
        pairs = pairs + [rows[2 * x + 1] + rows[2 * x + 2] for x in range(6)] + [rows[13]]
    return level_rows(pairs, sums)


def precond_kernel(weights, place, gathered, level, guess, both, inv,
                   precond, diag_out, part, low, high,
                   zero_level, narrow, alone, image, zero, guess_alone, sums,
                   spread, s10, s8, s6, ups, f12, f10):
    level_pre(lambda r, x: level[r, x], lambda x: level[2, x], narrow, zero_level, 4, 4)
    rows, rhs = coarse_rows(gathered)
    diag = coarse_diag_of(rows, weights)
    for x in range(KX):
        diag_out[x] = diag[x]
    value = coarse_solve(rhs, diag, weights)
    own = own_rows((24, 256), 4, 20)
    top = iota((8, LANES), 0) < 4
    for r in range(2):
        for x in (0, 1, 2, 3, 12, 13, 14, 15):
            alone[r, x] = jnp.zeros((24, 256), F32)

    def out(r, x, row):
        own_part = middle(row)
        precond[r, x] = own_part
        alone[r, x + 4] = jnp.where(own, row, 0.0)
        left, right = own_part[:, :LANES], own_part[:, LANES:]
        low[r, x, 0:8, :] = jnp.where(top, left[0:8], pltpu.roll(right[0:8], 4, 0))
        high[r, x, 0:8, :] = jnp.where(top, pltpu.roll(left[8:16], 4, 0), right[8:16])

    post(
        place, value, spread, narrow, lambda r, x: level[r, x], lambda x: level[2, x],
        guess, lambda r, x: both[r, x], inv, s10, s8, s6, ups, f12, f10, out,
    )
    level_row = share(
        alone, lambda x: both[2, x], lambda x: inv[x], image, zero, guess_alone, sums
    )
    for r in range(2):
        for x in range(8):
            row = level_row(8 * r + x)
            part[r, x] = row
            low[r, x, 8:16, :] = pltpu.roll(row, 14, 0)[0:8]
            high[r, x, 8:16, :] = row[8:16]


def final_kernel(weights, place, gathered, diag_in, narrow, level, first, image, inv, precond, right,
                 solution_field, residual, direction, zero, guess, spread, s10, s8, s6, ups, f12, f10):
    for r in range(2):
        for x in range(14):
            zero[r, x] = inv[x] * image[r, x]
    sweep_rows(guess, zero, lambda r, x: image[r, x], lambda x: inv[x], 12, 1)
    rows, rhs = coarse_rows(gathered)
    diag = [diag_in[x] for x in range(KX)]
    value = coarse_solve(rhs, diag, weights)
    sums = jnp.sum(total(rows), axis=0, keepdims=True)
    product = jnp.sum(total([a * b for a, b in zip(rhs, value)]), axis=0, keepdims=True)
    line = iota(sums.shape, 1)

    def pick(row, low, high):
        return jnp.sum(jnp.where((line >= low) & (line < high), row, 0.0), axis=1, keepdims=True)

    alphas, betas = [], []
    for r in range(2):
        rz = pick(sums, TOTAL_LANE + r, TOTAL_LANE + r + 1)
        pq = pick(sums, TOTAL_LANE + 2 + r, TOTAL_LANE + 3 + r)
        energy = pick(sums, TOTAL_LANE + 4 + r, TOTAL_LANE + 5 + r)
        energy = energy + 4.0 * pick(product, r * KZ, (r + 1) * KZ)
        alpha = rz / pq
        alphas.append(alpha)
        betas.append(alpha * alpha * energy / rz - 1.0)

    def out(r, x, row):
        p = precond[r, x]
        solution_field[r, x] = alphas[r] * p
        residual[r, x] = right[r, x] - alphas[r] * middle(image[r, x + 3])
        direction[r, x] = p - alphas[r] * middle(row) + betas[r] * p

    post(
        place, value, spread, narrow, lambda r, x: level[r, x - 2], lambda x: first[2, x],
        guess, lambda r, x: image[r, x], inv, s10, s8, s6, ups, f12, f10, out,
    )


def call(kernel, outs, scratch, place=None):
    vmem = pl.BlockSpec(memory_space=pltpu.VMEM)

    def run(*args):
        specs = [vmem] * len(args)
        if place is not None:
            args = (place,) + args
            specs = [pl.BlockSpec(memory_space=pltpu.SMEM)] + specs
        return pl.pallas_call(
            kernel,
            out_shape=[jax.ShapeDtypeStruct(shape, F32) for shape in outs],
            in_specs=specs,
            out_specs=[vmem] * len(outs),
            scratch_shapes=[pltpu.VMEM(shape, F32) for shape in scratch],
            compiler_params=pltpu.CompilerParams(vmem_limit_bytes=16 * 1024 * 1024),
        )(*args)

    return run


def swap_y(low, high):
    count = lax.axis_size("gy")
    even = lax.axis_index("gy") % 2 == 0
    near_pairs = [(i, i + 1) for i in range(0, count, 2)]
    far_pairs = [(i, i + 1) for i in range(1, count - 1, 2)]
    near_pairs = near_pairs + [(b, a) for a, b in near_pairs]
    far_pairs = far_pairs + [(b, a) for a, b in far_pairs]
    far = lax.ppermute(jnp.where(even, low, high), "gy", far_pairs)
    near = lax.ppermute(jnp.where(even, high, low), "gy", near_pairs)
    return jnp.where(even, far, near), jnp.where(even, near, far)


def swap_x(low, high):
    count = lax.axis_size("gx")
    forward = [(i, i + 1) for i in range(count - 1)]
    backward = [(b, a) for a, b in forward]
    return lax.ppermute(high, "gx", forward), lax.ppermute(low, "gx", backward)


def extended_x(block, width):
    low, high = swap_x(block[:, :width], block[:, block.shape[1] - width :])
    return jnp.concatenate([low, block, high], axis=1)


def extended(block):
    low, high = swap_y(block[:, :, :3], block[:, :, block.shape[2] - 3 :])
    block = jnp.concatenate([low, block, high], axis=2)
    return extended_x(jnp.pad(block, ((0, 0), (0, 0), (1, 1), (0, 0))), 3)


def extended_level(level):
    low, high = swap_y(level[:, :, :4], level[:, :, 4:])
    return extended_x(jnp.concatenate([low, level, high], axis=2), 4)


def halves_to_rows(block):
    return jnp.concatenate([block[..., :LANES], block[..., LANES:]], axis=2)


def rows_to_halves(block):
    rows = block.shape[2] // 2
    return jnp.concatenate([block[:, :, :rows], block[:, :, rows:]], axis=3)


def exchange_shares(precond, part, low, high):
    low, high = swap_y(low, high)
    wide = jnp.concatenate([rows_to_halves(low[:, :, :8]), precond, rows_to_halves(high[:, :, :8])], axis=2)
    part = part + jnp.pad(low[:, :, 8:14], ((0, 0), (0, 0), (0, 10), (0, 0)))
    part = part + jnp.pad(high[:, :, 8:14], ((0, 0), (0, 0), (10, 0), (0, 0)))
    low = jnp.concatenate([halves_to_rows(wide[:, :4]), part[:, :4]], axis=2)
    high = jnp.concatenate([halves_to_rows(wide[:, 4:]), part[:, 4:]], axis=2)
    low, high = swap_x(low, high)
    wide = jnp.concatenate([rows_to_halves(low[:, :, :48]), wide, rows_to_halves(high[:, :, :48])], axis=1)
    part = jnp.concatenate([part[:, :4] + low[:, :, 48:], part[:, 4:] + high[:, :, 48:]], axis=1)
    return wide, part


def gather_y(line):
    return lax.all_to_all(line, "gy", 0, 0, tiled=True)


def gather_x(rows, beside=None):
    size_x = lax.axis_size("gx")
    rows = rows.reshape(KY, rows.shape[0] // KY, LANES)
    even, odd = rows[:, 0], rows[:, 1]
    other = jnp.pad(even[1:], ((0, 1), (0, 0))) + jnp.pad(odd[:-1], ((1, 0), (0, 0)))
    other = jnp.pad(other[:, OTHER_LANE : 2 * OTHER_LANE], ((0, 0), (0, LANES - OTHER_LANE)))
    rows = even + odd + other
    if beside is not None:
        rows, beside = lax.optimization_barrier((rows, beside))
    spread = jnp.broadcast_to(rows[None], (size_x, KY, LANES))
    return lax.all_to_all(spread, "gx", 0, 0, tiled=True), beside


def local(right_side, diagonal):
    block_x = right_side.shape[1] * lax.axis_size("gx") // 2 // KX
    block_y = right_side.shape[2] * lax.axis_size("gy") // 2 // KY
    block_z = right_side.shape[3] // 2 // KZ
    size_y = lax.axis_size("gy")
    weights = (float(block_y * block_z), float(block_x * block_z), float(block_x * block_y))
    place = jnp.stack([lax.axis_index("gx"), lax.axis_index("gy")]).astype(jnp.int32)

    both = extended(jnp.concatenate([right_side, diagonal[None]], axis=0))
    inv, guess, level, line = call(
        fine_kernel,
        [(14, 24, 256), (2, 12, 24, 256), (3, 4, 8, LANES), (size_y, LANES)],
        [(2, 14, 24, 256), (448, LANES), (2, 12, 16, LANES), (2, 10, 16, LANES)],
        place,
    )(both)
    rows, level = lax.optimization_barrier((gather_y(line), level))
    gathered, _ = gather_x(rows)
    first = extended_level(level)
    post_scratch = [
        (2, KX + 2, 8 + KY + 8, LANES), (2, 10, 16, LANES), (2, 8, 16, LANES), (2, 6, 16, LANES),
        (384, LANES), (2, 12, 24, 256), (2, 10, 24, 256),
    ]
    precond, diag, part, low, high = call(
        functools.partial(precond_kernel, weights),
        [(2, 8, 16, 256), (KX, KY, LANES), (2, 8, 16, LANES), (2, 8, 16, LANES), (2, 8, 16, LANES)],
        [
            (2, 12, 16, LANES), (2, 10, 16, LANES), (2, 16, 24, 256), (2, 14, 24, 256),
            (2, 14, 24, 256), (2, 16, 24, 256), (512, LANES),
        ] + post_scratch,
        place,
    )(gathered, first, guess, both, inv)
    wide, level_q = exchange_shares(precond, part, low, high)
    image, inner, line_q = call(
        image_kernel,
        [(2, 14, 24, 256), (2, 6, 16, LANES), (size_y, LANES)],
        [(2, 14, 24, 256), (2, 12, 24, 256), (2, 8, 16, LANES)],
    )(wide, level_q, first, both, inv)
    low, high = swap_x(inner[:, 2:4], inner[:, 2:4])
    gathered_q, narrow_q = gather_x(gather_y(line_q), jnp.concatenate([low, inner, high], axis=1))
    return tuple(
        call(
            functools.partial(final_kernel, weights),
            [(2, 8, 16, 256)] * 3,
            [(2, 14, 24, 256), (2, 12, 24, 256)] + post_scratch,
            place,
        )(gathered_q, diag, narrow_q, level_q, first, image, inv, precond, right_side)
    )


def solution(mesh):
    placed = (P(None, "gx", "gy", None), P("gx", "gy", None))
    return jax.shard_map(
        local,
        mesh=mesh,
        in_specs=placed,
        out_specs=(P(None, "gx", "gy", None),) * 3,
        check_vma=False,
    )
```

```python
import functools

import jax
import jax.numpy as jnp
from jax import lax
from jax.experimental import pallas as pl
from jax.experimental.pallas import tpu as pltpu
from jax.sharding import PartitionSpec as P

KX = 16
KY = 16
KZ = 8
CSWEEPS = 4
OMEGA = 0.8
HIGH = lax.Precision.HIGHEST
F32 = jnp.float32
LANES = 128
SIDE_LANE = 16
OTHER_LANE = 48
DIAG_GROUP = 12
DIAG_LANE = 96
TOTAL_LANE = 104


def dot(a, b):
    return jnp.dot(a, b, precision=HIGH, preferred_element_type=F32)


def table_dot(a, table):
    parts = []
    for _ in range(3):
        part = a.astype(jnp.bfloat16).astype(F32)
        a = a - part
        parts.append(part)
    rows = a.shape[0]
    stacked = jnp.concatenate(parts, axis=0).astype(jnp.bfloat16)
    product = jnp.dot(stacked, table.astype(jnp.bfloat16), preferred_element_type=F32)
    return product[:rows] + product[rows : 2 * rows] + product[2 * rows :]


def iota(shape, dim):
    return lax.broadcasted_iota(jnp.int32, shape, dim)


def z_sides(row):
    lane = iota((row.shape[0], LANES), 1)
    parts = [row[:, i : i + LANES] for i in range(0, row.shape[1], LANES)]
    before = [pltpu.roll(part, 1, 1) for part in parts]
    after = [pltpu.roll(part, LANES - 1, 1) for part in parts]
    out = []
    for i in range(len(parts)):
        first = before[i - 1] if i > 0 else 0.0
        last = after[i + 1] if i < len(parts) - 1 else 0.0
        out.append(
            jnp.where(lane == 0, first, before[i]) + jnp.where(lane == LANES - 1, last, after[i])
        )
    return jnp.concatenate(out, axis=1) if len(out) > 1 else out[0]


def sides(ref, r, x):
    row = ref[r, x]
    rows = row.shape[0]
    along_y = pltpu.roll(row, 1, 0) + pltpu.roll(row, rows - 1, 0)
    return ref[r, x - 1] + ref[r, x + 1] + along_y + z_sides(row)


def swept(field, rhs, inverse, r, x):
    return (1.0 - OMEGA) * field[r, x] + inverse * (rhs + sides(field, r, x))


def sweep_rows(out, field, rhs, inverse, count, shift):
    for r in range(2):
        for x in range(count):
            out[r, x] = swept(field, rhs(r, x + shift), inverse(x + shift), r, x + 1)


def inverse_of(kappa):
    return jnp.where(kappa > 0.0, OMEGA / (6.0 + kappa), 0.0)


def pair_table(wide, narrow):
    return (iota((wide, narrow), 0) // 2 == iota((wide, narrow), 1)).astype(F32)


def copy_table(narrow, wide):
    return (iota((narrow, wide), 0) == iota((narrow, wide), 1) // 2).astype(F32)


def fine_pre(wide, kappa, inv, zero, guess, sums):
    for r in range(2):
        for x in range(14):
            zero[r, x] = inv(x) * wide[r, x]
    sweep_rows(guess, zero, lambda r, x: wide[r, x], inv, 12, 1)
    left = []
    for r in range(2):
        rows = []
        for x in range(8):
            image = (6.0 + kappa(x + 3)) * guess[r, x + 2] - sides(guess, r, x + 2)
            rows.append(wide[r, x + 3] - image)
        left.append(rows)
    pairs = [left[r][2 * x] + left[r][2 * x + 1] for r in range(2) for x in range(4)]
    return level_rows(pairs + [kappa(2 * x + 1) + kappa(2 * x + 2) for x in range(6)], sums)


def level_rows(pairs, sums):
    table = pair_table(256, LANES)
    sums[...] = jnp.zeros(sums.shape, F32)
    product = table_dot(jnp.concatenate(pairs, axis=0), table)
    for i in range(len(pairs)):
        sums[pl.ds(32 * i + 4, 24), :] = product[24 * i : 24 * (i + 1)]

    def level_row(i):
        pair = sums[pl.ds(32 * i, 16, stride=2), :] + sums[pl.ds(32 * i + 1, 16, stride=2), :]
        return pair * 0.25

    return level_row


def own_rows(shape, low, high):
    row = iota(shape, 0)
    return (row >= low) & (row < high)


def own_eight(row):
    return pltpu.roll(row, 12, 0)[0:8]


def gathered_line(vectors):
    row = iota((16, LANES), 0)
    stacked = jnp.zeros((16, LANES), F32)
    for group, vector in vectors.items():
        stacked = jnp.where(row == group, vector, stacked)
    table = iota((LANES, LANES), 0) // (LANES // KZ) == iota((LANES, LANES), 1) % KZ
    spread = table_dot(stacked, table.astype(F32))
    return jnp.sum(jnp.where(iota((16, LANES), 1) // KZ == row, spread, 0.0), axis=0, keepdims=True)


def level_pre(rhs, extra, guess, zero, first, last):
    linv = [inverse_of(extra(x)) for x in range(12)]
    for r in range(2):
        for x in range(12):
            zero[r, x] = linv[x] * rhs(r, x)
    sweep_rows(guess, zero, rhs, lambda x: linv[x], 10, 1)
    left = []
    for r in range(2):
        rows = []
        for x in range(first, last):
            image = (6.0 + extra(x)) * guess[r, x - 1] - sides(guess, r, x - 1)
            rows.append(rhs(r, x) - image)
        left.append(rows)
    return left


def total(rows):
    out = rows[0]
    for row in rows[1:]:
        out = out + row
    return out


def fine_kernel(place, both, inv, guess, level, line, zero, sums, zero_level, guess_level):
    for x in range(14):
        inv[x] = inverse_of(both[2, x])
    level_row = fine_pre(both, lambda x: both[2, x], lambda x: inv[x], zero, guess, sums)
    own = own_rows((16, LANES), 4, 12)
    nothing = jnp.zeros((16, LANES), F32)
    rhs = [[jnp.where(own, level_row(4 * r + x), 0.0) for x in range(4)] for r in range(2)]
    extra = [level_row(8 + x) for x in range(6)]
    for r in range(2):
        for x in range(4):
            level[r, x] = own_eight(rhs[r][x])
    for x in range(4):
        level[2, x] = own_eight(extra[x + 1])
    left = level_pre(
        lambda r, x: rhs[r][x - 4] if 4 <= x < 8 else nothing,
        lambda x: extra[x - 3] if 3 <= x < 9 else nothing,
        guess_level, zero_level, 2, 10,
    )
    row = iota((16, LANES), 0)
    odd = place[1] % 2
    other = (row < 4 * (1 - odd)) | (row >= 16 - 4 * odd)
    vectors = {}
    for r in range(2):
        for side, rows in enumerate((left[r][2:6], left[r][0:2], left[r][6:8])):
            column = total(rows)
            for far in range(2):
                part = jnp.where(other, column, 0.0) if far else jnp.where(other, 0.0, column)
                vectors[(3 * far + side) * 2 + r] = jnp.sum(part, axis=0, keepdims=True)
    diag_sum = jnp.where(own, total(extra[1:5]), 0.0)
    vectors[DIAG_GROUP] = jnp.sum(diag_sum, axis=0, keepdims=True)
    line[...] = jnp.broadcast_to(gathered_line(vectors), line.shape)


def fold(field):
    folded = field[0:8] + field[8:16] + field[16:24]
    return folded[:, :LANES] + folded[:, LANES:]


def image_kernel(wide, level, first, both, inv, image, narrow, line, zero, guess, zero_level):
    for r in range(2):
        for x in range(14):
            image[r, x] = (6.0 + both[2, x]) * wide[r, x + 1] - sides(wide, r, x + 1)
            zero[r, x] = inv[x] * image[r, x]
    sweep_rows(guess, zero, lambda r, x: image[r, x], lambda x: inv[x], 12, 1)
    own = own_rows((24, 256), 4, 20)
    own_level = own_rows((16, LANES), 4, 12)
    extra = lambda x: first[2, x + 2]
    linv = [inverse_of(extra(x)) for x in range(8)]
    for r in range(2):
        for x in range(8):
            zero_level[r, x] = linv[x] * level[r, x]
    level_rhs = lambda r, x: level[r, x]
    sweep_rows(narrow, zero_level, level_rhs, lambda x: linv[x], 6, 1)
    vectors = {}
    totals = []
    for r in range(2):
        rz = total([both[r, x + 3] * wide[r, x + 4] for x in range(8)])
        pq = total([image[r, x + 3] * wide[r, x + 4] for x in range(8)])
        energy = None
        for x in range(8):
            back = (6.0 + both[2, x + 3]) * guess[r, x + 2] - sides(guess, r, x + 2)
            term = guess[r, x + 2] * (2.0 * image[r, x + 3] - back)
            energy = term if energy is None else energy + term
        energy = fold(jnp.where(own, energy, 0.0))
        column = None
        for x in range(4):
            back = (6.0 + extra(x + 2)) * narrow[r, x + 1] - sides(narrow, r, x + 1)
            left = level[r, x + 2] - back
            column = left if column is None else column + left
            term = narrow[r, x + 1] * (level[r, x + 2] + left)
            term = 4.0 * jnp.where(own_level, term, 0.0)
            energy = energy + term[0:8] + term[8:16]
        vectors[r] = jnp.sum(jnp.where(own_level, column, 0.0), axis=0, keepdims=True)
        totals.append((TOTAL_LANE + r, fold(jnp.where(own, rz, 0.0))))
        totals.append((TOTAL_LANE + 2 + r, fold(jnp.where(own, pq, 0.0))))
        totals.append((TOTAL_LANE + 4 + r, energy))
    out = gathered_line(vectors)
    lane = iota((1, LANES), 1)
    for place, part in totals:
        value = jnp.sum(jnp.sum(part, axis=0, keepdims=True), axis=1, keepdims=True)
        out = jnp.where(lane == place, value, out)
    line[...] = jnp.broadcast_to(out, line.shape)


def coarse_rows(gathered):
    rows = [gathered[x] for x in range(KX)]
    lane = iota(rows[0].shape, 1)
    out = []
    for x in range(KX):
        row = rows[x]
        if x < KX - 1:
            row = row + pltpu.roll(rows[x + 1], LANES - SIDE_LANE, 1)
        if x > 0:
            row = row + pltpu.roll(rows[x - 1], LANES - 2 * SIDE_LANE, 1)
        out.append(jnp.where(lane < 2 * KZ, row, 0.0))
    return rows, out


def coarse_solve(rhs, diag, weights):
    weight_x, weight_y, weight_z = weights
    shape = rhs[0].shape
    row = iota(shape, 0)
    lane = iota(shape, 1) % KZ
    inverse = [OMEGA / d for d in diag]
    value = [i * b for i, b in zip(inverse, rhs)]
    nothing = jnp.zeros(shape, F32)
    for _ in range(CSWEEPS - 1):
        new = []
        for x in range(KX):
            v = value[x]
            below = value[x - 1] if x > 0 else nothing
            above = value[x + 1] if x < KX - 1 else nothing
            along_y = jnp.where(row == 0, 0.0, pltpu.roll(v, 1, 0))
            along_y = along_y + jnp.where(row == KY - 1, 0.0, pltpu.roll(v, shape[0] - 1, 0))
            along_z = jnp.where(lane == 0, 0.0, pltpu.roll(v, 1, 1))
            along_z = along_z + jnp.where(lane == KZ - 1, 0.0, pltpu.roll(v, LANES - 1, 1))
            image = diag[x] * v - (
                weight_x * (below + above) + weight_y * along_y + weight_z * along_z
            )
            new.append(v + inverse[x] * (rhs[x] - image))
        value = new
    return value


def coarse_diag_of(rows, weights):
    lane = iota(rows[0].shape, 1)
    base = 2.0 * (weights[0] + weights[1] + weights[2])
    out = []
    for row in rows:
        first = pltpu.roll(row, LANES - DIAG_LANE, 1)
        second = pltpu.roll(row, LANES - DIAG_LANE + KZ, 1)
        both = jnp.where(lane < KZ, first, jnp.where(lane < 2 * KZ, second, 0.0))
        out.append(base + both)
    return out


def up_blocks(place, value, spread, narrow, target):
    gx, gy = place[0], place[1]
    spread[...] = jnp.zeros(spread.shape, F32)
    stacked = jnp.concatenate(value, axis=0)
    lane_table = iota((LANES, LANES), 0)
    col = iota((LANES, LANES), 1) // (LANES // KZ)
    for r in range(2):
        wide = table_dot(stacked, (lane_table == r * KZ + col).astype(F32))
        for x in range(KX):
            spread[r, x + 1, pl.ds(8, KY), :] = wide[KY * x : KY * (x + 1)]
    odd = gy % 2
    low = gy // 2 + odd + 7
    row = iota((16, LANES), 0)
    limit = 4 + 8 * odd
    for r in range(2):
        for x in range(3):
            first = spread[r, gx + x, pl.ds(low, 1), :]
            second = spread[r, gx + x, pl.ds(low + 1, 1), :]
            tile = jnp.where(row < limit, first, second)
            for i in ((0, 1, 2), (3, 4, 5, 6), (7, 8, 9))[x]:
                target[r, i] = narrow[r, i] + tile


def post(place, value, spread, narrow, level_rhs, extra, guess, rhs, inv, s10, s8, s6, ups, f12, f10, out):
    up_blocks(place, value, spread, narrow, s10)
    linv = {x: inverse_of(extra(x)) for x in range(2, 10)}
    sweep_rows(s8, s10, level_rhs, lambda x: linv[x], 8, 2)
    sweep_rows(s6, s8, level_rhs, lambda x: linv[x], 6, 3)
    table_z = copy_table(LANES, 256)
    for r in range(2):
        for x in range(6):
            base = 32 * (6 * r + x)
            ups[pl.ds(base, 16, stride=2), :] = s6[r, x]
            ups[pl.ds(base + 1, 16, stride=2), :] = s6[r, x]
    rows = [ups[pl.ds(32 * i + 4, 24), :] for i in range(12)]
    product = table_dot(jnp.concatenate(rows, axis=0), table_z)
    for r in range(2):
        for x in range(12):
            i = 6 * r + x // 2
            f12[r, x] = guess[r, x] + product[24 * i : 24 * (i + 1)]
    sweep_rows(f10, f12, rhs, lambda x: inv[x], 10, 2)
    for r in range(2):
        for x in range(8):
            out(r, x, swept(f10, rhs(r, x + 3), inv[x + 3], r, x + 1))


def middle(row):
    return pltpu.roll(row, row.shape[0] - 4, 0)[0:16]


def share(alone, kappa, inv, image, zero, guess, sums):
    nothing = jnp.zeros((24, 256), F32)
    for r in range(2):
        for x in range(14):
            if 2 <= x < 12:
                image[r, x] = (6.0 + kappa(x)) * alone[r, x + 1] - sides(alone, r, x + 1)
                zero[r, x] = inv(x) * image[r, x]
            else:
                image[r, x] = nothing
                zero[r, x] = nothing
        for x in (0, 1, 14, 15):
            guess[r, x] = nothing
        for x in range(2, 14):
            guess[r, x] = swept(zero, image[r, x - 1], inv(x - 1), r, x - 1)
    pairs = []
    for r in range(2):
        rows = []
        for x in range(14):
            back = (6.0 + kappa(x)) * guess[r, x + 1] - sides(guess, r, x + 1)
            rows.append(image[r, x] - back)
        pairs = pairs + [rows[0]]
        pairs = pairs + [rows[2 * x + 1] + rows[2 * x + 2] for x in range(6)] + [rows[13]]
    return level_rows(pairs, sums)


def precond_kernel(weights, place, gathered, level, guess, both, inv,
                   precond, diag_out, part, low, high,
                   zero_level, narrow, alone, image, zero, guess_alone, sums,
                   spread, s10, s8, s6, ups, f12, f10):
    level_pre(lambda r, x: level[r, x], lambda x: level[2, x], narrow, zero_level, 4, 4)
    rows, rhs = coarse_rows(gathered)
    diag = coarse_diag_of(rows, weights)
    for x in range(KX):
        diag_out[x] = diag[x]
    value = coarse_solve(rhs, diag, weights)
    own = own_rows((24, 256), 4, 20)
    top = iota((8, LANES), 0) < 4
    for r in range(2):
        for x in (0, 1, 2, 3, 12, 13, 14, 15):
            alone[r, x] = jnp.zeros((24, 256), F32)

    def out(r, x, row):
        own_part = middle(row)
        precond[r, x] = own_part
        alone[r, x + 4] = jnp.where(own, row, 0.0)
        left, right = own_part[:, :LANES], own_part[:, LANES:]
        low[r, x, 0:8, :] = jnp.where(top, left[0:8], pltpu.roll(right[0:8], 4, 0))
        high[r, x, 0:8, :] = jnp.where(top, pltpu.roll(left[8:16], 4, 0), right[8:16])

    post(
        place, value, spread, narrow, lambda r, x: level[r, x], lambda x: level[2, x],
        guess, lambda r, x: both[r, x], inv, s10, s8, s6, ups, f12, f10, out,
    )
    level_row = share(
        alone, lambda x: both[2, x], lambda x: inv[x], image, zero, guess_alone, sums
    )
    for r in range(2):
        for x in range(8):
            row = level_row(8 * r + x)
            part[r, x] = row
            low[r, x, 8:16, :] = pltpu.roll(row, 14, 0)[0:8]
            high[r, x, 8:16, :] = row[8:16]


def final_kernel(weights, place, gathered, diag_in, narrow, level, first, image, inv, precond, right,
                 solution_field, residual, direction, zero, guess, spread, s10, s8, s6, ups, f12, f10):
    for r in range(2):
        for x in range(14):
            zero[r, x] = inv[x] * image[r, x]
    sweep_rows(guess, zero, lambda r, x: image[r, x], lambda x: inv[x], 12, 1)
    rows, rhs = coarse_rows(gathered)
    diag = [diag_in[x] for x in range(KX)]
    value = coarse_solve(rhs, diag, weights)
    sums = jnp.sum(total(rows), axis=0, keepdims=True)
    product = jnp.sum(total([a * b for a, b in zip(rhs, value)]), axis=0, keepdims=True)
    line = iota(sums.shape, 1)

    def pick(row, low, high):
        return jnp.sum(jnp.where((line >= low) & (line < high), row, 0.0), axis=1, keepdims=True)

    alphas, betas = [], []
    for r in range(2):
        rz = pick(sums, TOTAL_LANE + r, TOTAL_LANE + r + 1)
        pq = pick(sums, TOTAL_LANE + 2 + r, TOTAL_LANE + 3 + r)
        energy = pick(sums, TOTAL_LANE + 4 + r, TOTAL_LANE + 5 + r)
        energy = energy + 4.0 * pick(product, r * KZ, (r + 1) * KZ)
        alpha = rz / pq
        alphas.append(alpha)
        betas.append(alpha * alpha * energy / rz - 1.0)

    def out(r, x, row):
        p = precond[r, x]
        solution_field[r, x] = alphas[r] * p
        residual[r, x] = right[r, x] - alphas[r] * middle(image[r, x + 3])
        direction[r, x] = p - alphas[r] * middle(row) + betas[r] * p

    post(
        place, value, spread, narrow, lambda r, x: level[r, x - 2], lambda x: first[2, x],
        guess, lambda r, x: image[r, x], inv, s10, s8, s6, ups, f12, f10, out,
    )


def call(kernel, outs, scratch, place=None):
    vmem = pl.BlockSpec(memory_space=pltpu.VMEM)

    def run(*args):
        specs = [vmem] * len(args)
        if place is not None:
            args = (place,) + args
            specs = [pl.BlockSpec(memory_space=pltpu.SMEM)] + specs
        return pl.pallas_call(
            kernel,
            out_shape=[jax.ShapeDtypeStruct(shape, F32) for shape in outs],
            in_specs=specs,
            out_specs=[vmem] * len(outs),
            scratch_shapes=[pltpu.VMEM(shape, F32) for shape in scratch],
            compiler_params=pltpu.CompilerParams(vmem_limit_bytes=16 * 1024 * 1024),
        )(*args)

    return run


def swap_y(low, high):
    count = lax.axis_size("gy")
    even = lax.axis_index("gy") % 2 == 0
    near_pairs = [(i, i + 1) for i in range(0, count, 2)]
    far_pairs = [(i, i + 1) for i in range(1, count - 1, 2)]
    near_pairs = near_pairs + [(b, a) for a, b in near_pairs]
    far_pairs = far_pairs + [(b, a) for a, b in far_pairs]
    far = lax.ppermute(jnp.where(even, low, high), "gy", far_pairs)
    near = lax.ppermute(jnp.where(even, high, low), "gy", near_pairs)
    return jnp.where(even, far, near), jnp.where(even, near, far)


def swap_x(low, high):
    count = lax.axis_size("gx")
    forward = [(i, i + 1) for i in range(count - 1)]
    backward = [(b, a) for a, b in forward]
    return lax.ppermute(high, "gx", forward), lax.ppermute(low, "gx", backward)


def extended_x(block, width):
    low, high = swap_x(block[:, :width], block[:, block.shape[1] - width :])
    return jnp.concatenate([low, block, high], axis=1)


def extended(block):
    low, high = swap_y(block[:, :, :3], block[:, :, block.shape[2] - 3 :])
    block = jnp.concatenate([low, block, high], axis=2)
    return extended_x(jnp.pad(block, ((0, 0), (0, 0), (1, 1), (0, 0))), 3)


def extended_level(level):
    low, high = swap_y(level[:, :, :4], level[:, :, 4:])
    return extended_x(jnp.concatenate([low, level, high], axis=2), 4)


def halves_to_rows(block):
    return jnp.concatenate([block[..., :LANES], block[..., LANES:]], axis=2)


def rows_to_halves(block):
    rows = block.shape[2] // 2
    return jnp.concatenate([block[:, :, :rows], block[:, :, rows:]], axis=3)


def exchange_shares(precond, part, low, high):
    low, high = swap_y(low, high)
    wide = jnp.concatenate([rows_to_halves(low[:, :, :8]), precond, rows_to_halves(high[:, :, :8])], axis=2)
    part = part + jnp.pad(low[:, :, 8:14], ((0, 0), (0, 0), (0, 10), (0, 0)))
    part = part + jnp.pad(high[:, :, 8:14], ((0, 0), (0, 0), (10, 0), (0, 0)))
    low = jnp.concatenate([halves_to_rows(wide[:, :4]), part[:, :4]], axis=2)
    high = jnp.concatenate([halves_to_rows(wide[:, 4:]), part[:, 4:]], axis=2)
    low, high = swap_x(low, high)
    wide = jnp.concatenate([rows_to_halves(low[:, :, :48]), wide, rows_to_halves(high[:, :, :48])], axis=1)
    part = jnp.concatenate([part[:, :4] + low[:, :, 48:], part[:, 4:] + high[:, :, 48:]], axis=1)
    return wide, part


def gather_all(line, beside):
    size_x = lax.axis_size("gx")
    size_y = lax.axis_size("gy")
    rows = lax.all_to_all(line, "gy", 0, 0, tiled=True).reshape(KY, size_y // KY, LANES)
    even, odd = rows[:, 0], rows[:, 1]
    other = jnp.pad(even[1:], ((0, 1), (0, 0))) + jnp.pad(odd[:-1], ((1, 0), (0, 0)))
    other = jnp.pad(other[:, OTHER_LANE : 2 * OTHER_LANE], ((0, 0), (0, LANES - OTHER_LANE)))
    rows, beside = lax.optimization_barrier((even + odd + other, beside))
    spread = jnp.broadcast_to(rows[None], (size_x, KY, LANES))
    return lax.all_to_all(spread, "gx", 0, 0, tiled=True), beside


def local(right_side, diagonal):
    block_x = right_side.shape[1] * lax.axis_size("gx") // 2 // KX
    block_y = right_side.shape[2] * lax.axis_size("gy") // 2 // KY
    block_z = right_side.shape[3] // 2 // KZ
    size_y = lax.axis_size("gy")
    weights = (float(block_y * block_z), float(block_x * block_z), float(block_x * block_y))
    place = jnp.stack([lax.axis_index("gx"), lax.axis_index("gy")]).astype(jnp.int32)

    both = extended(jnp.concatenate([right_side, diagonal[None]], axis=0))
    inv, guess, level, line = call(
        fine_kernel,
        [(14, 24, 256), (2, 12, 24, 256), (3, 4, 8, LANES), (size_y, LANES)],
        [(2, 14, 24, 256), (448, LANES), (2, 12, 16, LANES), (2, 10, 16, LANES)],
        place,
    )(both)
    gathered, first = gather_all(line, extended_level(level))
    post_scratch = [
        (2, KX + 2, 8 + KY + 8, LANES), (2, 10, 16, LANES), (2, 8, 16, LANES), (2, 6, 16, LANES),
        (384, LANES), (2, 12, 24, 256), (2, 10, 24, 256),
    ]
    precond, diag, part, low, high = call(
        functools.partial(precond_kernel, weights),
        [(2, 8, 16, 256), (KX, KY, LANES), (2, 8, 16, LANES), (2, 8, 16, LANES), (2, 8, 16, LANES)],
        [
            (2, 12, 16, LANES), (2, 10, 16, LANES), (2, 16, 24, 256), (2, 14, 24, 256),
            (2, 14, 24, 256), (2, 16, 24, 256), (512, LANES),
        ] + post_scratch,
        place,
    )(gathered, first, guess, both, inv)
    wide, level_q = exchange_shares(precond, part, low, high)
    image, inner, line_q = call(
        image_kernel,
        [(2, 14, 24, 256), (2, 6, 16, LANES), (size_y, LANES)],
        [(2, 14, 24, 256), (2, 12, 24, 256), (2, 8, 16, LANES)],
    )(wide, level_q, first, both, inv)
    low, high = swap_x(inner[:, 2:4], inner[:, 2:4])
    gathered_q, narrow_q = gather_all(line_q, jnp.concatenate([low, inner, high], axis=1))
    return tuple(
        call(
            functools.partial(final_kernel, weights),
            [(2, 8, 16, 256)] * 3,
            [(2, 14, 24, 256), (2, 12, 24, 256)] + post_scratch,
            place,
        )(gathered_q, diag, narrow_q, level_q, first, image, inv, precond, right_side)
    )


def solution(mesh):
    placed = (P(None, "gx", "gy", None), P("gx", "gy", None))
    return jax.shard_map(
        local,
        mesh=mesh,
        in_specs=placed,
        out_specs=(P(None, "gx", "gy", None),) * 3,
        check_vma=False,
    )
```

```python
import functools

import jax
import jax.numpy as jnp
from jax import lax
from jax.experimental import pallas as pl
from jax.experimental.pallas import tpu as pltpu
from jax.sharding import PartitionSpec as P

KX = 16
KY = 16
KZ = 8
CSWEEPS = 4
OMEGA = 0.8
HIGH = lax.Precision.HIGHEST
F32 = jnp.float32
LANES = 128
SIDE_LANE = 16
OTHER_LANE = 48
DIAG_GROUP = 12
DIAG_LANE = 96
TOTAL_LANE = 104


def dot(a, b):
    return jnp.dot(a, b, precision=HIGH, preferred_element_type=F32)


def table_dot(a, table):
    parts = []
    for _ in range(3):
        part = a.astype(jnp.bfloat16).astype(F32)
        a = a - part
        parts.append(part)
    rows = a.shape[0]
    stacked = jnp.concatenate(parts, axis=0).astype(jnp.bfloat16)
    product = jnp.dot(stacked, table.astype(jnp.bfloat16), preferred_element_type=F32)
    return product[:rows] + product[rows : 2 * rows] + product[2 * rows :]


def iota(shape, dim):
    return lax.broadcasted_iota(jnp.int32, shape, dim)


def z_sides(row):
    lane = iota((row.shape[0], LANES), 1)
    parts = [row[:, i : i + LANES] for i in range(0, row.shape[1], LANES)]
    before = [pltpu.roll(part, 1, 1) for part in parts]
    after = [pltpu.roll(part, LANES - 1, 1) for part in parts]
    out = []
    for i in range(len(parts)):
        first = before[i - 1] if i > 0 else 0.0
        last = after[i + 1] if i < len(parts) - 1 else 0.0
        out.append(
            jnp.where(lane == 0, first, before[i]) + jnp.where(lane == LANES - 1, last, after[i])
        )
    return jnp.concatenate(out, axis=1) if len(out) > 1 else out[0]


def sides(ref, r, x):
    row = ref[r, x]
    rows = row.shape[0]
    along_y = pltpu.roll(row, 1, 0) + pltpu.roll(row, rows - 1, 0)
    return ref[r, x - 1] + ref[r, x + 1] + along_y + z_sides(row)


def swept(field, rhs, inverse, r, x):
    return (1.0 - OMEGA) * field[r, x] + inverse * (rhs + sides(field, r, x))


def sweep_rows(out, field, rhs, inverse, count, shift):
    for r in range(2):
        for x in range(count):
            out[r, x] = swept(field, rhs(r, x + shift), inverse(x + shift), r, x + 1)


def inverse_of(kappa):
    return jnp.where(kappa > 0.0, OMEGA / (6.0 + kappa), 0.0)


def pair_table(wide, narrow):
    return (iota((wide, narrow), 0) // 2 == iota((wide, narrow), 1)).astype(F32)


def copy_table(narrow, wide):
    return (iota((narrow, wide), 0) == iota((narrow, wide), 1) // 2).astype(F32)


def fine_pre(wide, kappa, inv, zero, guess, sums):
    for r in range(2):
        for x in range(14):
            zero[r, x] = inv(x) * wide[r, x]
    sweep_rows(guess, zero, lambda r, x: wide[r, x], inv, 12, 1)
    left = []
    for r in range(2):
        rows = []
        for x in range(8):
            image = (6.0 + kappa(x + 3)) * guess[r, x + 2] - sides(guess, r, x + 2)
            rows.append(wide[r, x + 3] - image)
        left.append(rows)
    pairs = [left[r][2 * x] + left[r][2 * x + 1] for r in range(2) for x in range(4)]
    return level_rows(pairs + [kappa(2 * x + 1) + kappa(2 * x + 2) for x in range(6)], sums)


def level_rows(pairs, sums):
    table = pair_table(256, LANES)
    sums[...] = jnp.zeros(sums.shape, F32)
    product = table_dot(jnp.concatenate(pairs, axis=0), table)
    for i in range(len(pairs)):
        sums[pl.ds(32 * i + 4, 24), :] = product[24 * i : 24 * (i + 1)]

    def level_row(i):
        pair = sums[pl.ds(32 * i, 16, stride=2), :] + sums[pl.ds(32 * i + 1, 16, stride=2), :]
        return pair * 0.25

    return level_row


def own_rows(shape, low, high):
    row = iota(shape, 0)
    return (row >= low) & (row < high)


def own_eight(row):
    return pltpu.roll(row, 12, 0)[0:8]


def gathered_line(vectors):
    row = iota((16, LANES), 0)
    stacked = jnp.zeros((16, LANES), F32)
    for group, vector in vectors.items():
        stacked = jnp.where(row == group, vector, stacked)
    table = iota((LANES, LANES), 0) // (LANES // KZ) == iota((LANES, LANES), 1) % KZ
    spread = table_dot(stacked, table.astype(F32))
    return jnp.sum(jnp.where(iota((16, LANES), 1) // KZ == row, spread, 0.0), axis=0, keepdims=True)


def level_pre(rhs, extra, guess, zero, first, last):
    linv = [inverse_of(extra(x)) for x in range(12)]
    for r in range(2):
        for x in range(12):
            zero[r, x] = linv[x] * rhs(r, x)
    sweep_rows(guess, zero, rhs, lambda x: linv[x], 10, 1)
    left = []
    for r in range(2):
        rows = []
        for x in range(first, last):
            image = (6.0 + extra(x)) * guess[r, x - 1] - sides(guess, r, x - 1)
            rows.append(rhs(r, x) - image)
        left.append(rows)
    return left


def total(rows):
    out = rows[0]
    for row in rows[1:]:
        out = out + row
    return out


def fine_kernel(place, both, inv, guess, level, line, zero, sums, zero_level, guess_level):
    for x in range(14):
        inv[x] = inverse_of(both[2, x])
    level_row = fine_pre(both, lambda x: both[2, x], lambda x: inv[x], zero, guess, sums)
    own = own_rows((16, LANES), 4, 12)
    nothing = jnp.zeros((16, LANES), F32)
    rhs = [[jnp.where(own, level_row(4 * r + x), 0.0) for x in range(4)] for r in range(2)]
    extra = [level_row(8 + x) for x in range(6)]
    for r in range(2):
        for x in range(4):
            level[r, x] = own_eight(rhs[r][x])
    for x in range(4):
        level[2, x] = own_eight(extra[x + 1])
    left = level_pre(
        lambda r, x: rhs[r][x - 4] if 4 <= x < 8 else nothing,
        lambda x: extra[x - 3] if 3 <= x < 9 else nothing,
        guess_level, zero_level, 2, 10,
    )
    row = iota((16, LANES), 0)
    odd = place[1] % 2
    other = (row < 4 * (1 - odd)) | (row >= 16 - 4 * odd)
    vectors = {}
    for r in range(2):
        for side, rows in enumerate((left[r][2:6], left[r][0:2], left[r][6:8])):
            column = total(rows)
            for far in range(2):
                part = jnp.where(other, column, 0.0) if far else jnp.where(other, 0.0, column)
                vectors[(3 * far + side) * 2 + r] = jnp.sum(part, axis=0, keepdims=True)
    diag_sum = jnp.where(own, total(extra[1:5]), 0.0)
    vectors[DIAG_GROUP] = jnp.sum(diag_sum, axis=0, keepdims=True)
    line[...] = jnp.broadcast_to(gathered_line(vectors), line.shape)


def fold(field):
    folded = field[0:8] + field[8:16] + field[16:24]
    return folded[:, :LANES] + folded[:, LANES:]


def image_kernel(wide, level, first, both, inv, image, narrow, line, zero, guess, zero_level):
    for r in range(2):
        for x in range(14):
            image[r, x] = (6.0 + both[2, x]) * wide[r, x + 1] - sides(wide, r, x + 1)
            zero[r, x] = inv[x] * image[r, x]
    sweep_rows(guess, zero, lambda r, x: image[r, x], lambda x: inv[x], 12, 1)
    own = own_rows((24, 256), 4, 20)
    own_level = own_rows((16, LANES), 4, 12)
    extra = lambda x: first[2, x + 2]
    linv = [inverse_of(extra(x)) for x in range(8)]
    for r in range(2):
        for x in range(8):
            zero_level[r, x] = linv[x] * level[r, x]
    level_rhs = lambda r, x: level[r, x]
    sweep_rows(narrow, zero_level, level_rhs, lambda x: linv[x], 6, 1)
    vectors = {}
    totals = []
    for r in range(2):
        rz = total([both[r, x + 3] * wide[r, x + 4] for x in range(8)])
        pq = total([image[r, x + 3] * wide[r, x + 4] for x in range(8)])
        energy = None
        for x in range(8):
            back = (6.0 + both[2, x + 3]) * guess[r, x + 2] - sides(guess, r, x + 2)
            term = guess[r, x + 2] * (2.0 * image[r, x + 3] - back)
            energy = term if energy is None else energy + term
        energy = fold(jnp.where(own, energy, 0.0))
        column = None
        for x in range(4):
            back = (6.0 + extra(x + 2)) * narrow[r, x + 1] - sides(narrow, r, x + 1)
            left = level[r, x + 2] - back
            column = left if column is None else column + left
            term = narrow[r, x + 1] * (level[r, x + 2] + left)
            term = 4.0 * jnp.where(own_level, term, 0.0)
            energy = energy + term[0:8] + term[8:16]
        vectors[r] = jnp.sum(jnp.where(own_level, column, 0.0), axis=0, keepdims=True)
        totals.append((TOTAL_LANE + r, fold(jnp.where(own, rz, 0.0))))
        totals.append((TOTAL_LANE + 2 + r, fold(jnp.where(own, pq, 0.0))))
        totals.append((TOTAL_LANE + 4 + r, energy))
    out = gathered_line(vectors)
    lane = iota((1, LANES), 1)
    for place, part in totals:
        value = jnp.sum(jnp.sum(part, axis=0, keepdims=True), axis=1, keepdims=True)
        out = jnp.where(lane == place, value, out)
    line[...] = jnp.broadcast_to(out, line.shape)


def coarse_rows(gathered):
    rows = [gathered[x] for x in range(KX)]
    lane = iota(rows[0].shape, 1)
    out = []
    for x in range(KX):
        row = rows[x]
        if x < KX - 1:
            row = row + pltpu.roll(rows[x + 1], LANES - SIDE_LANE, 1)
        if x > 0:
            row = row + pltpu.roll(rows[x - 1], LANES - 2 * SIDE_LANE, 1)
        out.append(jnp.where(lane < 2 * KZ, row, 0.0))
    return rows, out


def coarse_solve(rhs, diag, weights):
    weight_x, weight_y, weight_z = weights
    shape = rhs[0].shape
    row = iota(shape, 0)
    lane = iota(shape, 1) % KZ
    inverse = [OMEGA / d for d in diag]
    value = [i * b for i, b in zip(inverse, rhs)]
    nothing = jnp.zeros(shape, F32)
    for _ in range(CSWEEPS - 1):
        new = []
        for x in range(KX):
            v = value[x]
            below = value[x - 1] if x > 0 else nothing
            above = value[x + 1] if x < KX - 1 else nothing
            along_y = jnp.where(row == 0, 0.0, pltpu.roll(v, 1, 0))
            along_y = along_y + jnp.where(row == KY - 1, 0.0, pltpu.roll(v, shape[0] - 1, 0))
            along_z = jnp.where(lane == 0, 0.0, pltpu.roll(v, 1, 1))
            along_z = along_z + jnp.where(lane == KZ - 1, 0.0, pltpu.roll(v, LANES - 1, 1))
            image = diag[x] * v - (
                weight_x * (below + above) + weight_y * along_y + weight_z * along_z
            )
            new.append(v + inverse[x] * (rhs[x] - image))
        value = new
    return value


def coarse_diag_of(rows, weights):
    lane = iota(rows[0].shape, 1)
    base = 2.0 * (weights[0] + weights[1] + weights[2])
    out = []
    for row in rows:
        first = pltpu.roll(row, LANES - DIAG_LANE, 1)
        second = pltpu.roll(row, LANES - DIAG_LANE + KZ, 1)
        both = jnp.where(lane < KZ, first, jnp.where(lane < 2 * KZ, second, 0.0))
        out.append(base + both)
    return out


def up_blocks(place, value, spread, narrow, target):
    gx, gy = place[0], place[1]
    spread[...] = jnp.zeros(spread.shape, F32)
    stacked = jnp.concatenate(value, axis=0)
    lane_table = iota((LANES, LANES), 0)
    col = iota((LANES, LANES), 1) // (LANES // KZ)
    for r in range(2):
        wide = table_dot(stacked, (lane_table == r * KZ + col).astype(F32))
        for x in range(KX):
            spread[r, x + 1, pl.ds(8, KY), :] = wide[KY * x : KY * (x + 1)]
    odd = gy % 2
    low = gy // 2 + odd + 7
    row = iota((16, LANES), 0)
    limit = 4 + 8 * odd
    for r in range(2):
        for x in range(3):
            first = spread[r, gx + x, pl.ds(low, 1), :]
            second = spread[r, gx + x, pl.ds(low + 1, 1), :]
            tile = jnp.where(row < limit, first, second)
            for i in ((0, 1, 2), (3, 4, 5, 6), (7, 8, 9))[x]:
                target[r, i] = narrow[r, i] + tile


def post(place, value, spread, narrow, level_rhs, extra, guess, rhs, inv, s10, s8, s6, ups, f12, f10, out):
    up_blocks(place, value, spread, narrow, s10)
    linv = {x: inverse_of(extra(x)) for x in range(2, 10)}
    sweep_rows(s8, s10, level_rhs, lambda x: linv[x], 8, 2)
    sweep_rows(s6, s8, level_rhs, lambda x: linv[x], 6, 3)
    table_z = copy_table(LANES, 256)
    for r in range(2):
        for x in range(6):
            base = 32 * (6 * r + x)
            ups[pl.ds(base, 16, stride=2), :] = s6[r, x]
            ups[pl.ds(base + 1, 16, stride=2), :] = s6[r, x]
    rows = [ups[pl.ds(32 * i + 4, 24), :] for i in range(12)]
    product = table_dot(jnp.concatenate(rows, axis=0), table_z)
    for r in range(2):
        for x in range(12):
            i = 6 * r + x // 2
            f12[r, x] = guess[r, x] + product[24 * i : 24 * (i + 1)]
    sweep_rows(f10, f12, rhs, lambda x: inv[x], 10, 2)
    for r in range(2):
        for x in range(8):
            out(r, x, swept(f10, rhs(r, x + 3), inv[x + 3], r, x + 1))


def middle(row):
    return pltpu.roll(row, row.shape[0] - 4, 0)[0:16]


def share(alone, kappa, inv, image, zero, guess, sums):
    nothing = jnp.zeros((24, 256), F32)
    for r in range(2):
        for x in range(14):
            if 2 <= x < 12:
                image[r, x] = (6.0 + kappa(x)) * alone[r, x + 1] - sides(alone, r, x + 1)
                zero[r, x] = inv(x) * image[r, x]
            else:
                image[r, x] = nothing
                zero[r, x] = nothing
        for x in (0, 1, 14, 15):
            guess[r, x] = nothing
        for x in range(2, 14):
            guess[r, x] = swept(zero, image[r, x - 1], inv(x - 1), r, x - 1)
    pairs = []
    for r in range(2):
        rows = []
        for x in range(14):
            back = (6.0 + kappa(x)) * guess[r, x + 1] - sides(guess, r, x + 1)
            rows.append(image[r, x] - back)
        pairs = pairs + [rows[0]]
        pairs = pairs + [rows[2 * x + 1] + rows[2 * x + 2] for x in range(6)] + [rows[13]]
    return level_rows(pairs, sums)


def precond_kernel(weights, place, gathered, level, guess, both, inv,
                   precond, diag_out, part, low, high,
                   zero_level, narrow, alone, image, zero, guess_alone, sums,
                   spread, s10, s8, s6, ups, f12, f10):
    level_pre(lambda r, x: level[r, x], lambda x: level[2, x], narrow, zero_level, 4, 4)
    rows, rhs = coarse_rows(gathered)
    diag = coarse_diag_of(rows, weights)
    for x in range(KX):
        diag_out[x] = diag[x]
    value = coarse_solve(rhs, diag, weights)
    own = own_rows((24, 256), 4, 20)
    top = iota((8, LANES), 0) < 4
    for r in range(2):
        for x in (0, 1, 2, 3, 12, 13, 14, 15):
            alone[r, x] = jnp.zeros((24, 256), F32)

    def out(r, x, row):
        own_part = middle(row)
        precond[r, x] = own_part
        alone[r, x + 4] = jnp.where(own, row, 0.0)
        left, right = own_part[:, :LANES], own_part[:, LANES:]
        low[r, x, 0:8, :] = jnp.where(top, left[0:8], pltpu.roll(right[0:8], 4, 0))
        high[r, x, 0:8, :] = jnp.where(top, pltpu.roll(left[8:16], 4, 0), right[8:16])

    post(
        place, value, spread, narrow, lambda r, x: level[r, x], lambda x: level[2, x],
        guess, lambda r, x: both[r, x], inv, s10, s8, s6, ups, f12, f10, out,
    )
    level_row = share(
        alone, lambda x: both[2, x], lambda x: inv[x], image, zero, guess_alone, sums
    )
    for r in range(2):
        for x in range(8):
            row = level_row(8 * r + x)
            part[r, x] = row
            low[r, x, 8:16, :] = pltpu.roll(row, 14, 0)[0:8]
            high[r, x, 8:16, :] = row[8:16]


def final_kernel(weights, place, gathered, diag_in, narrow, level, first, image, inv, precond, right,
                 solution_field, residual, direction, zero, guess, spread, s10, s8, s6, ups, f12, f10):
    for r in range(2):
        for x in range(14):
            zero[r, x] = inv[x] * image[r, x]
    sweep_rows(guess, zero, lambda r, x: image[r, x], lambda x: inv[x], 12, 1)
    rows, rhs = coarse_rows(gathered)
    diag = [diag_in[x] for x in range(KX)]
    value = coarse_solve(rhs, diag, weights)
    sums = jnp.sum(total(rows), axis=0, keepdims=True)
    product = jnp.sum(total([a * b for a, b in zip(rhs, value)]), axis=0, keepdims=True)
    line = iota(sums.shape, 1)

    def pick(row, low, high):
        return jnp.sum(jnp.where((line >= low) & (line < high), row, 0.0), axis=1, keepdims=True)

    alphas, betas = [], []
    for r in range(2):
        rz = pick(sums, TOTAL_LANE + r, TOTAL_LANE + r + 1)
        pq = pick(sums, TOTAL_LANE + 2 + r, TOTAL_LANE + 3 + r)
        energy = pick(sums, TOTAL_LANE + 4 + r, TOTAL_LANE + 5 + r)
        energy = energy + 4.0 * pick(product, r * KZ, (r + 1) * KZ)
        alpha = rz / pq
        alphas.append(alpha)
        betas.append(alpha * alpha * energy / rz - 1.0)

    def out(r, x, row):
        p = precond[r, x]
        solution_field[r, x] = alphas[r] * p
        residual[r, x] = right[r, x] - alphas[r] * middle(image[r, x + 3])
        direction[r, x] = p - alphas[r] * middle(row) + betas[r] * p

    post(
        place, value, spread, narrow, lambda r, x: level[r, x - 2], lambda x: first[2, x],
        guess, lambda r, x: image[r, x], inv, s10, s8, s6, ups, f12, f10, out,
    )


def call(kernel, outs, scratch, place=None):
    vmem = pl.BlockSpec(memory_space=pltpu.VMEM)

    def run(*args):
        specs = [vmem] * len(args)
        if place is not None:
            args = (place,) + args
            specs = [pl.BlockSpec(memory_space=pltpu.SMEM)] + specs
        return pl.pallas_call(
            kernel,
            out_shape=[jax.ShapeDtypeStruct(shape, F32) for shape in outs],
            in_specs=specs,
            out_specs=[vmem] * len(outs),
            scratch_shapes=[pltpu.VMEM(shape, F32) for shape in scratch],
            compiler_params=pltpu.CompilerParams(vmem_limit_bytes=16 * 1024 * 1024),
        )(*args)

    return run


def swap_y(low, high):
    count = lax.axis_size("gy")
    even = lax.axis_index("gy") % 2 == 0
    near_pairs = [(i, i + 1) for i in range(0, count, 2)]
    far_pairs = [(i, i + 1) for i in range(1, count - 1, 2)]
    near_pairs = near_pairs + [(b, a) for a, b in near_pairs]
    far_pairs = far_pairs + [(b, a) for a, b in far_pairs]
    far = lax.ppermute(jnp.where(even, low, high), "gy", far_pairs)
    near = lax.ppermute(jnp.where(even, high, low), "gy", near_pairs)
    return jnp.where(even, far, near), jnp.where(even, near, far)


def swap_x(low, high):
    count = lax.axis_size("gx")
    forward = [(i, i + 1) for i in range(count - 1)]
    backward = [(b, a) for a, b in forward]
    return lax.ppermute(high, "gx", forward), lax.ppermute(low, "gx", backward)


def extended_x(block, width):
    low, high = swap_x(block[:, :width], block[:, block.shape[1] - width :])
    return jnp.concatenate([low, block, high], axis=1)


def extended(block):
    low, high = swap_y(block[:, :, :3], block[:, :, block.shape[2] - 3 :])
    block = jnp.concatenate([low, block, high], axis=2)
    return extended_x(jnp.pad(block, ((0, 0), (0, 0), (1, 1), (0, 0))), 3)


def extended_level(level):
    low, high = swap_y(level[:, :, :4], level[:, :, 4:])
    return extended_x(jnp.concatenate([low, level, high], axis=2), 4)


def halves_to_rows(block):
    return jnp.concatenate([block[..., :LANES], block[..., LANES:]], axis=2)


def rows_to_halves(block):
    rows = block.shape[2] // 2
    return jnp.concatenate([block[:, :, :rows], block[:, :, rows:]], axis=3)


def exchange_shares(precond, part, low, high):
    low, high = swap_y(low, high)
    wide = jnp.concatenate([rows_to_halves(low[:, :, :8]), precond, rows_to_halves(high[:, :, :8])], axis=2)
    part = part + jnp.pad(low[:, :, 8:14], ((0, 0), (0, 0), (0, 10), (0, 0)))
    part = part + jnp.pad(high[:, :, 8:14], ((0, 0), (0, 0), (10, 0), (0, 0)))
    low = jnp.concatenate([halves_to_rows(wide[:, :4]), part[:, :4]], axis=2)
    high = jnp.concatenate([halves_to_rows(wide[:, 4:]), part[:, 4:]], axis=2)
    low, high = swap_x(low, high)
    wide = jnp.concatenate([rows_to_halves(low[:, :, :48]), wide, rows_to_halves(high[:, :, :48])], axis=1)
    part = jnp.concatenate([part[:, :4] + low[:, :, 48:], part[:, 4:] + high[:, :, 48:]], axis=1)
    return wide, part


def gather_all(line, beside=None):
    size_x = lax.axis_size("gx")
    size_y = lax.axis_size("gy")
    rows = lax.all_to_all(line, "gy", 0, 0, tiled=True).reshape(KY, size_y // KY, LANES)
    even, odd = rows[:, 0], rows[:, 1]
    other = jnp.pad(even[1:], ((0, 1), (0, 0))) + jnp.pad(odd[:-1], ((1, 0), (0, 0)))
    other = jnp.pad(other[:, OTHER_LANE : 2 * OTHER_LANE], ((0, 0), (0, LANES - OTHER_LANE)))
    rows = even + odd + other
    if beside is not None:
        rows, beside = lax.optimization_barrier((rows, beside))
    spread = jnp.broadcast_to(rows[None], (size_x, KY, LANES))
    return lax.all_to_all(spread, "gx", 0, 0, tiled=True), beside


def local(right_side, diagonal):
    block_x = right_side.shape[1] * lax.axis_size("gx") // 2 // KX
    block_y = right_side.shape[2] * lax.axis_size("gy") // 2 // KY
    block_z = right_side.shape[3] // 2 // KZ
    size_y = lax.axis_size("gy")
    weights = (float(block_y * block_z), float(block_x * block_z), float(block_x * block_y))
    place = jnp.stack([lax.axis_index("gx"), lax.axis_index("gy")]).astype(jnp.int32)

    both = extended(jnp.concatenate([right_side, diagonal[None]], axis=0))
    inv, guess, level, line = call(
        fine_kernel,
        [(14, 24, 256), (2, 12, 24, 256), (3, 4, 8, LANES), (size_y, LANES)],
        [(2, 14, 24, 256), (448, LANES), (2, 12, 16, LANES), (2, 10, 16, LANES)],
        place,
    )(both)
    gathered, _ = gather_all(line)
    first = extended_level(level)
    post_scratch = [
        (2, KX + 2, 8 + KY + 8, LANES), (2, 10, 16, LANES), (2, 8, 16, LANES), (2, 6, 16, LANES),
        (384, LANES), (2, 12, 24, 256), (2, 10, 24, 256),
    ]
    precond, diag, part, low, high = call(
        functools.partial(precond_kernel, weights),
        [(2, 8, 16, 256), (KX, KY, LANES), (2, 8, 16, LANES), (2, 8, 16, LANES), (2, 8, 16, LANES)],
        [
            (2, 12, 16, LANES), (2, 10, 16, LANES), (2, 16, 24, 256), (2, 14, 24, 256),
            (2, 14, 24, 256), (2, 16, 24, 256), (512, LANES),
        ] + post_scratch,
        place,
    )(gathered, first, guess, both, inv)
    wide, level_q = exchange_shares(precond, part, low, high)
    image, inner, line_q = call(
        image_kernel,
        [(2, 14, 24, 256), (2, 6, 16, LANES), (size_y, LANES)],
        [(2, 14, 24, 256), (2, 12, 24, 256), (2, 8, 16, LANES)],
    )(wide, level_q, first, both, inv)
    low, high = swap_x(inner[:, 2:4], inner[:, 2:4])
    gathered_q, narrow_q = gather_all(line_q, jnp.concatenate([low, inner, high], axis=1))
    return tuple(
        call(
            functools.partial(final_kernel, weights),
            [(2, 8, 16, 256)] * 3,
            [(2, 14, 24, 256), (2, 12, 24, 256)] + post_scratch,
            place,
        )(gathered_q, diag, narrow_q, level_q, first, image, inv, precond, right_side)
    )


def solution(mesh):
    placed = (P(None, "gx", "gy", None), P("gx", "gy", None))
    return jax.shard_map(
        local,
        mesh=mesh,
        in_specs=placed,
        out_specs=(P(None, "gx", "gy", None),) * 3,
        check_vma=False,
    )
```
